256 devices in a mesh: frame: 64 (over y, x_hi, z), row: 4 (over x_lo, core).
Axes of the slice: x: 4 (x_hi: 2, x_lo: 2; x = x_hi * 2 + x_lo), y: 4, z: 8, core: 2. Of those that a mesh axis runs over, the one named last changes fastest.
Arguments:
- tokens: bfloat16 [256, 8, 32, 1024], P('frame', 'row'), may hold values from -6 to 6
- norm_gain: float32 [1024], replicated, may hold values from 0.1 to 1.9
- qkv_weight: bfloat16 [3, 1024, 1024], P(None, None, 'row')
- out_weight: bfloat16 [1024, 1024], P('row'), may hold values from -6 to 6
- key_offsets: int32 [256, 16], P('frame'), may hold values from -8 to 8, as said below
- feat_gain: float32 [1024], replicated, may hold values from 0.1 to 1.9
- proj_weight: bfloat16 [1024, 256], replicated, may hold values from -0.1875 to 0.1875
- conv_one: bfloat16 [3, 3, 256, 256], replicated, may hold values from -0.125 to 0.125
- conv_two: bfloat16 [3, 3, 256, 256], replicated, may hold values from -0.125 to 0.125
Outputs:
- attended: bfloat16 [256, 8, 32, 1024], P('frame', 'row')
- joined_map: bfloat16 [256, 8, 32, 256], P('frame', 'row')
The draws below stay inside these ranges and needn't reach their ends.
Inputs may be any that keep to these rules, and one draw needn't show every extreme that they name: `key_offsets`: each row holds 0, 8, -8 and 13 further offsets, all distinct.
All inputs are finite; a program needn't handle non-finite values.
Results may differ from the reference program's by a relative error of at most 0.023.
Values may be sent and summed in bfloat16 or wider, within the bound.
No kernel may reach another device: no remote copies, remote signals or barrier semaphores. Data moves between devices by JAX's collectives and lax.ppermute only.
A program may use at most 64 MiB of HBM per device.

```python
import jax
import jax.numpy as jnp
from jax import lax

D = 1024
HEADS = 16
CH = 256
PW = 32
HEAD_DIM = 64
PH = 8
FRAMES = 256
RADIUS = 8
KEYS = 16


def draw_qkv_weight(key, part):
    key = jax.random.fold_in(key, 11)
    normal_part = jax.random.normal(key, (3, D, D), jnp.float32) * D ** (-0.5)
    return normal_part.astype(jnp.bfloat16)


def draw_key_offsets(key, part):
    key = jax.random.fold_in(key, 23)
    extra_count = KEYS - 3
    choices_count = 2 * RADIUS - 2

    def draw_row(subkey):
        chosen = jax.random.permutation(subkey, choices_count)[:extra_count].astype(jnp.int32)
        return chosen - (RADIUS - 1) + (chosen >= RADIUS - 1).astype(jnp.int32)
    others = jax.vmap(draw_row)(jax.random.split(key, FRAMES))
    fixed = jnp.broadcast_to(jnp.array([0, RADIUS, -RADIUS], jnp.int32), (FRAMES, 3))
    return jnp.concatenate([fixed, others.astype(jnp.int32)], axis=1)


def shard_levels(rng, shape, cuts, low, high):
    def one(position, shards_of):
        draws = jax.random.uniform(jax.random.fold_in(jax.random.fold_in(rng, 6), position), (shards_of,), jnp.float32, low / len(cuts), high / len(cuts))
        return jnp.repeat(jnp.exp(draws), shape[position] // shards_of).reshape((-1,) + (1,) * (len(shape) - position - 1))

    level = one(*cuts[0])
    for cut in cuts[1:]:
        level = level * one(*cut)
    return level


def centred(rng, shape, scale, reach, cuts=(), kind=jnp.bfloat16):
    values = scale * jax.random.normal(rng, shape, jnp.float32)
    if cuts:
        values = values * shard_levels(rng, shape, cuts, -0.22, 0.18)
    return jnp.clip(values, -reach, reach).astype(kind)


def setup_inputs(seed: int = 0) -> dict:
    key_of = jax.random.split(jax.random.key(seed), 10)
    tokens = centred(key_of[0], (FRAMES, PH, PW, D), 1.0, 6.0, ((0, 64), (1, 4)))
    norm_gain = jnp.clip(1.0 + 0.18 * jax.random.normal(key_of[1], (D,), jnp.float32), 0.1, 1.9)
    qkv_weight = draw_qkv_weight(jax.random.fold_in(key_of[9], 71), 0)
    out_weight = centred(key_of[3], (D, D), 1.0, 6.0, ((0, 4),))
    key_offsets = draw_key_offsets(jax.random.fold_in(key_of[9], 71), 0)
    feat_gain = jnp.clip(1.0 + 0.18 * jax.random.normal(key_of[5], (D,), jnp.float32), 0.1, 1.9)
    proj_weight = centred(key_of[6], (D, CH), D ** -0.5, 0.1875)
    conv_one = centred(key_of[7], (3, 3, CH, CH), (9 * CH) ** -0.5, 0.125)
    conv_two = centred(key_of[8], (3, 3, CH, CH), (9 * CH) ** -0.5, 0.125)
    return dict(tokens=tokens, norm_gain=norm_gain, qkv_weight=qkv_weight, out_weight=out_weight, key_offsets=key_offsets, feat_gain=feat_gain, proj_weight=proj_weight, conv_one=conv_one, conv_two=conv_two)


EPSILON = 1e-06

def layer_norm(values, gain_vec):
    average = lax.optimization_barrier(jnp.mean(values, axis=-1, keepdims=True))
    centered = values - average
    spread = lax.optimization_barrier(jnp.mean(centered * centered, axis=-1, keepdims=True))
    return centered * lax.rsqrt(spread + EPSILON) * gain_vec

def convolve(field, weight):
    widened = jnp.pad(field, ((0, 0), (1, 1), (1, 1), (0, 0)))
    summed = jnp.zeros(field.shape[:3] + (weight.shape[3],), jnp.float32)
    for row_step in range(3):
        for col_step in range(3):
            window = widened[:, row_step:row_step + PH, col_step:col_step + PW].astype(jnp.float32)
            summed = summed + jnp.einsum('fhwc,cd->fhwd', window, weight[row_step, col_step].astype(jnp.float32))
    return summed

def reference(tokens, norm_gain, qkv_weight, out_weight, key_offsets, feat_gain, proj_weight, conv_one, conv_two):
    frame_len = PH * PW
    flat_tokens = tokens.reshape(FRAMES * frame_len, D)
    normed = layer_norm(flat_tokens.astype(jnp.float32), norm_gain).astype(jnp.bfloat16)
    projected = [jnp.dot(normed, qkv_weight[which], preferred_element_type=jnp.float32).astype(jnp.bfloat16).reshape(FRAMES, frame_len, HEADS, HEAD_DIM) for which in range(3)]
    queries, key_part, value_part = projected
    score_scale = HEAD_DIM ** (-0.5)

    def attend(frame_inputs):
        frame_id, frame_queries, frame_offsets = frame_inputs
        key_frames = jnp.mod(frame_id + frame_offsets, FRAMES).astype(jnp.int32)
        gathered_keys = jnp.take(key_part, key_frames, axis=0).reshape(KEYS * frame_len, HEADS, HEAD_DIM).astype(jnp.float32)
        gathered_values = jnp.take(value_part, key_frames, axis=0).reshape(KEYS * frame_len, HEADS, HEAD_DIM).astype(jnp.float32)
        scores = jnp.einsum('qhd,khd->hqk', frame_queries.astype(jnp.float32), gathered_keys) * score_scale
        highest = lax.optimization_barrier(jnp.max(scores, axis=-1, keepdims=True))
        weights = jnp.exp(scores - highest)
        denominator = lax.optimization_barrier(jnp.sum(weights, axis=-1, keepdims=True))
        rounded = lax.optimization_barrier(weights.astype(jnp.bfloat16))
        numerator = jnp.einsum('hqk,khd->hqd', rounded.astype(jnp.float32), gathered_values)
        context = (numerator / denominator).astype(jnp.bfloat16)
        return jnp.transpose(context, (1, 0, 2)).reshape(frame_len, D)
    contexts = lax.map(attend, (jnp.arange(FRAMES, dtype=jnp.int32), queries, key_offsets))
    contexts = contexts.reshape(FRAMES * frame_len, D)
    attended = (flat_tokens.astype(jnp.float32) + jnp.dot(contexts, out_weight, preferred_element_type=jnp.float32)).astype(jnp.bfloat16)
    lifted = layer_norm(attended.astype(jnp.float32), feat_gain).astype(jnp.bfloat16)
    mapped = jnp.dot(lifted, proj_weight, preferred_element_type=jnp.float32).astype(jnp.bfloat16).reshape(FRAMES, PH, PW, CH)
    inner_map = jax.nn.relu(convolve(jax.nn.relu(mapped), conv_one)).astype(jnp.bfloat16)
    joined_map = (mapped.astype(jnp.float32) + convolve(inner_map, conv_two)).astype(jnp.bfloat16)
    return (attended.reshape(FRAMES, PH, PW, D), joined_map)
```

```python
import functools

import jax
import jax.numpy as jnp
import numpy as np
from jax import lax
from jax.experimental import pallas as pl
from jax.experimental.pallas import tpu as pltpu
from jax.sharding import PartitionSpec as P

EPSILON = 1e-06
HEAD = 64
HEADS_HERE = 4
FRAMES_HERE = 4
QUARTER = 64
WIDTH = 256
QUERY_SCALE = 1.4426950408889634 / 8.0
VMEM = pl.BlockSpec(memory_space=pltpu.VMEM)
SMEM = pl.BlockSpec(memory_space=pltpu.SMEM)
ANY = pl.BlockSpec(memory_space=pl.ANY)

CORE_PAIRS = [(0, 1), (1, 0), (2, 3), (3, 2)]
CHIP_PAIRS = [(0, 2), (2, 0), (1, 3), (3, 1)]
CROSS_PAIRS = [(0, 3), (3, 0), (1, 2), (2, 1)]


def from_behind(value, steps):
    count = lax.axis_size("frame")
    pairs = [(source, (source + steps) % count) for source in range(count)]
    return lax.ppermute(value, "frame", pairs)


def layer_norm(values, gain_vec):
    average = jnp.mean(values, axis=-1, keepdims=True)
    centered = values - average
    spread = jnp.mean(centered * centered, axis=-1, keepdims=True)
    return centered * lax.rsqrt(spread + EPSILON) * gain_vec


def project_kernel(first_ref, second_ref, gain_ref, weight_ref, kv_ref, query_ref):
    gain = gain_ref[...]
    normed = [
        layer_norm(ref[...].astype(jnp.float32), gain).astype(jnp.bfloat16)
        for ref in (first_ref, second_ref)
    ]
    rows = []
    for frame in range(FRAMES_HERE):
        for part in normed:
            rows.append(part[frame * QUARTER : (frame + 1) * QUARTER])
    rows = jnp.concatenate(rows, axis=0)
    key = jnp.dot(rows, weight_ref[1], preferred_element_type=jnp.float32)
    key = key.astype(jnp.bfloat16)
    value = jnp.dot(rows, weight_ref[2], preferred_element_type=jnp.float32)
    value = value.T.astype(jnp.bfloat16)
    query = jnp.dot(rows, weight_ref[0], preferred_element_type=jnp.float32)
    query = (query * QUERY_SCALE).T.astype(jnp.bfloat16)
    for frame in range(FRAMES_HERE):
        span = slice(frame * 128, (frame + 1) * 128)
        kv_ref[frame, 0:128, :] = key[span]
        kv_ref[frame, 128:256, 0:128] = value[0:128, span]
        kv_ref[frame, 128:256, 128:256] = value[128:256, span]
        query_ref[frame] = query[:, span]


def project(first, second, gain, weight):
    return pl.pallas_call(
        project_kernel,
        in_specs=[VMEM] * 4,
        out_specs=[VMEM] * 2,
        out_shape=[
            jax.ShapeDtypeStruct((FRAMES_HERE, 256, 256), jnp.bfloat16),
            jax.ShapeDtypeStruct((FRAMES_HERE, WIDTH, 128), jnp.bfloat16),
        ],
        compiler_params=pltpu.CompilerParams(vmem_limit_bytes=32 << 20),
        cost_estimate=pl.CostEstimate(
            flops=2 * 512 * 1024 * 768, bytes_accessed=3 << 20, transcendentals=0
        ),
    )(first, second, gain, weight)


def attend_kernel(blocks, tiles, begins, ends, *refs):
    index_ref, keep_ref, query_a, query_b = refs[:4]
    refs = refs[4:]
    block_refs, refs = refs[:blocks], refs[blocks:]
    if not begins:
        high_in, total_in, refs = refs[0], refs[1], refs[2:]
    if ends:
        outs, refs = refs[:4], refs[4:]
    else:
        high_out, total_out, refs = refs[0], refs[1], refs[2:]
    held, sems = refs
    frame = pl.program_id(0)

    @pl.when(frame == 0)
    def _():
        copies = [
            pltpu.make_async_copy(
                block_refs[b],
                held.at[pl.ds(b * FRAMES_HERE, FRAMES_HERE)],
                sems.at[b],
            )
            for b in range(blocks)
        ]
        for copy in copies:
            copy.start()
        for copy in copies:
            copy.wait()

    index = [index_ref[frame, t] for t in range(tiles)]
    keep = [keep_ref[frame, t].astype(jnp.bfloat16) for t in range(tiles)]
    ones = jnp.ones((16, 128), jnp.bfloat16)
    zeros = jnp.zeros((HEAD, 256), jnp.bfloat16)

    def score(head):
        pair = head // 2
        query = jnp.concatenate(
            [
                query_a[frame, head * HEAD : (head + 1) * HEAD, :],
                query_b[frame, head * HEAD : (head + 1) * HEAD, :],
            ],
            axis=1,
        )
        both = [query, zeros] if head % 2 == 0 else [zeros, query]
        both = jnp.concatenate(both, axis=0)
        return [
            jnp.dot(
                held[index[t], 0:128, pair * 128 : (pair + 1) * 128],
                both,
                preferred_element_type=jnp.float32,
            )
            for t in range(tiles)
        ]

    def absorb(head, scores):
        pair = head // 2
        start = 128 + (head % 2) * HEAD
        high = scores[0].reshape(-1, 8, 256).max(axis=0)
        for s in scores[1:]:
            high = jnp.maximum(high, s.reshape(-1, 8, 256).max(axis=0))
        high = jnp.max(high, axis=0, keepdims=True)
        total = None
        if not begins:
            old = high_in[0, head, 0:1, :]
            high = jnp.maximum(high, old)
            total = total_in[0, head] * jnp.exp2(old - high)
        for t in range(0, tiles, 2):
            group = range(t, min(t + 2, tiles))
            weights = [jnp.exp2(scores[g] - high).astype(jnp.bfloat16) for g in group]
            sides = [
                jnp.concatenate(
                    [
                        held[index[g], start : start + HEAD, pair * 128 : (pair + 1) * 128],
                        ones,
                    ],
                    axis=0,
                )
                * keep[g]
                for g in group
            ]
            added = jnp.dot(
                jnp.concatenate(sides, axis=1),
                jnp.concatenate(weights, axis=0),
                preferred_element_type=jnp.float32,
            )
            total = added if total is None else total + added
        if ends:
            return total[0:HEAD] / total[HEAD : HEAD + 1]
        total_out[0, head] = total
        high_out[0, head] = jnp.broadcast_to(high, (8, 256))
        return None

    contexts = []
    scores = score(0)
    for head in range(HEADS_HERE):
        later = score(head + 1) if head + 1 < HEADS_HERE else None
        contexts.append(absorb(head, scores))
        scores = later
    if ends:
        context = jnp.concatenate(contexts, axis=0).T.astype(jnp.bfloat16)
        for j in range(4):
            outs[j][...] = context[j * QUARTER : (j + 1) * QUARTER]


def attend(index, keep, query_a, query_b, block_list, state, ends):
    blocks, tiles = len(block_list), index.shape[1]
    high_spec = pl.BlockSpec((1, HEADS_HERE, 8, 256), lambda f: (f, 0, 0, 0))
    total_spec = pl.BlockSpec((1, HEADS_HERE, HEAD + 16, 256), lambda f: (f, 0, 0, 0))
    state_specs = [high_spec, total_spec]
    if ends:
        out_specs = [pl.BlockSpec((QUARTER, WIDTH), lambda f: (f, 0))] * 4
        out_shape = [jax.ShapeDtypeStruct((FRAMES_HERE * QUARTER, WIDTH), jnp.bfloat16)] * 4
    else:
        out_specs = state_specs
        out_shape = [
            jax.ShapeDtypeStruct((FRAMES_HERE, HEADS_HERE, 8, 256), jnp.float32),
            jax.ShapeDtypeStruct((FRAMES_HERE, HEADS_HERE, HEAD + 16, 256), jnp.float32),
        ]
    inputs = [index, keep, query_a, query_b, *block_list, *(state or ())]
    in_specs = [SMEM, SMEM, VMEM, VMEM] + [ANY] * blocks + (state_specs if state else [])
    return pl.pallas_call(
        functools.partial(attend_kernel, blocks, tiles, not state, ends),
        grid=(FRAMES_HERE,),
        in_specs=in_specs,
        out_specs=out_specs,
        out_shape=out_shape,
        scratch_shapes=[
            pltpu.VMEM((blocks * FRAMES_HERE, 256, 256), jnp.bfloat16),
            pltpu.SemaphoreType.DMA((blocks,)),
        ],
        compiler_params=pltpu.CompilerParams(
            vmem_limit_bytes=48 << 20, dimension_semantics=("arbitrary",)
        ),
        cost_estimate=pl.CostEstimate(
            flops=4 * 4 * tiles * 2 * 2 * 128 * 256 * 256,
            bytes_accessed=blocks << 19,
            transcendentals=16 * tiles * 128 * 256,
        ),
    )(*inputs)


def tile_table(valid, positions, slots, fallback):
    positions, slots = np.array(positions), np.array(slots)
    there = jnp.stack([valid[f, positions[f]] for f in range(FRAMES_HERE)])
    other = np.roll(slots, -fallback, axis=1)
    index = jnp.where(there, slots, other).astype(jnp.int32)
    return index, there.astype(jnp.float32)


def finish_kernel(c0, c1, c2, c3, w0, w1, w2, w3, token_ref, gain_ref, proj_ref, out_ref, map_ref):
    total = token_ref[...].astype(jnp.float32)
    mixed = jnp.dot(c0[...], w0[...], preferred_element_type=jnp.float32)
    for c, w in ((c1, w1), (c2, w2), (c3, w3)):
        mixed = mixed + jnp.dot(c[...], w[...], preferred_element_type=jnp.float32)
    attended = (total + mixed).astype(jnp.bfloat16)
    out_ref[...] = attended
    lifted = layer_norm(attended.astype(jnp.float32), gain_ref[...]).astype(jnp.bfloat16)
    mapped = jnp.dot(lifted, proj_ref[...], preferred_element_type=jnp.float32)
    map_ref[...] = mapped.astype(jnp.bfloat16)


def finish(contexts, weights, tokens, gain, proj):
    return pl.pallas_call(
        finish_kernel,
        in_specs=[VMEM] * 11,
        out_specs=[VMEM] * 2,
        out_shape=[
            jax.ShapeDtypeStruct((256, 1024), jnp.bfloat16),
            jax.ShapeDtypeStruct((256, 256), jnp.bfloat16),
        ],
        compiler_params=pltpu.CompilerParams(vmem_limit_bytes=32 << 20),
        cost_estimate=pl.CostEstimate(
            flops=2 * 256 * 1024 * 1280, bytes_accessed=4 << 20, transcendentals=0
        ),
    )(*contexts, *weights, tokens, gain, proj)


def join_kernel(edge_ref, before_ref, own_ref, after_ref, one_ref, two_ref, out_ref):
    def widen(values):
        count = values.shape[0]
        column = lax.broadcasted_iota(jnp.int32, (count, 256), 0) % 32
        left = jnp.where(column == 0, 0.0, pltpu.roll(values, 1, 0))
        right = jnp.where(column == 31, 0.0, pltpu.roll(values, count - 1, 0))
        return jnp.concatenate(
            [left.astype(jnp.bfloat16), values.astype(jnp.bfloat16), right.astype(jnp.bfloat16)],
            axis=1,
        )

    def conv(wide, rows_in, weight_ref):
        rows_out = rows_in - 2
        summed = None
        for a in range(3):
            window = jnp.concatenate(
                [
                    wide[(f * rows_in + a) * 32 : (f * rows_in + a + rows_out) * 32]
                    for f in range(FRAMES_HERE)
                ],
                axis=0,
            )
            added = jnp.dot(window, weight_ref[a], preferred_element_type=jnp.float32)
            summed = added if summed is None else summed + added
        return summed

    own = own_ref[...].astype(jnp.float32)
    before = before_ref[...].astype(jnp.float32)
    after = after_ref[...].astype(jnp.float32)
    six = []
    for f in range(FRAMES_HERE):
        span = slice(f * QUARTER, (f + 1) * QUARTER)
        six += [before[span], own[span], after[span]]
    six = jnp.maximum(jnp.concatenate(six, axis=0), 0.0)
    inner = conv(widen(six), 6, one_ref)
    inner = jnp.maximum(inner, 0.0)
    row = (lax.broadcasted_iota(jnp.int32, (512, 256), 0) // 32) % 4
    has_before, has_after = edge_ref[0], edge_ref[1]
    drop = ((row == 0) & (has_before == 0)) | ((row == 3) & (has_after == 0))
    inner = jnp.where(drop, 0.0, inner)
    joined = conv(widen(inner), 4, two_ref)
    out_ref[...] = (own + joined).astype(jnp.bfloat16)


def join(edge, before, own, after, one, two):
    return pl.pallas_call(
        join_kernel,
        in_specs=[SMEM] + [VMEM] * 5,
        out_specs=VMEM,
        out_shape=jax.ShapeDtypeStruct((256, 256), jnp.bfloat16),
        compiler_params=pltpu.CompilerParams(vmem_limit_bytes=32 << 20),
        cost_estimate=pl.CostEstimate(
            flops=2 * 768 * 2304 * 256, bytes_accessed=3 << 20, transcendentals=0
        ),
    )(edge, before, own, after, one, two)


def shards(
    tokens,
    norm_gain,
    qkv_weight,
    out_weight,
    key_offsets,
    feat_gain,
    proj_weight,
    conv_one,
    conv_two,
):
    own = tokens.reshape(FRAMES_HERE * QUARTER, 1024)
    core = lambda value: lax.ppermute(value, "row", CORE_PAIRS)
    chip = lambda value: lax.ppermute(value, "row", CHIP_PAIRS)
    gain = norm_gain.reshape(1, 1024)

    positions = np.arange(20)
    distance = positions[None, :] - 8 - np.arange(FRAMES_HERE)[:, None]
    valid = jnp.any(key_offsets[:, :, None] == distance[:, None, :], axis=1)

    far = chip(own)
    near = core(own)
    kv_a, query_a = project(own, near, gain, qkv_weight)
    behind_a, ahead_a = from_behind(kv_a, 1), from_behind(kv_a, -1)
    far_near = core(far)
    kv_b, query_b = project(far, far_near, gain, qkv_weight)
    behind_b, ahead_b = from_behind(kv_b, 1), from_behind(kv_b, -1)
    behind_2a, ahead_2a = from_behind(behind_a, 1), from_behind(ahead_a, -1)
    behind_2b, ahead_2b = from_behind(behind_b, 1), from_behind(ahead_b, -1)

    weight_chip = chip(out_weight)
    weight_core = core(out_weight)
    weight_cross = core(weight_chip)

    frames = range(FRAMES_HERE)
    near_positions = [[*range(4, 8), *range(12, 16)] for f in frames]
    near_slots = [[*range(0, 4), *range(4, 8)] for f in frames]
    wide_positions = [[*range(f, 4), *range(16, 17 + f)] for f in frames]
    wide_slots = [[*range(f, 4), *range(4, 5 + f)] for f in frames]
    own_positions = [[p for p in range(8, 12) for _ in range(2)] for f in frames]
    own_slots = [[s + half * 4 for s in range(4) for half in range(2)] for f in frames]
    half_positions = [near_positions[f] + wide_positions[f] for f in frames]
    half_slots = [near_slots[f] + [s + 8 for s in wide_slots[f]] for f in frames]

    table = tile_table(valid, own_positions, own_slots, 2)
    state = attend(*table, query_a, query_b, [kv_a, kv_b], None, False)
    table = tile_table(valid, half_positions, half_slots, 1)
    state = attend(
        *table, query_a, query_b, [behind_a, ahead_a, behind_2a, ahead_2a], state, False
    )
    table = tile_table(valid, near_positions, near_slots, 1)
    state = attend(*table, query_a, query_b, [behind_b, ahead_b], state, False)
    table = tile_table(valid, wide_positions, wide_slots, 1)
    parts = attend(*table, query_a, query_b, [behind_2b, ahead_2b], state, True)

    contexts = [
        parts[0],
        core(parts[1]),
        chip(parts[2]),
        lax.ppermute(parts[3], "row", CROSS_PAIRS),
    ]
    weights = [out_weight, weight_core, weight_chip, weight_cross]
    attended, mapped = finish(contexts, weights, own, feat_gain.reshape(1, 1024), proj_weight)

    before = lax.ppermute(mapped, "row", [(0, 1), (1, 2), (2, 3)])
    after = lax.ppermute(mapped, "row", [(1, 0), (2, 1), (3, 2)])
    place = lax.axis_index("row")
    edge = jnp.stack([place > 0, place < 3]).astype(jnp.int32)
    joined = join(
        edge,
        before,
        mapped,
        after,
        conv_one.reshape(3, 768, 256),
        conv_two.reshape(3, 768, 256),
    )
    return attended.reshape(tokens.shape), joined.reshape(tokens.shape[:3] + (256,))


def solution(mesh):
    in_specs = (
        P("frame", "row", None, None),
        P(),
        P(None, None, "row"),
        P("row", None),
        P("frame", None),
        P(),
        P(),
        P(),
        P(),
    )
    out_specs = (P("frame", "row", None, None), P("frame", "row", None, None))
    return jax.shard_map(shards, mesh=mesh, in_specs=in_specs, out_specs=out_specs, check_vma=False)
```

```python
import functools

import jax
import jax.numpy as jnp
import numpy as np
from jax import lax
from jax.experimental import pallas as pl
from jax.experimental.pallas import tpu as pltpu
from jax.sharding import PartitionSpec as P

EPSILON = 1e-06
HEAD = 64
HEADS_HERE = 4
FRAMES_HERE = 4
QUARTER = 64
WIDTH = 256
QUERY_SCALE = 1.4426950408889634 / 8.0
LARGE = 20 << 20
EDGE = 8
VMEM = pl.BlockSpec(memory_space=pltpu.VMEM)
SMEM = pl.BlockSpec(memory_space=pltpu.SMEM)
ANY = pl.BlockSpec(memory_space=pl.ANY)
HBM = pl.BlockSpec(memory_space=pltpu.HBM)

CORE_PAIRS = [(0, 1), (1, 0), (2, 3), (3, 2)]
CHIP_PAIRS = [(0, 2), (2, 0), (1, 3), (3, 1)]
CROSS_PAIRS = [(0, 3), (3, 0), (1, 2), (2, 1)]


def shifted(value, steps):
    count = lax.axis_size("frame")
    pairs = [(source, (source + steps) % count) for source in range(count)]
    return lax.ppermute(value, "frame", pairs)


def shifted_across(value, steps):
    count = lax.axis_size("frame")
    pairs = []
    for source in range(count):
        target = (source + steps) % count
        flip = 2 if source // EDGE != target // EDGE else 0
        pairs += [(source * 4 + row, target * 4 + (row ^ flip)) for row in range(4)]
    return lax.ppermute(value, ("frame", "row"), pairs)


def layer_norm(values, gain_vec):
    average = jnp.mean(values, axis=-1, keepdims=True)
    centered = values - average
    spread = jnp.mean(centered * centered, axis=-1, keepdims=True)
    return centered * lax.rsqrt(spread + EPSILON) * gain_vec


def norm_kernel(token_hbm, gain_hbm, out_ref, token, gain, sems):
    copies = [
        pltpu.make_async_copy(token_hbm, token, sems.at[0]),
        pltpu.make_async_copy(gain_hbm, gain, sems.at[1]),
    ]
    for copy in copies:
        copy.start()
    for copy in copies:
        copy.wait()
    values = layer_norm(token[...].astype(jnp.float32), gain[...])
    out_ref[...] = values.astype(jnp.bfloat16)


def normalise(tokens, gain):
    return pl.pallas_call(
        norm_kernel,
        in_specs=[HBM] * 2,
        out_specs=VMEM,
        out_shape=jax.ShapeDtypeStruct(tokens.shape, jnp.bfloat16),
        scratch_shapes=[
            pltpu.VMEM(tokens.shape, jnp.bfloat16),
            pltpu.VMEM(gain.shape, jnp.float32),
            pltpu.SemaphoreType.DMA((2,)),
        ],
        compiler_params=pltpu.CompilerParams(vmem_limit_bytes=LARGE),
        cost_estimate=pl.CostEstimate(flops=1 << 22, bytes_accessed=1 << 20, transcendentals=256),
    )(tokens, gain)


def project_kernel(blocks, queries, *refs):
    parts, refs = refs[: 2 * blocks], refs[2 * blocks :]
    weight_hbm, refs = refs[0], refs[1:]
    kv_refs, refs = refs[:blocks], refs[blocks:]
    if queries:
        query_ref, refs = refs[0], refs[1:]
    weight, sem = refs
    first = 0 if queries else 1
    copies = [
        pltpu.make_async_copy(weight_hbm.at[which], weight.at[which - first], sem.at[which - first])
        for which in range(first, 3)
    ]
    for which in ([1, 2, 0] if queries else [0, 1]):
        copies[which].start()
    for copy in copies:
        copy.wait()
    for block in range(blocks):
        rows = []
        for frame in range(FRAMES_HERE):
            for part in parts[2 * block : 2 * block + 2]:
                rows.append(part[frame * QUARTER : (frame + 1) * QUARTER])
        rows = jnp.concatenate(rows, axis=0)
        key = jnp.dot(rows, weight[1 - first], preferred_element_type=jnp.float32)
        key = key.astype(jnp.bfloat16)
        value = jnp.dot(rows, weight[2 - first], preferred_element_type=jnp.float32)
        value = value.T.astype(jnp.bfloat16)
        kv_ref = kv_refs[block]
        for frame in range(FRAMES_HERE):
            span = slice(frame * 128, (frame + 1) * 128)
            kv_ref[frame, 0:128, :] = key[span]
            kv_ref[frame, 128:256, 0:128] = value[0:128, span]
            kv_ref[frame, 128:256, 128:256] = value[128:256, span]
        if queries:
            query = jnp.dot(rows, weight[0], preferred_element_type=jnp.float32)
            query = (query * QUERY_SCALE).T.astype(jnp.bfloat16)
            for frame in range(FRAMES_HERE):
                query_ref[frame] = query[:, frame * 128 : (frame + 1) * 128]


def project(parts, weight, queries):
    blocks = len(parts) // 2
    out_shape = [jax.ShapeDtypeStruct((FRAMES_HERE, 256, 256), jnp.bfloat16)] * blocks
    if queries:
        out_shape.append(jax.ShapeDtypeStruct((FRAMES_HERE, WIDTH, 128), jnp.bfloat16))
    used = 3 if queries else 2
    return pl.pallas_call(
        functools.partial(project_kernel, blocks, queries),
        in_specs=[VMEM] * (2 * blocks) + [HBM],
        out_specs=[VMEM] * len(out_shape),
        out_shape=out_shape,
        scratch_shapes=[pltpu.VMEM((used, 1024, WIDTH), jnp.bfloat16), pltpu.SemaphoreType.DMA((used,))],
        compiler_params=pltpu.CompilerParams(vmem_limit_bytes=LARGE),
        cost_estimate=pl.CostEstimate(
            flops=2 * 512 * 1024 * 256 * used * blocks,
            bytes_accessed=3 << 20,
            transcendentals=0,
        ),
    )(*parts, weight)


def tile_slots(kind, frame):
    if kind == "own":
        return [
            (t // 2 + 4 * (t % 2), (t // 2 + 1) % 4 + 4 * (t % 2), 8 + t // 2) for t in range(8)
        ]
    if kind == "near":
        return [(t, (t + 1) % 8, 4 + t if t < 4 else 8 + t) for t in range(8)]
    slots = []
    for t in range(5):
        slot = frame + t
        slots.append((slot, frame + (t + 1) % 5, jnp.where(slot < 4, slot, slot + 12)))
    return slots


TILES = {"own": 8, "near": 8, "wide": 5}


def attend_kernel(kind, begins, ends, *refs):
    tiles, blocks = TILES[kind], 2
    valid_ref, query_a, query_b = refs[:3]
    refs = refs[3:]
    block_refs, refs = refs[:blocks], refs[blocks:]
    if not begins:
        high_in, total_in, refs = refs[0], refs[1], refs[2:]
    if ends:
        outs, refs = refs[:4], refs[4:]
    else:
        high_out, total_out, refs = refs[0], refs[1], refs[2:]
    held, sems = refs
    frame = pl.program_id(0)

    @pl.when(frame == 0)
    def _():
        copies = [
            pltpu.make_async_copy(
                block_refs[b],
                held.at[pl.ds(b * FRAMES_HERE, FRAMES_HERE)],
                sems.at[b],
            )
            for b in range(blocks)
        ]
        for copy in copies:
            copy.start()
        for copy in copies:
            copy.wait()

    index, keep = [], []
    for slot, other, position in tile_slots(kind, frame):
        there = valid_ref[frame, position]
        index.append(jnp.where(there != 0, slot, other))
        keep.append(there.astype(jnp.float32).astype(jnp.bfloat16))
    ones = jnp.ones((16, 128), jnp.bfloat16)
    zeros = jnp.zeros((HEAD, 256), jnp.bfloat16)

    def score(head):
        pair = head // 2
        query = jnp.concatenate(
            [
                query_a[frame, head * HEAD : (head + 1) * HEAD, :],
                query_b[frame, head * HEAD : (head + 1) * HEAD, :],
            ],
            axis=1,
        )
        both = [query, zeros] if head % 2 == 0 else [zeros, query]
        both = jnp.concatenate(both, axis=0)
        return [
            jnp.dot(
                held[index[t], 0:128, pair * 128 : (pair + 1) * 128],
                both,
                preferred_element_type=jnp.float32,
            )
            for t in range(tiles)
        ]

    def absorb(head, scores):
        pair = head // 2
        start = 128 + (head % 2) * HEAD
        high = scores[0].reshape(-1, 8, 256).max(axis=0)
        for s in scores[1:]:
            high = jnp.maximum(high, s.reshape(-1, 8, 256).max(axis=0))
        high = jnp.max(high, axis=0, keepdims=True)
        total = None
        if not begins:
            old = high_in[0, head, 0:1, :]
            high = jnp.maximum(high, old)
            total = total_in[0, head] * jnp.exp2(old - high)
        for t in range(0, tiles, 2):
            group = range(t, min(t + 2, tiles))
            weights = [jnp.exp2(scores[g] - high).astype(jnp.bfloat16) for g in group]
            sides = [
                jnp.concatenate(
                    [
                        held[index[g], start : start + HEAD, pair * 128 : (pair + 1) * 128],
                        ones,
                    ],
                    axis=0,
                )
                * keep[g]
                for g in group
            ]
            added = jnp.dot(
                jnp.concatenate(sides, axis=1),
                jnp.concatenate(weights, axis=0),
                preferred_element_type=jnp.float32,
            )
            total = added if total is None else total + added
        if ends:
            return total[0:HEAD] / total[HEAD : HEAD + 1]
        total_out[0, head] = total
        high_out[0, head] = jnp.broadcast_to(high, (8, 256))
        return None

    contexts = []
    scores = score(0)
    for head in range(HEADS_HERE):
        later = score(head + 1) if head + 1 < HEADS_HERE else None
        contexts.append(absorb(head, scores))
        scores = later
    if ends:
        context = jnp.concatenate(contexts, axis=0).T.astype(jnp.bfloat16)
        for j in range(4):
            outs[j][...] = context[j * QUARTER : (j + 1) * QUARTER]


def attend(kind, valid, query_a, query_b, block_list, state, ends=False):
    blocks, tiles = len(block_list), TILES[kind]
    high_spec = pl.BlockSpec((1, HEADS_HERE, 8, 256), lambda f: (f, 0, 0, 0))
    total_spec = pl.BlockSpec((1, HEADS_HERE, HEAD + 16, 256), lambda f: (f, 0, 0, 0))
    state_specs = [high_spec, total_spec]
    if ends:
        out_specs = [pl.BlockSpec((QUARTER, WIDTH), lambda f: (f, 0))] * 4
        out_shape = [jax.ShapeDtypeStruct((FRAMES_HERE * QUARTER, WIDTH), jnp.bfloat16)] * 4
    else:
        out_specs = state_specs
        out_shape = [
            jax.ShapeDtypeStruct((FRAMES_HERE, HEADS_HERE, 8, 256), jnp.float32),
            jax.ShapeDtypeStruct((FRAMES_HERE, HEADS_HERE, HEAD + 16, 256), jnp.float32),
        ]
    inputs = [valid, query_a, query_b, *block_list, *(state or ())]
    in_specs = [SMEM, VMEM, VMEM] + [ANY] * blocks + (state_specs if state else [])
    return pl.pallas_call(
        functools.partial(attend_kernel, kind, not state, ends),
        grid=(FRAMES_HERE,),
        in_specs=in_specs,
        out_specs=out_specs,
        out_shape=out_shape,
        scratch_shapes=[
            pltpu.VMEM((blocks * FRAMES_HERE, 256, 256), jnp.bfloat16),
            pltpu.SemaphoreType.DMA((blocks,)),
        ],
        compiler_params=pltpu.CompilerParams(
            vmem_limit_bytes=48 << 20, dimension_semantics=("arbitrary",)
        ),
        cost_estimate=pl.CostEstimate(
            flops=4 * 4 * tiles * 2 * 2 * 128 * 256 * 256,
            bytes_accessed=blocks << 19,
            transcendentals=16 * tiles * 128 * 256,
        ),
    )(*inputs)


def finish_kernel(c0, c1, c2, c3, w0, w1, w2, w3, token_ref, gain_ref, proj_ref, out_ref, map_ref):
    total = token_ref[...].astype(jnp.float32)
    mixed = jnp.dot(c0[...], w0[...], preferred_element_type=jnp.float32)
    for c, w in ((c1, w1), (c2, w2), (c3, w3)):
        mixed = mixed + jnp.dot(c[...], w[...], preferred_element_type=jnp.float32)
    attended = (total + mixed).astype(jnp.bfloat16)
    out_ref[...] = attended
    lifted = layer_norm(attended.astype(jnp.float32), gain_ref[...]).astype(jnp.bfloat16)
    mapped = jnp.dot(lifted, proj_ref[...], preferred_element_type=jnp.float32)
    map_ref[...] = mapped.astype(jnp.bfloat16)


def finish(contexts, weights, tokens, gain, proj):
    return pl.pallas_call(
        finish_kernel,
        in_specs=[VMEM] * 11,
        out_specs=[VMEM] * 2,
        out_shape=[
            jax.ShapeDtypeStruct((256, 1024), jnp.bfloat16),
            jax.ShapeDtypeStruct((256, 256), jnp.bfloat16),
        ],
        compiler_params=pltpu.CompilerParams(vmem_limit_bytes=32 << 20),
        cost_estimate=pl.CostEstimate(
            flops=2 * 256 * 1024 * 1280, bytes_accessed=4 << 20, transcendentals=0
        ),
    )(*contexts, *weights, tokens, gain, proj)


def join_kernel(edge_ref, before_ref, own_ref, after_ref, one_ref, two_ref, out_ref):
    def widen(values):
        count = values.shape[0]
        column = lax.broadcasted_iota(jnp.int32, (count, 256), 0) % 32
        left = jnp.where(column == 0, 0.0, pltpu.roll(values, 1, 0))
        right = jnp.where(column == 31, 0.0, pltpu.roll(values, count - 1, 0))
        return jnp.concatenate(
            [left.astype(jnp.bfloat16), values.astype(jnp.bfloat16), right.astype(jnp.bfloat16)],
            axis=1,
        )

    def conv(wide, rows_in, weight_ref):
        rows_out = rows_in - 2
        summed = None
        for a in range(3):
            window = jnp.concatenate(
                [
                    wide[(f * rows_in + a) * 32 : (f * rows_in + a + rows_out) * 32]
                    for f in range(FRAMES_HERE)
                ],
                axis=0,
            )
            added = jnp.dot(window, weight_ref[a], preferred_element_type=jnp.float32)
            summed = added if summed is None else summed + added
        return summed

    own = own_ref[...].astype(jnp.float32)
    before = before_ref[...].astype(jnp.float32)
    after = after_ref[...].astype(jnp.float32)
    six = []
    for f in range(FRAMES_HERE):
        span = slice(f * QUARTER, (f + 1) * QUARTER)
        six += [before[span], own[span], after[span]]
    six = jnp.maximum(jnp.concatenate(six, axis=0), 0.0)
    inner = conv(widen(six), 6, one_ref)
    inner = jnp.maximum(inner, 0.0)
    row = (lax.broadcasted_iota(jnp.int32, (512, 256), 0) // 32) % 4
    has_before, has_after = edge_ref[0], edge_ref[1]
    drop = ((row == 0) & (has_before == 0)) | ((row == 3) & (has_after == 0))
    inner = jnp.where(drop, 0.0, inner)
    joined = conv(widen(inner), 4, two_ref)
    out_ref[...] = (own + joined).astype(jnp.bfloat16)


def join(edge, before, own, after, one, two):
    return pl.pallas_call(
        join_kernel,
        in_specs=[SMEM] + [VMEM] * 5,
        out_specs=VMEM,
        out_shape=jax.ShapeDtypeStruct((256, 256), jnp.bfloat16),
        compiler_params=pltpu.CompilerParams(vmem_limit_bytes=32 << 20),
        cost_estimate=pl.CostEstimate(
            flops=2 * 768 * 2304 * 256, bytes_accessed=3 << 20, transcendentals=0
        ),
    )(edge, before, own, after, one, two)


def shards(
    tokens,
    norm_gain,
    qkv_weight,
    out_weight,
    key_offsets,
    feat_gain,
    proj_weight,
    conv_one,
    conv_two,
):
    own = tokens.reshape(FRAMES_HERE * QUARTER, 1024)
    core = lambda value: lax.ppermute(value, "row", CORE_PAIRS)
    chip = lambda value: lax.ppermute(value, "row", CHIP_PAIRS)
    tie = lax.optimization_barrier

    positions = np.arange(20)
    distance = positions[None, :] - 8 - np.arange(FRAMES_HERE)[:, None]
    valid = jnp.any(key_offsets[:, :, None] == distance[:, None, :], axis=1).astype(jnp.int32)
    place = lax.axis_index("frame") % EDGE
    last, first = place == EDGE - 1, place == 0

    normed = normalise(own, norm_gain.reshape(1, 1024))
    near = core(normed)
    far = chip(normed)
    behind = shifted_across(normed, 1)
    ahead = shifted_across(normed, -1)
    kv_a, query_a = project([normed, near], qkv_weight, True)
    far, kv_a = tie((far, kv_a))
    far_near = core(far)
    behind, ahead, kv_a = tie((behind, ahead, kv_a))
    behind_2, ahead_2 = shifted_across(behind, 1), shifted_across(ahead, -1)
    behind_near, ahead_near = core(behind), core(ahead)
    far_near, behind_near, ahead_near = tie((far_near, behind_near, ahead_near))
    kv_b, query_b = project([far, far_near], qkv_weight, True)
    behind_b = shifted(jnp.where(last, kv_a, kv_b), 1)
    ahead_b = shifted(jnp.where(first, kv_a, kv_b), -1)

    weight_core = core(out_weight)
    out_late, kv_b = tie((out_weight, kv_b))
    weight_chip = chip(out_late)
    weight_cross = core(weight_chip)

    state = attend("own", valid, query_a, query_b, [kv_a, kv_b], None)
    behind_a, ahead_a = project([behind, behind_near, ahead, ahead_near], qkv_weight, False)
    behind_2, ahead_2, state = tie((behind_2, ahead_2, state))
    behind_2near, ahead_2near = core(behind_2), core(ahead_2)
    state = attend("near", valid, query_a, query_b, [behind_a, ahead_a], state)
    behind_on = jnp.where(last, behind_a, behind_b)
    ahead_on = jnp.where(first, ahead_a, ahead_b)
    behind_on, ahead_on, state = tie((behind_on, ahead_on, state))
    behind_2b, ahead_2b = shifted(behind_on, 1), shifted(ahead_on, -1)
    behind_2a, ahead_2a = project(
        [behind_2, behind_2near, ahead_2, ahead_2near], qkv_weight, False
    )
    state = attend("wide", valid, query_a, query_b, [behind_2a, ahead_2a], state)
    state = attend("near", valid, query_a, query_b, [behind_b, ahead_b], state)
    parts = attend("wide", valid, query_a, query_b, [behind_2b, ahead_2b], state, True)

    contexts = [
        parts[0],
        core(parts[1]),
        chip(parts[2]),
        lax.ppermute(parts[3], "row", CROSS_PAIRS),
    ]
    weights = [out_weight, weight_core, weight_chip, weight_cross]
    attended, mapped = finish(contexts, weights, own, feat_gain.reshape(1, 1024), proj_weight)

    before = lax.ppermute(mapped, "row", [(0, 1), (1, 2), (2, 3)])
    after = lax.ppermute(mapped, "row", [(1, 0), (2, 1), (3, 2)])
    place = lax.axis_index("row")
    edge = jnp.stack([place > 0, place < 3]).astype(jnp.int32)
    joined = join(
        edge,
        before,
        mapped,
        after,
        conv_one.reshape(3, 768, 256),
        conv_two.reshape(3, 768, 256),
    )
    return attended.reshape(tokens.shape), joined.reshape(tokens.shape[:3] + (256,))


def solution(mesh):
    in_specs = (
        P("frame", "row", None, None),
        P(),
        P(None, None, "row"),
        P("row", None),
        P("frame", None),
        P(),
        P(),
        P(),
        P(),
    )
    out_specs = (P("frame", "row", None, None), P("frame", "row", None, None))
    return jax.shard_map(shards, mesh=mesh, in_specs=in_specs, out_specs=out_specs, check_vma=False)
```

```python
import functools

import jax
import jax.numpy as jnp
import numpy as np
from jax import lax
from jax.experimental import pallas as pl
from jax.experimental.pallas import tpu as pltpu
from jax.sharding import PartitionSpec as P

EPSILON = 1e-06
HEAD = 64
HEADS_HERE = 4
FRAMES_HERE = 4
QUARTER = 64
WIDTH = 256
QUERY_SCALE = 1.4426950408889634 / 8.0
LARGE = 20 << 20
BRIEF = pl.CostEstimate(flops=1, bytes_accessed=1, transcendentals=0)
EDGE = 8
VMEM = pl.BlockSpec(memory_space=pltpu.VMEM)
SMEM = pl.BlockSpec(memory_space=pltpu.SMEM)
ANY = pl.BlockSpec(memory_space=pl.ANY)
HBM = pl.BlockSpec(memory_space=pltpu.HBM)

CORE_PAIRS = [(0, 1), (1, 0), (2, 3), (3, 2)]
CHIP_PAIRS = [(0, 2), (2, 0), (1, 3), (3, 1)]
CROSS_PAIRS = [(0, 3), (3, 0), (1, 2), (2, 1)]


def swapped(value, offset, across=False):
    count = lax.axis_size("frame")
    pairs = []
    for low in range(offset, count, 2):
        high = (low + 1) % count
        flip = 2 if across and low // EDGE != high // EDGE else 0
        for row in range(4):
            pairs.append((low * 4 + row, high * 4 + (row ^ flip)))
            pairs.append((high * 4 + (row ^ flip), low * 4 + row))
    return lax.ppermute(value, ("frame", "row"), pairs)


def layer_norm(values, gain_vec):
    average = jnp.mean(values, axis=-1, keepdims=True)
    centered = values - average
    spread = jnp.mean(centered * centered, axis=-1, keepdims=True)
    return centered * lax.rsqrt(spread + EPSILON) * gain_vec


def norm_kernel(token_hbm, gain_hbm, out_ref, token, gain, sems):
    copies = [
        pltpu.make_async_copy(token_hbm, token, sems.at[0]),
        pltpu.make_async_copy(gain_hbm, gain, sems.at[1]),
    ]
    for copy in copies:
        copy.start()
    for copy in copies:
        copy.wait()
    values = layer_norm(token[...].astype(jnp.float32), gain[...])
    out_ref[...] = values.astype(jnp.bfloat16)


def normalise(tokens, gain):
    return pl.pallas_call(
        norm_kernel,
        in_specs=[HBM] * 2,
        out_specs=VMEM,
        out_shape=jax.ShapeDtypeStruct(tokens.shape, jnp.bfloat16),
        scratch_shapes=[
            pltpu.VMEM(tokens.shape, jnp.bfloat16),
            pltpu.VMEM(gain.shape, jnp.float32),
            pltpu.SemaphoreType.DMA((2,)),
        ],
        compiler_params=pltpu.CompilerParams(vmem_limit_bytes=60 << 20),
        cost_estimate=BRIEF,
    )(tokens, gain)


def project_kernel(blocks, queries, *refs):
    parts, refs = refs[: 2 * blocks], refs[2 * blocks :]
    weight_hbm, refs = refs[0], refs[1:]
    kv_refs, refs = refs[:blocks], refs[blocks:]
    if queries:
        query_ref, refs = refs[0], refs[1:]
    weight, sem = refs
    first = 0 if queries else 1
    copies = [
        pltpu.make_async_copy(weight_hbm.at[which], weight.at[which - first], sem.at[which - first])
        for which in range(first, 3)
    ]
    for which in ([1, 2, 0] if queries else [0, 1]):
        copies[which].start()
    for copy in copies:
        copy.wait()
    for block in range(blocks):
        rows = []
        for frame in range(FRAMES_HERE):
            for part in parts[2 * block : 2 * block + 2]:
                rows.append(part[frame * QUARTER : (frame + 1) * QUARTER])
        rows = jnp.concatenate(rows, axis=0)
        key = jnp.dot(rows, weight[1 - first], preferred_element_type=jnp.float32)
        key = key.astype(jnp.bfloat16)
        value = jnp.dot(rows, weight[2 - first], preferred_element_type=jnp.float32)
        value = value.T.astype(jnp.bfloat16)
        kv_ref = kv_refs[block]
        for frame in range(FRAMES_HERE):
            span = slice(frame * 128, (frame + 1) * 128)
            kv_ref[frame, 0:128, :] = key[span]
            kv_ref[frame, 128:256, 0:128] = value[0:128, span]
            kv_ref[frame, 128:256, 128:256] = value[128:256, span]
        if queries:
            query = jnp.dot(rows, weight[0], preferred_element_type=jnp.float32)
            query = (query * QUERY_SCALE).T.astype(jnp.bfloat16)
            for frame in range(FRAMES_HERE):
                query_ref[frame] = query[:, frame * 128 : (frame + 1) * 128]


def project(parts, weight, queries):
    blocks = len(parts) // 2
    out_shape = [jax.ShapeDtypeStruct((FRAMES_HERE, 256, 256), jnp.bfloat16)] * blocks
    if queries:
        out_shape.append(jax.ShapeDtypeStruct((FRAMES_HERE, WIDTH, 128), jnp.bfloat16))
    used = 3 if queries else 2
    return pl.pallas_call(
        functools.partial(project_kernel, blocks, queries),
        in_specs=[VMEM] * (2 * blocks) + [HBM],
        out_specs=[VMEM] * len(out_shape),
        out_shape=out_shape,
        scratch_shapes=[pltpu.VMEM((used, 1024, WIDTH), jnp.bfloat16), pltpu.SemaphoreType.DMA((used,))],
        compiler_params=pltpu.CompilerParams(vmem_limit_bytes=LARGE),
        cost_estimate=BRIEF,
    )(*parts, weight)


def tile_slots(kind, frame):
    if kind == "own":
        return [
            (t // 2 + 4 * (t % 2), (t // 2 + 1) % 4 + 4 * (t % 2), 8 + t // 2) for t in range(8)
        ]
    if kind == "near":
        return [(t, (t + 1) % 8, 4 + t if t < 4 else 8 + t) for t in range(8)]
    slots = []
    for t in range(5):
        slot = frame + t
        slots.append((slot, frame + (t + 1) % 5, jnp.where(slot < 4, slot, slot + 12)))
    return slots


TILES = {"own": 8, "near": 8, "wide": 5}


def attend_kernel(kind, begins, ends, *refs):
    tiles, blocks = TILES[kind], 2
    valid_ref, query_a, query_b = refs[:3]
    refs = refs[3:]
    block_refs, refs = refs[:blocks], refs[blocks:]
    if not begins:
        high_in, total_in, refs = refs[0], refs[1], refs[2:]
    if ends:
        outs, refs = refs[:4], refs[4:]
    else:
        high_out, total_out, refs = refs[0], refs[1], refs[2:]
    held, sems = refs
    frame = pl.program_id(0)

    @pl.when(frame == 0)
    def _():
        first = 0 if kind == "own" else valid_ref[FRAMES_HERE, 0] * FRAMES_HERE
        copies = [
            pltpu.make_async_copy(block_refs[0], held.at[pl.ds(first, FRAMES_HERE)], sems.at[0]),
            pltpu.make_async_copy(
                block_refs[1], held.at[pl.ds(FRAMES_HERE - first, FRAMES_HERE)], sems.at[1]
            ),
        ]
        for copy in copies:
            copy.start()
        for copy in copies:
            copy.wait()

    index, keep = [], []
    for slot, other, position in tile_slots(kind, frame):
        there = valid_ref[frame, position]
        index.append(jnp.where(there != 0, slot, other))
        keep.append(there.astype(jnp.float32).astype(jnp.bfloat16))
    ones = jnp.ones((16, 128), jnp.bfloat16)
    zeros = jnp.zeros((HEAD, 256), jnp.bfloat16)

    def score(head):
        pair = head // 2
        query = jnp.concatenate(
            [
                query_a[frame, head * HEAD : (head + 1) * HEAD, :],
                query_b[frame, head * HEAD : (head + 1) * HEAD, :],
            ],
            axis=1,
        )
        both = [query, zeros] if head % 2 == 0 else [zeros, query]
        both = jnp.concatenate(both, axis=0)
        return [
            jnp.dot(
                held[index[t], 0:128, pair * 128 : (pair + 1) * 128],
                both,
                preferred_element_type=jnp.float32,
            )
            for t in range(tiles)
        ]

    def absorb(head, scores):
        pair = head // 2
        start = 128 + (head % 2) * HEAD
        high = scores[0].reshape(-1, 8, 256).max(axis=0)
        for s in scores[1:]:
            high = jnp.maximum(high, s.reshape(-1, 8, 256).max(axis=0))
        high = jnp.max(high, axis=0, keepdims=True)
        total = None
        if not begins:
            old = high_in[0, head, 0:1, :]
            high = jnp.maximum(high, old)
            total = total_in[0, head] * jnp.exp2(old - high)
        for t in range(0, tiles, 2):
            group = range(t, min(t + 2, tiles))
            weights = [jnp.exp2(scores[g] - high).astype(jnp.bfloat16) for g in group]
            sides = [
                jnp.concatenate(
                    [
                        held[index[g], start : start + HEAD, pair * 128 : (pair + 1) * 128],
                        ones,
                    ],
                    axis=0,
                )
                * keep[g]
                for g in group
            ]
            added = jnp.dot(
                jnp.concatenate(sides, axis=1),
                jnp.concatenate(weights, axis=0),
                preferred_element_type=jnp.float32,
            )
            total = added if total is None else total + added
        if ends:
            return total[0:HEAD] / total[HEAD : HEAD + 1]
        total_out[0, head] = total
        high_out[0, head] = jnp.broadcast_to(high, (8, 256))
        return None

    contexts = []
    scores = score(0)
    for head in range(HEADS_HERE):
        later = score(head + 1) if head + 1 < HEADS_HERE else None
        contexts.append(absorb(head, scores))
        scores = later
    if ends:
        context = jnp.concatenate(contexts, axis=0).T.astype(jnp.bfloat16)
        for j in range(4):
            outs[j][...] = context[j * QUARTER : (j + 1) * QUARTER]


def attend(kind, valid, query_a, query_b, block_list, state, ends=False):
    blocks, tiles = len(block_list), TILES[kind]
    high_spec = pl.BlockSpec((1, HEADS_HERE, 8, 256), lambda f: (f, 0, 0, 0))
    total_spec = pl.BlockSpec((1, HEADS_HERE, HEAD + 16, 256), lambda f: (f, 0, 0, 0))
    state_specs = [high_spec, total_spec]
    if ends:
        out_specs = [pl.BlockSpec((QUARTER, WIDTH), lambda f: (f, 0))] * 4
        out_shape = [jax.ShapeDtypeStruct((FRAMES_HERE * QUARTER, WIDTH), jnp.bfloat16)] * 4
    else:
        out_specs = state_specs
        out_shape = [
            jax.ShapeDtypeStruct((FRAMES_HERE, HEADS_HERE, 8, 256), jnp.float32),
            jax.ShapeDtypeStruct((FRAMES_HERE, HEADS_HERE, HEAD + 16, 256), jnp.float32),
        ]
    inputs = [valid, query_a, query_b, *block_list, *(state or ())]
    in_specs = [SMEM, VMEM, VMEM] + [ANY] * blocks + (state_specs if state else [])
    return pl.pallas_call(
        functools.partial(attend_kernel, kind, not state, ends),
        grid=(FRAMES_HERE,),
        in_specs=in_specs,
        out_specs=out_specs,
        out_shape=out_shape,
        scratch_shapes=[
            pltpu.VMEM((blocks * FRAMES_HERE, 256, 256), jnp.bfloat16),
            pltpu.SemaphoreType.DMA((blocks,)),
        ],
        compiler_params=pltpu.CompilerParams(
            vmem_limit_bytes=48 << 20, dimension_semantics=("arbitrary",)
        ),
        cost_estimate=BRIEF,
    )(*inputs)


def finish_kernel(c0, c1, c2, c3, w0, w1, w2, w3, token_ref, gain_ref, proj_ref, out_ref, map_ref):
    total = token_ref[...].astype(jnp.float32)
    mixed = jnp.dot(c0[...], w0[...], preferred_element_type=jnp.float32)
    for c, w in ((c1, w1), (c2, w2), (c3, w3)):
        mixed = mixed + jnp.dot(c[...], w[...], preferred_element_type=jnp.float32)
    attended = (total + mixed).astype(jnp.bfloat16)
    out_ref[...] = attended
    lifted = layer_norm(attended.astype(jnp.float32), gain_ref[...]).astype(jnp.bfloat16)
    mapped = jnp.dot(lifted, proj_ref[...], preferred_element_type=jnp.float32)
    map_ref[...] = mapped.astype(jnp.bfloat16)


def finish(contexts, weights, tokens, gain, proj):
    return pl.pallas_call(
        finish_kernel,
        in_specs=[VMEM] * 11,
        out_specs=[VMEM] * 2,
        out_shape=[
            jax.ShapeDtypeStruct((256, 1024), jnp.bfloat16),
            jax.ShapeDtypeStruct((256, 256), jnp.bfloat16),
        ],
        compiler_params=pltpu.CompilerParams(vmem_limit_bytes=32 << 20),
        cost_estimate=BRIEF,
    )(*contexts, *weights, tokens, gain, proj)


def join_kernel(row_ref, beside_ref, own_ref, across_ref, one_ref, two_ref, out_ref):
    def widen(values):
        count = values.shape[0]
        column = lax.broadcasted_iota(jnp.int32, (count, 256), 0) % 32
        left = jnp.where(column == 0, 0.0, pltpu.roll(values, 1, 0))
        right = jnp.where(column == 31, 0.0, pltpu.roll(values, count - 1, 0))
        return jnp.concatenate(
            [left.astype(jnp.bfloat16), values.astype(jnp.bfloat16), right.astype(jnp.bfloat16)],
            axis=1,
        )

    def conv(wide, rows_in, weight_ref):
        rows_out = rows_in - 2
        summed = None
        for a in range(3):
            window = jnp.concatenate(
                [
                    wide[(f * rows_in + a) * 32 : (f * rows_in + a + rows_out) * 32]
                    for f in range(FRAMES_HERE)
                ],
                axis=0,
            )
            added = jnp.dot(window, weight_ref[a], preferred_element_type=jnp.float32)
            summed = added if summed is None else summed + added
        return summed

    own = own_ref[...].astype(jnp.float32)
    place = row_ref[0]
    odd = place % 2 == 1
    beside = beside_ref[...].astype(jnp.float32)
    across = across_ref[...].astype(jnp.float32)
    before = jnp.where(odd, beside, across)
    after = jnp.where(odd, across, beside)
    six = []
    for f in range(FRAMES_HERE):
        span = slice(f * QUARTER, (f + 1) * QUARTER)
        six += [before[span], own[span], after[span]]
    six = jnp.maximum(jnp.concatenate(six, axis=0), 0.0)
    inner = conv(widen(six), 6, one_ref)
    inner = jnp.maximum(inner, 0.0)
    row = (lax.broadcasted_iota(jnp.int32, (512, 256), 0) // 32) % 4
    drop = ((row == 0) & (place == 0)) | ((row == 3) & (place == 3))
    inner = jnp.where(drop, 0.0, inner)
    joined = conv(widen(inner), 4, two_ref)
    out_ref[...] = (own + joined).astype(jnp.bfloat16)


def join(row, beside, own, across, one, two):
    return pl.pallas_call(
        join_kernel,
        in_specs=[SMEM] + [VMEM] * 5,
        out_specs=VMEM,
        out_shape=jax.ShapeDtypeStruct((256, 256), jnp.bfloat16),
        compiler_params=pltpu.CompilerParams(vmem_limit_bytes=32 << 20),
        cost_estimate=BRIEF,
    )(row, beside, own, across, one, two)


def shards(
    tokens,
    norm_gain,
    qkv_weight,
    out_weight,
    key_offsets,
    feat_gain,
    proj_weight,
    conv_one,
    conv_two,
):
    own = tokens.reshape(FRAMES_HERE * QUARTER, 1024)
    core = lambda value: lax.ppermute(value, "row", CORE_PAIRS)
    chip = lambda value: lax.ppermute(value, "row", CHIP_PAIRS)
    tie = lax.optimization_barrier

    positions = np.arange(20)
    distance = positions[None, :] - 8 - np.arange(FRAMES_HERE)[:, None]
    valid = jnp.any(key_offsets[:, :, None] == distance[:, None, :], axis=1).astype(jnp.int32)
    block = lax.axis_index("frame")
    even = 1 - block % 2
    valid = jnp.concatenate([valid, jnp.full((1, 20), even, jnp.int32)], axis=0)
    edge_block = (block % EDGE == 0) | (block % EDGE == EDGE - 1)

    normed = normalise(own, norm_gain.reshape(1, 1024))
    near = core(normed)
    far = chip(normed)
    side = swapped(normed, 0)
    other = swapped(normed, 1, True)
    kv_a, query_a = project([normed, near], qkv_weight, True)
    far, side, other, kv_a = tie((far, side, other, kv_a))
    far_near, side_near, other_near = core(far), core(side), core(other)
    side_2, other_2 = swapped(other, 0), swapped(side, 1, True)
    far_near, side_near, other_near = tie((far_near, side_near, other_near))
    kv_b, query_b = project([far, far_near], qkv_weight, True)
    side_b = swapped(kv_b, 0)
    other_b = swapped(jnp.where(edge_block, kv_a, kv_b), 1)
    out_late, kv_b = tie((out_weight, kv_b))
    weight_chip = chip(out_late)

    state = attend("own", valid, query_a, query_b, [kv_a, kv_b], None)
    side, state = tie((side, state))
    side_a, other_a = project([side, side_near, other, other_near], qkv_weight, False)
    side_2, other_2, side_a, other_a = tie((side_2, other_2, side_a, other_a))
    side_2near, other_2near = core(side_2), core(other_2)
    state = attend("near", valid, query_a, query_b, [side_a, other_a], state)
    on_side, on_other = other_b, jnp.where(edge_block, side_a, side_b)
    on_side, on_other, state = tie((on_side, on_other, state))
    side_2b, other_2b = swapped(on_side, 0), swapped(on_other, 1)
    side_2a, other_2a = project([side_2, side_2near, other_2, other_2near], qkv_weight, False)
    state = attend("wide", valid, query_a, query_b, [side_2a, other_2a], state)
    out_last, weight_chip, state = tie((out_weight, weight_chip, state))
    weight_core = core(out_last)
    weight_cross = core(weight_chip)
    state = attend("near", valid, query_a, query_b, [side_b, other_b], state)
    parts = attend("wide", valid, query_a, query_b, [side_2b, other_2b], state, True)

    contexts = [
        parts[0],
        core(parts[1]),
        chip(parts[2]),
        lax.ppermute(parts[3], "row", CROSS_PAIRS),
    ]
    weights = [out_weight, weight_core, weight_chip, weight_cross]
    attended, mapped = finish(contexts, weights, own, feat_gain.reshape(1, 1024), proj_weight)

    across = lax.ppermute(mapped, "row", [(1, 2), (2, 1)])
    beside = core(mapped)
    place = lax.axis_index("row").astype(jnp.int32).reshape(1)
    joined = join(
        place,
        beside,
        mapped,
        across,
        conv_one.reshape(3, 768, 256),
        conv_two.reshape(3, 768, 256),
    )
    return attended.reshape(tokens.shape), joined.reshape(tokens.shape[:3] + (256,))


def solution(mesh):
    in_specs = (
        P("frame", "row", None, None),
        P(),
        P(None, None, "row"),
        P("row", None),
        P("frame", None),
        P(),
        P(),
        P(),
        P(),
    )
    out_specs = (P("frame", "row", None, None), P("frame", "row", None, None))
    return jax.shard_map(shards, mesh=mesh, in_specs=in_specs, out_specs=out_specs, check_vma=False)
```

```python
import functools

import jax
import jax.numpy as jnp
import numpy as np
from jax import lax
from jax.experimental import pallas as pl
from jax.experimental.pallas import tpu as pltpu
from jax.sharding import PartitionSpec as P

EPSILON = 1e-06
HEAD = 64
HEADS_HERE = 4
FRAMES_HERE = 4
QUARTER = 64
WIDTH = 256
QUERY_SCALE = 1.4426950408889634 / 8.0
LARGE = 20 << 20
BRIEF = pl.CostEstimate(flops=1, bytes_accessed=1, transcendentals=0)
EDGE = 8
VMEM = pl.BlockSpec(memory_space=pltpu.VMEM)
SMEM = pl.BlockSpec(memory_space=pltpu.SMEM)
ANY = pl.BlockSpec(memory_space=pl.ANY)
HBM = pl.BlockSpec(memory_space=pltpu.HBM)

CORE_PAIRS = [(0, 1), (1, 0), (2, 3), (3, 2)]
CHIP_PAIRS = [(0, 2), (2, 0), (1, 3), (3, 1)]
CROSS_PAIRS = [(0, 3), (3, 0), (1, 2), (2, 1)]


def swapped(value, offset, across=False):
    count = lax.axis_size("frame")
    pairs = []
    for low in range(offset, count, 2):
        high = (low + 1) % count
        flip = 2 if across and low // EDGE != high // EDGE else 0
        for row in range(4):
            pairs.append((low * 4 + row, high * 4 + (row ^ flip)))
            pairs.append((high * 4 + (row ^ flip), low * 4 + row))
    return lax.ppermute(value, ("frame", "row"), pairs)


def layer_norm(values, gain_vec):
    average = jnp.mean(values, axis=-1, keepdims=True)
    centered = values - average
    spread = jnp.mean(centered * centered, axis=-1, keepdims=True)
    return centered * lax.rsqrt(spread + EPSILON) * gain_vec


def norm_kernel(token_hbm, gain_hbm, out_ref, token, gain, sems):
    copies = [
        pltpu.make_async_copy(token_hbm, token, sems.at[0]),
        pltpu.make_async_copy(gain_hbm, gain, sems.at[1]),
    ]
    for copy in copies:
        copy.start()
    for copy in copies:
        copy.wait()
    values = layer_norm(token[...].astype(jnp.float32), gain[...])
    out_ref[...] = values.astype(jnp.bfloat16)


def normalise(tokens, gain):
    return pl.pallas_call(
        norm_kernel,
        in_specs=[HBM] * 2,
        out_specs=VMEM,
        out_shape=jax.ShapeDtypeStruct(tokens.shape, jnp.bfloat16),
        scratch_shapes=[
            pltpu.VMEM(tokens.shape, jnp.bfloat16),
            pltpu.VMEM(gain.shape, jnp.float32),
            pltpu.SemaphoreType.DMA((2,)),
        ],
        compiler_params=pltpu.CompilerParams(vmem_limit_bytes=60 << 20),
        cost_estimate=BRIEF,
    )(tokens, gain)


def project_kernel(blocks, queries, *refs):
    parts, refs = refs[: 2 * blocks], refs[2 * blocks :]
    weight_hbm, refs = refs[0], refs[1:]
    kv_refs, refs = refs[:blocks], refs[blocks:]
    if queries:
        query_ref, refs = refs[0], refs[1:]
    weight, sem = refs
    first = 0 if queries else 1
    copies = [
        pltpu.make_async_copy(weight_hbm.at[which], weight.at[which - first], sem.at[which - first])
        for which in range(first, 3)
    ]
    for which in ([1, 2, 0] if queries else [0, 1]):
        copies[which].start()
    for copy in copies:
        copy.wait()
    for block in range(blocks):
        rows = []
        for frame in range(FRAMES_HERE):
            for part in parts[2 * block : 2 * block + 2]:
                rows.append(part[frame * QUARTER : (frame + 1) * QUARTER])
        rows = jnp.concatenate(rows, axis=0)
        key = jnp.dot(rows, weight[1 - first], preferred_element_type=jnp.float32)
        key = key.astype(jnp.bfloat16)
        value = jnp.dot(rows, weight[2 - first], preferred_element_type=jnp.float32)
        value = value.T.astype(jnp.bfloat16)
        kv_ref = kv_refs[block]
        for frame in range(FRAMES_HERE):
            span = slice(frame * 128, (frame + 1) * 128)
            kv_ref[frame, 0:128, :] = key[span]
            kv_ref[frame, 128:256, 0:128] = value[0:128, span]
            kv_ref[frame, 128:256, 128:256] = value[128:256, span]
        if queries:
            query = jnp.dot(rows, weight[0], preferred_element_type=jnp.float32)
            query = (query * QUERY_SCALE).T.astype(jnp.bfloat16)
            for frame in range(FRAMES_HERE):
                query_ref[frame] = query[:, frame * 128 : (frame + 1) * 128]


def project(parts, weight, queries):
    blocks = len(parts) // 2
    out_shape = [jax.ShapeDtypeStruct((FRAMES_HERE, 256, 256), jnp.bfloat16)] * blocks
    if queries:
        out_shape.append(jax.ShapeDtypeStruct((FRAMES_HERE, WIDTH, 128), jnp.bfloat16))
    used = 3 if queries else 2
    return pl.pallas_call(
        functools.partial(project_kernel, blocks, queries),
        in_specs=[VMEM] * (2 * blocks) + [HBM],
        out_specs=[VMEM] * len(out_shape),
        out_shape=out_shape,
        scratch_shapes=[pltpu.VMEM((used, 1024, WIDTH), jnp.bfloat16), pltpu.SemaphoreType.DMA((used,))],
        compiler_params=pltpu.CompilerParams(vmem_limit_bytes=LARGE),
        cost_estimate=BRIEF,
    )(*parts, weight)


def tile_slots(kind, frame):
    if kind == "own":
        return [
            (t // 2 + 4 * (t % 2), (t // 2 + 1) % 4 + 4 * (t % 2), 8 + t // 2) for t in range(8)
        ]
    if kind == "near":
        return [(t, (t + 1) % 8, 4 + t if t < 4 else 8 + t) for t in range(8)]
    slots = []
    for t in range(5):
        slot = frame + t
        slots.append((slot, frame + (t + 1) % 5, jnp.where(slot < 4, slot, slot + 12)))
    return slots


TILES = {"own": 8, "near": 8, "wide": 5}


def weigh(scores, high):
    return jnp.exp2(scores - high).astype(jnp.bfloat16)


def attend_kernel(kind, begins, ends, *refs):
    tiles, blocks = TILES[kind], 2
    valid_ref, query_a, query_b = refs[:3]
    refs = refs[3:]
    block_refs, refs = refs[:blocks], refs[blocks:]
    if not begins:
        high_in, total_in, refs = refs[0], refs[1], refs[2:]
    if ends:
        outs, refs = refs[:4], refs[4:]
    else:
        high_out, total_out, refs = refs[0], refs[1], refs[2:]
    held, sems = refs
    frame = pl.program_id(0)

    @pl.when(frame == 0)
    def _():
        first = 0 if kind == "own" else valid_ref[FRAMES_HERE, 0] * FRAMES_HERE
        copies = [
            pltpu.make_async_copy(block_refs[0], held.at[pl.ds(first, FRAMES_HERE)], sems.at[0]),
            pltpu.make_async_copy(
                block_refs[1], held.at[pl.ds(FRAMES_HERE - first, FRAMES_HERE)], sems.at[1]
            ),
        ]
        for copy in copies:
            copy.start()
        for copy in copies:
            copy.wait()

    index, keep = [], []
    for slot, other, position in tile_slots(kind, frame):
        there = valid_ref[frame, position]
        index.append(jnp.where(there != 0, slot, other))
        keep.append(there.astype(jnp.float32).astype(jnp.bfloat16))
    ones = jnp.ones((16, 128), jnp.bfloat16)
    zeros = jnp.zeros((HEAD, 256), jnp.bfloat16)

    def score(head):
        pair = head // 2
        query = jnp.concatenate(
            [
                query_a[frame, head * HEAD : (head + 1) * HEAD, :],
                query_b[frame, head * HEAD : (head + 1) * HEAD, :],
            ],
            axis=1,
        )
        both = [query, zeros] if head % 2 == 0 else [zeros, query]
        both = jnp.concatenate(both, axis=0)
        return [
            jnp.dot(
                held[index[t], 0:128, pair * 128 : (pair + 1) * 128],
                both,
                preferred_element_type=jnp.float32,
            )
            for t in range(tiles)
        ]

    def absorb(head, scores):
        pair = head // 2
        start = 128 + (head % 2) * HEAD
        high = scores[0].reshape(-1, 8, 256).max(axis=0)
        for s in scores[1:]:
            high = jnp.maximum(high, s.reshape(-1, 8, 256).max(axis=0))
        high = jnp.max(high, axis=0, keepdims=True)
        total = None
        if not begins:
            old = high_in[0, head, 0:1, :]
            high = jnp.maximum(high, old)
            total = total_in[0, head] * jnp.exp2(old - high)
        for t in range(0, tiles, 2):
            group = range(t, min(t + 2, tiles))
            weights = [weigh(scores[g], high) for g in group]
            sides = [
                jnp.concatenate(
                    [
                        held[index[g], start : start + HEAD, pair * 128 : (pair + 1) * 128],
                        ones,
                    ],
                    axis=0,
                )
                * keep[g]
                for g in group
            ]
            added = jnp.dot(
                jnp.concatenate(sides, axis=1),
                jnp.concatenate(weights, axis=0),
                preferred_element_type=jnp.float32,
            )
            total = added if total is None else total + added
        if ends:
            return total[0:HEAD] / total[HEAD : HEAD + 1]
        total_out[0, head] = total
        high_out[0, head] = jnp.broadcast_to(high, (8, 256))
        return None

    contexts = []
    scores = score(0)
    for head in range(HEADS_HERE):
        later = score(head + 1) if head + 1 < HEADS_HERE else None
        contexts.append(absorb(head, scores))
        scores = later
    if ends:
        context = jnp.concatenate(contexts, axis=0).T.astype(jnp.bfloat16)
        for j in range(4):
            outs[j][...] = context[j * QUARTER : (j + 1) * QUARTER]


def attend(kind, valid, query_a, query_b, block_list, state, ends=False):
    blocks, tiles = len(block_list), TILES[kind]
    high_spec = pl.BlockSpec((1, HEADS_HERE, 8, 256), lambda f: (f, 0, 0, 0))
    total_spec = pl.BlockSpec((1, HEADS_HERE, HEAD + 16, 256), lambda f: (f, 0, 0, 0))
    state_specs = [high_spec, total_spec]
    if ends:
        out_specs = [pl.BlockSpec((QUARTER, WIDTH), lambda f: (f, 0))] * 4
        out_shape = [jax.ShapeDtypeStruct((FRAMES_HERE * QUARTER, WIDTH), jnp.bfloat16)] * 4
    else:
        out_specs = state_specs
        out_shape = [
            jax.ShapeDtypeStruct((FRAMES_HERE, HEADS_HERE, 8, 256), jnp.float32),
            jax.ShapeDtypeStruct((FRAMES_HERE, HEADS_HERE, HEAD + 16, 256), jnp.float32),
        ]
    inputs = [valid, query_a, query_b, *block_list, *(state or ())]
    in_specs = [SMEM, VMEM, VMEM] + [ANY] * blocks + (state_specs if state else [])
    return pl.pallas_call(
        functools.partial(attend_kernel, kind, not state, ends),
        grid=(FRAMES_HERE,),
        in_specs=in_specs,
        out_specs=out_specs,
        out_shape=out_shape,
        scratch_shapes=[
            pltpu.VMEM((blocks * FRAMES_HERE, 256, 256), jnp.bfloat16),
            pltpu.SemaphoreType.DMA((blocks,)),
        ],
        compiler_params=pltpu.CompilerParams(
            vmem_limit_bytes=48 << 20, dimension_semantics=("arbitrary",)
        ),
        cost_estimate=BRIEF,
    )(*inputs)


def finish_kernel(c0, c1, c2, c3, w0, w1, w2, w3, token_ref, gain_ref, proj_ref, out_ref, map_ref):
    total = token_ref[...].astype(jnp.float32)
    mixed = jnp.dot(c0[...], w0[...], preferred_element_type=jnp.float32)
    for c, w in ((c1, w1), (c2, w2), (c3, w3)):
        mixed = mixed + jnp.dot(c[...], w[...], preferred_element_type=jnp.float32)
    attended = (total + mixed).astype(jnp.bfloat16)
    out_ref[...] = attended
    lifted = layer_norm(attended.astype(jnp.float32), gain_ref[...]).astype(jnp.bfloat16)
    mapped = jnp.dot(lifted, proj_ref[...], preferred_element_type=jnp.float32)
    map_ref[...] = mapped.astype(jnp.bfloat16)


def finish(contexts, weights, tokens, gain, proj):
    return pl.pallas_call(
        finish_kernel,
        in_specs=[VMEM] * 11,
        out_specs=[VMEM] * 2,
        out_shape=[
            jax.ShapeDtypeStruct((256, 1024), jnp.bfloat16),
            jax.ShapeDtypeStruct((256, 256), jnp.bfloat16),
        ],
        compiler_params=pltpu.CompilerParams(vmem_limit_bytes=32 << 20),
        cost_estimate=BRIEF,
    )(*contexts, *weights, tokens, gain, proj)


def join_kernel(row_ref, beside_ref, own_ref, across_ref, one_ref, two_ref, out_ref):
    def widen(values):
        count = values.shape[0]
        column = lax.broadcasted_iota(jnp.int32, (count, 256), 0) % 32
        left = jnp.where(column == 0, 0.0, pltpu.roll(values, 1, 0))
        right = jnp.where(column == 31, 0.0, pltpu.roll(values, count - 1, 0))
        return jnp.concatenate(
            [left.astype(jnp.bfloat16), values.astype(jnp.bfloat16), right.astype(jnp.bfloat16)],
            axis=1,
        )

    def conv(wide, rows_in, weight_ref):
        rows_out = rows_in - 2
        summed = None
        for a in range(3):
            window = jnp.concatenate(
                [
                    wide[(f * rows_in + a) * 32 : (f * rows_in + a + rows_out) * 32]
                    for f in range(FRAMES_HERE)
                ],
                axis=0,
            )
            added = jnp.dot(window, weight_ref[a], preferred_element_type=jnp.float32)
            summed = added if summed is None else summed + added
        return summed

    own = own_ref[...].astype(jnp.float32)
    place = row_ref[0]
    odd = place % 2 == 1
    beside = beside_ref[...].astype(jnp.float32)
    across = across_ref[...].astype(jnp.float32)
    before = jnp.where(odd, beside, across)
    after = jnp.where(odd, across, beside)
    six = []
    for f in range(FRAMES_HERE):
        span = slice(f * QUARTER, (f + 1) * QUARTER)
        six += [before[span], own[span], after[span]]
    six = jnp.maximum(jnp.concatenate(six, axis=0), 0.0)
    inner = conv(widen(six), 6, one_ref)
    inner = jnp.maximum(inner, 0.0)
    row = (lax.broadcasted_iota(jnp.int32, (512, 256), 0) // 32) % 4
    drop = ((row == 0) & (place == 0)) | ((row == 3) & (place == 3))
    inner = jnp.where(drop, 0.0, inner)
    joined = conv(widen(inner), 4, two_ref)
    out_ref[...] = (own + joined).astype(jnp.bfloat16)


def join(row, beside, own, across, one, two):
    return pl.pallas_call(
        join_kernel,
        in_specs=[SMEM] + [VMEM] * 5,
        out_specs=VMEM,
        out_shape=jax.ShapeDtypeStruct((256, 256), jnp.bfloat16),
        compiler_params=pltpu.CompilerParams(vmem_limit_bytes=32 << 20),
        cost_estimate=BRIEF,
    )(row, beside, own, across, one, two)


def shards(
    tokens,
    norm_gain,
    qkv_weight,
    out_weight,
    key_offsets,
    feat_gain,
    proj_weight,
    conv_one,
    conv_two,
):
    own = tokens.reshape(FRAMES_HERE * QUARTER, 1024)
    core = lambda value: lax.ppermute(value, "row", CORE_PAIRS)
    chip = lambda value: lax.ppermute(value, "row", CHIP_PAIRS)
    tie = lax.optimization_barrier

    positions = np.arange(20)
    distance = positions[None, :] - 8 - np.arange(FRAMES_HERE)[:, None]
    valid = jnp.any(key_offsets[:, :, None] == distance[:, None, :], axis=1).astype(jnp.int32)
    block = lax.axis_index("frame")
    even = 1 - block % 2
    valid = jnp.concatenate([valid, jnp.full((1, 20), even, jnp.int32)], axis=0)
    edge_block = (block % EDGE == 0) | (block % EDGE == EDGE - 1)

    normed = normalise(own, norm_gain.reshape(1, 1024))
    near = core(normed)
    far = chip(normed)
    side = swapped(normed, 0)
    other = swapped(normed, 1, True)
    kv_a, query_a = project([normed, near], qkv_weight, True)
    far, kv_a = tie((far, kv_a))
    far_near = core(far)
    out_late, far = tie((out_weight, far))
    weight_chip = chip(out_late)
    far_near, side, other = tie((far_near, side, other))
    side_2, other_2 = swapped(other, 0), swapped(side, 1, True)
    kv_b, query_b = project([far, far_near], qkv_weight, True)
    side_b = swapped(kv_b, 0)
    other_b = swapped(jnp.where(edge_block, kv_a, kv_b), 1)
    side_near, other_near = core(side), core(other)

    state = attend("own", valid, query_a, query_b, [kv_a, kv_b], None)
    side, state = tie((side, state))
    side_a, other_a = project([side, side_near, other, other_near], qkv_weight, False)
    side_2, other_2, side_a, other_a = tie((side_2, other_2, side_a, other_a))
    side_2near, other_2near = core(side_2), core(other_2)
    state = attend("near", valid, query_a, query_b, [side_a, other_a], state)
    on_side, on_other = other_b, jnp.where(edge_block, side_a, side_b)
    on_side, on_other, state = tie((on_side, on_other, state))
    side_2b, other_2b = swapped(on_side, 0), swapped(on_other, 1)
    side_2a, other_2a = project([side_2, side_2near, other_2, other_2near], qkv_weight, False)
    state = attend("wide", valid, query_a, query_b, [side_2a, other_2a], state)
    state = attend("near", valid, query_a, query_b, [side_b, other_b], state)
    out_last, weight_chip, state = tie((out_weight, weight_chip, state))
    weight_core = core(out_last)
    weight_cross = core(weight_chip)
    parts = attend("wide", valid, query_a, query_b, [side_2b, other_2b], state, True)

    contexts = [
        parts[0],
        core(parts[1]),
        chip(parts[2]),
        lax.ppermute(parts[3], "row", CROSS_PAIRS),
    ]
    weights = [out_weight, weight_core, weight_chip, weight_cross]
    attended, mapped = finish(contexts, weights, own, feat_gain.reshape(1, 1024), proj_weight)

    across = lax.ppermute(mapped, "row", [(1, 2), (2, 1)])
    beside = core(mapped)
    place = lax.axis_index("row").astype(jnp.int32).reshape(1)
    joined = join(
        place,
        beside,
        mapped,
        across,
        conv_one.reshape(3, 768, 256),
        conv_two.reshape(3, 768, 256),
    )
    return attended.reshape(tokens.shape), joined.reshape(tokens.shape[:3] + (256,))


def solution(mesh):
    in_specs = (
        P("frame", "row", None, None),
        P(),
        P(None, None, "row"),
        P("row", None),
        P("frame", None),
        P(),
        P(),
        P(),
        P(),
    )
    out_specs = (P("frame", "row", None, None), P("frame", "row", None, None))
    return jax.shard_map(shards, mesh=mesh, in_specs=in_specs, out_specs=out_specs, check_vma=False)
```

```python
import functools

import jax
import jax.numpy as jnp
import numpy as np
from jax import lax
from jax.experimental import pallas as pl
from jax.experimental.pallas import tpu as pltpu
from jax.sharding import PartitionSpec as P

EPSILON = 1e-06
HEAD = 64
HEADS_HERE = 4
FRAMES_HERE = 4
QUARTER = 64
WIDTH = 256
QUERY_SCALE = 1.4426950408889634 / 8.0
LARGE = 20 << 20
BRIEF = pl.CostEstimate(flops=1, bytes_accessed=1, transcendentals=0)
EDGE = 8
VMEM = pl.BlockSpec(memory_space=pltpu.VMEM)
SMEM = pl.BlockSpec(memory_space=pltpu.SMEM)
ANY = pl.BlockSpec(memory_space=pl.ANY)
HBM = pl.BlockSpec(memory_space=pltpu.HBM)

CORE_PAIRS = [(0, 1), (1, 0), (2, 3), (3, 2)]
CHIP_PAIRS = [(0, 2), (2, 0), (1, 3), (3, 1)]
CROSS_PAIRS = [(0, 3), (3, 0), (1, 2), (2, 1)]


def swapped(value, offset, across=False):
    count = lax.axis_size("frame")
    pairs = []
    for low in range(offset, count, 2):
        high = (low + 1) % count
        flip = 2 if across and low // EDGE != high // EDGE else 0
        for row in range(4):
            pairs.append((low * 4 + row, high * 4 + (row ^ flip)))
            pairs.append((high * 4 + (row ^ flip), low * 4 + row))
    return lax.ppermute(value, ("frame", "row"), pairs)


def layer_norm(values, gain_vec):
    average = jnp.mean(values, axis=-1, keepdims=True)
    centered = values - average
    spread = jnp.mean(centered * centered, axis=-1, keepdims=True)
    return centered * lax.rsqrt(spread + EPSILON) * gain_vec


def norm_kernel(token_hbm, gain_hbm, out_ref, token, gain, sems):
    copies = [
        pltpu.make_async_copy(token_hbm, token, sems.at[0]),
        pltpu.make_async_copy(gain_hbm, gain, sems.at[1]),
    ]
    for copy in copies:
        copy.start()
    for copy in copies:
        copy.wait()
    values = layer_norm(token[...].astype(jnp.float32), gain[...])
    out_ref[...] = values.astype(jnp.bfloat16)


def normalise(tokens, gain):
    return pl.pallas_call(
        norm_kernel,
        in_specs=[HBM] * 2,
        out_specs=VMEM,
        out_shape=jax.ShapeDtypeStruct(tokens.shape, jnp.bfloat16),
        scratch_shapes=[
            pltpu.VMEM(tokens.shape, jnp.bfloat16),
            pltpu.VMEM(gain.shape, jnp.float32),
            pltpu.SemaphoreType.DMA((2,)),
        ],
        compiler_params=pltpu.CompilerParams(vmem_limit_bytes=60 << 20),
        cost_estimate=BRIEF,
    )(tokens, gain)


def project_kernel(blocks, queries, ordered, *refs):
    if ordered:
        valid_ref, refs = refs[0], refs[1:]
        first = valid_ref[FRAMES_HERE, 0] * FRAMES_HERE
        starts = [first, FRAMES_HERE - first]
    else:
        starts = [0] * blocks
    parts, refs = refs[: 2 * blocks], refs[2 * blocks :]
    weight_hbm, refs = refs[0], refs[1:]
    if ordered:
        kv_refs, refs = [refs[0]] * blocks, refs[1:]
    else:
        kv_refs, refs = refs[:blocks], refs[blocks:]
    if queries:
        query_ref, refs = refs[0], refs[1:]
    weight, sem = refs
    skip = 0 if queries else 1
    copies = [
        pltpu.make_async_copy(weight_hbm.at[which], weight.at[which - skip], sem.at[which - skip])
        for which in range(skip, 3)
    ]
    for which in ([1, 2, 0] if queries else [0, 1]):
        copies[which].start()
    for copy in copies:
        copy.wait()
    for block in range(blocks):
        rows = []
        for frame in range(FRAMES_HERE):
            for part in parts[2 * block : 2 * block + 2]:
                rows.append(part[frame * QUARTER : (frame + 1) * QUARTER])
        rows = jnp.concatenate(rows, axis=0)
        key = jnp.dot(rows, weight[1 - skip], preferred_element_type=jnp.float32)
        key = key.astype(jnp.bfloat16)
        value = jnp.dot(rows, weight[2 - skip], preferred_element_type=jnp.float32)
        value = value.T.astype(jnp.bfloat16)
        kv_ref = kv_refs[block]
        for frame in range(FRAMES_HERE):
            span = slice(frame * 128, (frame + 1) * 128)
            place = starts[block] + frame
            kv_ref[place, 0:128, :] = key[span]
            kv_ref[place, 128:256, 0:128] = value[0:128, span]
            kv_ref[place, 128:256, 128:256] = value[128:256, span]
        if queries:
            query = jnp.dot(rows, weight[0], preferred_element_type=jnp.float32)
            query = (query * QUERY_SCALE).T.astype(jnp.bfloat16)
            for frame in range(FRAMES_HERE):
                query_ref[frame] = query[:, frame * 128 : (frame + 1) * 128]


def project(parts, weight, queries, valid=None):
    blocks = len(parts) // 2
    ordered = valid is not None
    if ordered:
        out_shape = [jax.ShapeDtypeStruct((2 * FRAMES_HERE, 256, 256), jnp.bfloat16)]
    else:
        out_shape = [jax.ShapeDtypeStruct((FRAMES_HERE, 256, 256), jnp.bfloat16)] * blocks
    if queries:
        out_shape.append(jax.ShapeDtypeStruct((FRAMES_HERE, WIDTH, 128), jnp.bfloat16))
    used = 3 if queries else 2
    return pl.pallas_call(
        functools.partial(project_kernel, blocks, queries, ordered),
        in_specs=[SMEM] * ordered + [VMEM] * (2 * blocks) + [HBM],
        out_specs=[VMEM] * len(out_shape),
        out_shape=out_shape,
        scratch_shapes=[pltpu.VMEM((used, 1024, WIDTH), jnp.bfloat16), pltpu.SemaphoreType.DMA((used,))],
        compiler_params=pltpu.CompilerParams(vmem_limit_bytes=LARGE),
        cost_estimate=BRIEF,
    )(*([valid] if ordered else []), *parts, weight)


def weigh(scores, high):
    return jnp.exp2(scores - high).astype(jnp.bfloat16)


def near_tiles(refs, even, frame):
    tiles = []
    for which, ref in enumerate(refs):
        ahead = even if which == 0 else 1 - even
        for t in range(FRAMES_HERE):
            tiles.append((ref, t, (t + 1) % FRAMES_HERE, 4 + 8 * ahead + t))
    return tiles


def own_tiles(refs):
    return [(ref, t, (t + 1) % FRAMES_HERE, 8 + t) for t in range(FRAMES_HERE) for ref in refs]


def wide_tiles(ref, frame):
    tiles = []
    for t in range(FRAMES_HERE + 1):
        slot = frame + t
        position = jnp.where(slot < FRAMES_HERE, slot, slot + 12)
        tiles.append((ref, slot, frame + (t + 1) % (FRAMES_HERE + 1), position))
    return tiles


def attend_kernel(kind, *refs):
    begins, ends = kind == "first", kind == "last"
    valid_ref, query_a, query_b = refs[:3]
    refs = refs[3:]
    blocks = {"first": 4, "middle": 3, "last": 2}[kind]
    block_refs, refs = refs[:blocks], refs[blocks:]
    if not begins:
        high_in, total_in, refs = refs[0], refs[1], refs[2:]
    even = valid_ref[FRAMES_HERE, 0]
    if ends:
        outs, (held, sems) = refs[:4], refs[4:]
        first = even * FRAMES_HERE
        copies = [
            pltpu.make_async_copy(block_refs[0], held.at[pl.ds(first, FRAMES_HERE)], sems.at[0]),
            pltpu.make_async_copy(
                block_refs[1], held.at[pl.ds(FRAMES_HERE - first, FRAMES_HERE)], sems.at[1]
            ),
        ]
        for copy in copies:
            copy.start()
        for copy in copies:
            copy.wait()
    else:
        high_out, total_out = refs
    ones = jnp.ones((16, 128), jnp.bfloat16)
    zeros = jnp.zeros((HEAD, 256), jnp.bfloat16)

    def one_frame(frame, carried):
        if kind == "first":
            tiles = own_tiles(block_refs[:2]) + near_tiles(block_refs[2:], even, frame)
        elif kind == "middle":
            tiles = wide_tiles(block_refs[0], frame) + near_tiles(block_refs[1:], even, frame)
        else:
            tiles = wide_tiles(held, frame)
        held_refs, index, keep = [], [], []
        for ref, slot, other, position in tiles:
            there = valid_ref[frame, position]
            held_refs.append(ref)
            index.append(jnp.where(there != 0, slot, other))
            keep.append(there.astype(jnp.float32).astype(jnp.bfloat16))
        count = len(tiles)

        def score(head):
            pair = head // 2
            query = jnp.concatenate(
                [
                    query_a[frame, head * HEAD : (head + 1) * HEAD, :],
                    query_b[frame, head * HEAD : (head + 1) * HEAD, :],
                ],
                axis=1,
            )
            both = [query, zeros] if head % 2 == 0 else [zeros, query]
            both = jnp.concatenate(both, axis=0)
            return [
                jnp.dot(
                    held_refs[t][index[t], 0:128, pair * 128 : (pair + 1) * 128],
                    both,
                    preferred_element_type=jnp.float32,
                )
                for t in range(count)
            ]

        def absorb(head, scores):
            pair = head // 2
            start = 128 + (head % 2) * HEAD
            high = scores[0].reshape(-1, 8, 256).max(axis=0)
            for s in scores[1:]:
                high = jnp.maximum(high, s.reshape(-1, 8, 256).max(axis=0))
            high = jnp.max(high, axis=0, keepdims=True)
            total = None
            if not begins:
                old = high_in[frame, head, 0:1, :]
                high = jnp.maximum(high, old)
                total = total_in[frame, head] * jnp.exp2(old - high)
            for t in range(0, count, 2):
                group = range(t, min(t + 2, count))
                weights = [weigh(scores[g], high) for g in group]
                sides = []
                for g in group:
                    value = held_refs[g][
                        index[g], start : start + HEAD, pair * 128 : (pair + 1) * 128
                    ]
                    sides.append(jnp.concatenate([value, ones], axis=0) * keep[g])
                added = jnp.dot(
                    jnp.concatenate(sides, axis=1),
                    jnp.concatenate(weights, axis=0),
                    preferred_element_type=jnp.float32,
                )
                total = added if total is None else total + added
            if ends:
                return total[0:HEAD] / total[HEAD : HEAD + 1]
            total_out[frame, head] = total
            high_out[frame, head] = jnp.broadcast_to(high, (8, 256))
            return None

        contexts = []
        scores = score(0)
        for head in range(HEADS_HERE):
            later = score(head + 1) if head + 1 < HEADS_HERE else None
            contexts.append(absorb(head, scores))
            scores = later
        if ends:
            context = jnp.concatenate(contexts, axis=0).T.astype(jnp.bfloat16)
            rows = pl.ds(pl.multiple_of(frame * QUARTER, QUARTER), QUARTER)
            for j in range(4):
                outs[j][rows, :] = context[j * QUARTER : (j + 1) * QUARTER]
        return carried

    lax.fori_loop(0, FRAMES_HERE, one_frame, 0)


def attend(kind, valid, query_a, query_b, block_list, state=()):
    ends = kind == "last"
    if ends:
        out_shape = [jax.ShapeDtypeStruct((FRAMES_HERE * QUARTER, WIDTH), jnp.bfloat16)] * 4
        scratch = [
            pltpu.VMEM((2 * FRAMES_HERE, 256, 256), jnp.bfloat16),
            pltpu.SemaphoreType.DMA((2,)),
        ]
    else:
        out_shape = [
            jax.ShapeDtypeStruct((FRAMES_HERE, HEADS_HERE, 8, 256), jnp.float32),
            jax.ShapeDtypeStruct((FRAMES_HERE, HEADS_HERE, HEAD + 16, 256), jnp.float32),
        ]
        scratch = []
    inputs = [valid, query_a, query_b, *block_list, *state]
    return pl.pallas_call(
        functools.partial(attend_kernel, kind),
        in_specs=[SMEM] + [VMEM] * (len(inputs) - 1),
        out_specs=[VMEM] * len(out_shape),
        out_shape=out_shape,
        scratch_shapes=scratch,
        compiler_params=pltpu.CompilerParams(vmem_limit_bytes=36 << 20),
        cost_estimate=BRIEF,
    )(*inputs)


def finish_kernel(c0, c1, c2, c3, w0, w1, w2, w3, token_ref, gain_ref, proj_ref, out_ref, map_ref):
    total = token_ref[...].astype(jnp.float32)
    mixed = jnp.dot(c0[...], w0[...], preferred_element_type=jnp.float32)
    for c, w in ((c1, w1), (c2, w2), (c3, w3)):
        mixed = mixed + jnp.dot(c[...], w[...], preferred_element_type=jnp.float32)
    attended = (total + mixed).astype(jnp.bfloat16)
    out_ref[...] = attended
    lifted = layer_norm(attended.astype(jnp.float32), gain_ref[...]).astype(jnp.bfloat16)
    mapped = jnp.dot(lifted, proj_ref[...], preferred_element_type=jnp.float32)
    map_ref[...] = mapped.astype(jnp.bfloat16)


def finish(contexts, weights, tokens, gain, proj):
    return pl.pallas_call(
        finish_kernel,
        in_specs=[VMEM] * 11,
        out_specs=[VMEM] * 2,
        out_shape=[
            jax.ShapeDtypeStruct((256, 1024), jnp.bfloat16),
            jax.ShapeDtypeStruct((256, 256), jnp.bfloat16),
        ],
        compiler_params=pltpu.CompilerParams(vmem_limit_bytes=32 << 20),
        cost_estimate=BRIEF,
    )(*contexts, *weights, tokens, gain, proj)


def join_kernel(row_ref, beside_ref, own_ref, across_ref, one_ref, two_ref, out_ref):
    def widen(values):
        count = values.shape[0]
        column = lax.broadcasted_iota(jnp.int32, (count, 256), 0) % 32
        left = jnp.where(column == 0, 0.0, pltpu.roll(values, 1, 0))
        right = jnp.where(column == 31, 0.0, pltpu.roll(values, count - 1, 0))
        return jnp.concatenate(
            [left.astype(jnp.bfloat16), values.astype(jnp.bfloat16), right.astype(jnp.bfloat16)],
            axis=1,
        )

    def conv(wide, rows_in, weight_ref):
        rows_out = rows_in - 2
        summed = None
        for a in range(3):
            window = jnp.concatenate(
                [
                    wide[(f * rows_in + a) * 32 : (f * rows_in + a + rows_out) * 32]
                    for f in range(FRAMES_HERE)
                ],
                axis=0,
            )
            added = jnp.dot(window, weight_ref[a], preferred_element_type=jnp.float32)
            summed = added if summed is None else summed + added
        return summed

    own = own_ref[...].astype(jnp.float32)
    place = row_ref[0]
    odd = place % 2 == 1
    beside = beside_ref[...].astype(jnp.float32)
    across = across_ref[...].astype(jnp.float32)
    before = jnp.where(odd, beside, across)
    after = jnp.where(odd, across, beside)
    six = []
    for f in range(FRAMES_HERE):
        span = slice(f * QUARTER, (f + 1) * QUARTER)
        six += [before[span], own[span], after[span]]
    six = jnp.maximum(jnp.concatenate(six, axis=0), 0.0)
    inner = conv(widen(six), 6, one_ref)
    inner = jnp.maximum(inner, 0.0)
    row = (lax.broadcasted_iota(jnp.int32, (512, 256), 0) // 32) % 4
    drop = ((row == 0) & (place == 0)) | ((row == 3) & (place == 3))
    inner = jnp.where(drop, 0.0, inner)
    joined = conv(widen(inner), 4, two_ref)
    out_ref[...] = (own + joined).astype(jnp.bfloat16)


def join(row, beside, own, across, one, two):
    return pl.pallas_call(
        join_kernel,
        in_specs=[SMEM] + [VMEM] * 5,
        out_specs=VMEM,
        out_shape=jax.ShapeDtypeStruct((256, 256), jnp.bfloat16),
        compiler_params=pltpu.CompilerParams(vmem_limit_bytes=32 << 20),
        cost_estimate=BRIEF,
    )(row, beside, own, across, one, two)


def shards(
    tokens,
    norm_gain,
    qkv_weight,
    out_weight,
    key_offsets,
    feat_gain,
    proj_weight,
    conv_one,
    conv_two,
):
    own = tokens.reshape(FRAMES_HERE * QUARTER, 1024)
    core = lambda value: lax.ppermute(value, "row", CORE_PAIRS)
    chip = lambda value: lax.ppermute(value, "row", CHIP_PAIRS)
    tie = lax.optimization_barrier

    positions = np.arange(20)
    distance = positions[None, :] - 8 - np.arange(FRAMES_HERE)[:, None]
    valid = jnp.any(key_offsets[:, :, None] == distance[:, None, :], axis=1).astype(jnp.int32)
    block = lax.axis_index("frame")
    even = 1 - block % 2
    valid = jnp.concatenate([valid, jnp.full((1, 20), even, jnp.int32)], axis=0)
    edge_block = (block % EDGE == 0) | (block % EDGE == EDGE - 1)

    normed = normalise(own, norm_gain.reshape(1, 1024))
    near = core(normed)
    far = chip(normed)
    side = swapped(normed, 0)
    other = swapped(normed, 1, True)
    kv_a, query_a = project([normed, near], qkv_weight, True)
    far, kv_a = tie((far, kv_a))
    far_near = core(far)
    out_late, far = tie((out_weight, far))
    weight_chip = chip(out_late)
    far_near, side, other = tie((far_near, side, other))
    side_near, other_near = core(side), core(other)
    side_2, other_2 = swapped(other, 0), swapped(side, 1, True)
    far_near, side_near, other_near = tie((far_near, side_near, other_near))
    kv_b, query_b = project([far, far_near], qkv_weight, True)
    side_b = swapped(kv_b, 0)
    other_b = swapped(jnp.where(edge_block, kv_a, kv_b), 1)
    side_a, other_a = project([side, side_near, other, other_near], qkv_weight, False)
    query_b, weight_chip = tie((query_b, weight_chip))
    state = attend("first", valid, query_a, query_b, [kv_a, kv_b, side_a, other_a])
    on_side, on_other = other_b, jnp.where(edge_block, side_a, side_b)
    on_side, on_other, side_2, other_2, state = tie((on_side, on_other, side_2, other_2, state))
    side_2b, other_2b = swapped(on_side, 0), swapped(on_other, 1)
    side_2near, other_2near = core(side_2), core(other_2)
    (wide_a,) = project([side_2, side_2near, other_2, other_2near], qkv_weight, False, valid)
    state = attend("middle", valid, query_a, query_b, [wide_a, side_b, other_b], state)
    out_last, weight_chip, state = tie((out_weight, weight_chip, state))
    weight_core = core(out_last)
    weight_cross = core(weight_chip)
    parts = attend("last", valid, query_a, query_b, [side_2b, other_2b], state)

    contexts = [
        parts[0],
        core(parts[1]),
        chip(parts[2]),
        lax.ppermute(parts[3], "row", CROSS_PAIRS),
    ]
    weights = [out_weight, weight_core, weight_chip, weight_cross]
    attended, mapped = finish(contexts, weights, own, feat_gain.reshape(1, 1024), proj_weight)

    across = lax.ppermute(mapped, "row", [(1, 2), (2, 1)])
    beside = core(mapped)
    place = lax.axis_index("row").astype(jnp.int32).reshape(1)
    joined = join(
        place,
        beside,
        mapped,
        across,
        conv_one.reshape(3, 768, 256),
        conv_two.reshape(3, 768, 256),
    )
    return attended.reshape(tokens.shape), joined.reshape(tokens.shape[:3] + (256,))


def solution(mesh):
    in_specs = (
        P("frame", "row", None, None),
        P(),
        P(None, None, "row"),
        P("row", None),
        P("frame", None),
        P(),
        P(),
        P(),
        P(),
    )
    out_specs = (P("frame", "row", None, None), P("frame", "row", None, None))
    return jax.shard_map(shards, mesh=mesh, in_specs=in_specs, out_specs=out_specs, check_vma=False)
```

```python
import functools

import jax
import jax.numpy as jnp
import numpy as np
from jax import lax
from jax.experimental import pallas as pl
from jax.experimental.pallas import tpu as pltpu
from jax.sharding import PartitionSpec as P

EPSILON = 1e-06
HEAD = 64
HEADS_HERE = 4
FRAMES_HERE = 4
QUARTER = 64
WIDTH = 256
QUERY_SCALE = 1.4426950408889634 / 8.0
LARGE = 20 << 20
BRIEF = pl.CostEstimate(flops=1, bytes_accessed=1, transcendentals=0)
EDGE = 8
VMEM = pl.BlockSpec(memory_space=pltpu.VMEM)
SMEM = pl.BlockSpec(memory_space=pltpu.SMEM)
ANY = pl.BlockSpec(memory_space=pl.ANY)
HBM = pl.BlockSpec(memory_space=pltpu.HBM)

CORE_PAIRS = [(0, 1), (1, 0), (2, 3), (3, 2)]
CHIP_PAIRS = [(0, 2), (2, 0), (1, 3), (3, 1)]
CROSS_PAIRS = [(0, 3), (3, 0), (1, 2), (2, 1)]


def swapped(value, offset, across=False):
    count = lax.axis_size("frame")
    pairs = []
    for low in range(offset, count, 2):
        high = (low + 1) % count
        flip = 2 if across and low // EDGE != high // EDGE else 0
        for row in range(4):
            pairs.append((low * 4 + row, high * 4 + (row ^ flip)))
            pairs.append((high * 4 + (row ^ flip), low * 4 + row))
    return lax.ppermute(value, ("frame", "row"), pairs)


def layer_norm(values, gain_vec):
    average = jnp.mean(values, axis=-1, keepdims=True)
    centered = values - average
    spread = jnp.mean(centered * centered, axis=-1, keepdims=True)
    return centered * lax.rsqrt(spread + EPSILON) * gain_vec


def norm_kernel(token_hbm, gain_hbm, out_ref, token, gain, sems):
    copies = [
        pltpu.make_async_copy(token_hbm, token, sems.at[0]),
        pltpu.make_async_copy(gain_hbm, gain, sems.at[1]),
    ]
    for copy in copies:
        copy.start()
    for copy in copies:
        copy.wait()
    values = layer_norm(token[...].astype(jnp.float32), gain[...])
    out_ref[...] = values.astype(jnp.bfloat16)


def normalise(tokens, gain):
    return pl.pallas_call(
        norm_kernel,
        in_specs=[HBM] * 2,
        out_specs=VMEM,
        out_shape=jax.ShapeDtypeStruct(tokens.shape, jnp.bfloat16),
        scratch_shapes=[
            pltpu.VMEM(tokens.shape, jnp.bfloat16),
            pltpu.VMEM(gain.shape, jnp.float32),
            pltpu.SemaphoreType.DMA((2,)),
        ],
        compiler_params=pltpu.CompilerParams(vmem_limit_bytes=60 << 20),
        cost_estimate=BRIEF,
    )(tokens, gain)


def project_kernel(blocks, queries, *refs):
    parts, refs = refs[: 2 * blocks], refs[2 * blocks :]
    weight_hbm, refs = refs[0], refs[1:]
    kv_refs, refs = refs[:blocks], refs[blocks:]
    if queries:
        query_ref, refs = refs[0], refs[1:]
    weight, sem = refs
    skip = 0 if queries else 1
    copies = [
        pltpu.make_async_copy(weight_hbm.at[which], weight.at[which - skip], sem.at[which - skip])
        for which in range(skip, 3)
    ]
    for which in ([1, 2, 0] if queries else [0, 1]):
        copies[which].start()
    for copy in copies:
        copy.wait()
    for block in range(blocks):
        rows = []
        for frame in range(FRAMES_HERE):
            for part in parts[2 * block : 2 * block + 2]:
                rows.append(part[frame * QUARTER : (frame + 1) * QUARTER])
        rows = jnp.concatenate(rows, axis=0)
        key = jnp.dot(rows, weight[1 - skip], preferred_element_type=jnp.float32)
        key = key.astype(jnp.bfloat16)
        value = jnp.dot(rows, weight[2 - skip], preferred_element_type=jnp.float32)
        value = value.T.astype(jnp.bfloat16)
        kv_ref = kv_refs[block]
        for frame in range(FRAMES_HERE):
            span = slice(frame * 128, (frame + 1) * 128)
            kv_ref[frame, 0:128, :] = key[span]
            kv_ref[frame, 128:256, 0:128] = value[0:128, span]
            kv_ref[frame, 128:256, 128:256] = value[128:256, span]
        if queries:
            query = jnp.dot(rows, weight[0], preferred_element_type=jnp.float32)
            query = (query * QUERY_SCALE).T.astype(jnp.bfloat16)
            for frame in range(FRAMES_HERE):
                query_ref[frame] = query[:, frame * 128 : (frame + 1) * 128]


def project(parts, weight, queries):
    blocks = len(parts) // 2
    out_shape = [jax.ShapeDtypeStruct((FRAMES_HERE, 256, 256), jnp.bfloat16)] * blocks
    if queries:
        out_shape.append(jax.ShapeDtypeStruct((FRAMES_HERE, WIDTH, 128), jnp.bfloat16))
    used = 3 if queries else 2
    return pl.pallas_call(
        functools.partial(project_kernel, blocks, queries),
        in_specs=[VMEM] * (2 * blocks) + [HBM],
        out_specs=[VMEM] * len(out_shape),
        out_shape=out_shape,
        scratch_shapes=[pltpu.VMEM((used, 1024, WIDTH), jnp.bfloat16), pltpu.SemaphoreType.DMA((used,))],
        compiler_params=pltpu.CompilerParams(vmem_limit_bytes=LARGE),
        cost_estimate=BRIEF,
    )(*parts, weight)


def weigh(scores, high):
    return jnp.exp2(scores - high).astype(jnp.bfloat16)


def near_tiles(refs, even):
    tiles = []
    for which, ref in enumerate(refs):
        ahead = even if which == 0 else 1 - even
        for t in range(FRAMES_HERE):
            tiles.append((ref, t, (t + 1) % FRAMES_HERE, 4 + 8 * ahead + t))
    return tiles


def own_tiles(refs):
    return [(ref, t, (t + 1) % FRAMES_HERE, 8 + t) for t in range(FRAMES_HERE) for ref in refs]


def wide_tiles(ref, frame):
    tiles = []
    for t in range(FRAMES_HERE + 1):
        slot = frame + t
        position = jnp.where(slot < FRAMES_HERE, slot, slot + 12)
        tiles.append((ref, slot, frame + (t + 1) % (FRAMES_HERE + 1), position))
    return tiles


def attend_kernel(kind, *refs):
    begins, ends = kind == "own", kind == "last"
    valid_ref, query_a, query_b = refs[:3]
    refs = refs[3:]
    wide = kind in ("wide", "last")
    block_refs, refs = refs[:2], refs[2:]
    if not begins:
        high_in, total_in, refs = refs[0], refs[1], refs[2:]
    even = valid_ref[FRAMES_HERE, 0]
    if ends:
        outs, refs = refs[:4], refs[4:]
    else:
        high_out, total_out, refs = refs[0], refs[1], refs[2:]
    if wide:
        held, sems = refs
        first = even * FRAMES_HERE
        copies = [
            pltpu.make_async_copy(block_refs[0], held.at[pl.ds(first, FRAMES_HERE)], sems.at[0]),
            pltpu.make_async_copy(
                block_refs[1], held.at[pl.ds(FRAMES_HERE - first, FRAMES_HERE)], sems.at[1]
            ),
        ]
        for copy in copies:
            copy.start()
        for copy in copies:
            copy.wait()
    ones = jnp.ones((16, 128), jnp.bfloat16)
    zeros = jnp.zeros((HEAD, 256), jnp.bfloat16)

    def one_frame(frame, carried):
        if kind == "own":
            tiles = own_tiles(block_refs)
        elif kind == "near":
            tiles = near_tiles(block_refs, even)
        else:
            tiles = wide_tiles(held, frame)
        held_refs, index, keep = [], [], []
        for ref, slot, other, position in tiles:
            there = valid_ref[frame, position]
            held_refs.append(ref)
            index.append(jnp.where(there != 0, slot, other))
            keep.append(there.astype(jnp.float32).astype(jnp.bfloat16))
        count = len(tiles)

        def score(head):
            pair = head // 2
            query = jnp.concatenate(
                [
                    query_a[frame, head * HEAD : (head + 1) * HEAD, :],
                    query_b[frame, head * HEAD : (head + 1) * HEAD, :],
                ],
                axis=1,
            )
            both = [query, zeros] if head % 2 == 0 else [zeros, query]
            both = jnp.concatenate(both, axis=0)
            return [
                jnp.dot(
                    held_refs[t][index[t], 0:128, pair * 128 : (pair + 1) * 128],
                    both,
                    preferred_element_type=jnp.float32,
                )
                for t in range(count)
            ]

        def absorb(head, scores):
            pair = head // 2
            start = 128 + (head % 2) * HEAD
            high = scores[0].reshape(-1, 8, 256).max(axis=0)
            for s in scores[1:]:
                high = jnp.maximum(high, s.reshape(-1, 8, 256).max(axis=0))
            high = jnp.max(high, axis=0, keepdims=True)
            total = None
            if not begins:
                old = high_in[frame, head, 0:1, :]
                high = jnp.maximum(high, old)
                total = total_in[frame, head] * jnp.exp2(old - high)
            for t in range(0, count, 2):
                group = range(t, min(t + 2, count))
                weights = [weigh(scores[g], high) for g in group]
                sides = []
                for g in group:
                    value = held_refs[g][
                        index[g], start : start + HEAD, pair * 128 : (pair + 1) * 128
                    ]
                    sides.append(jnp.concatenate([value, ones], axis=0) * keep[g])
                added = jnp.dot(
                    jnp.concatenate(sides, axis=1),
                    jnp.concatenate(weights, axis=0),
                    preferred_element_type=jnp.float32,
                )
                total = added if total is None else total + added
            if ends:
                return total[0:HEAD] / total[HEAD : HEAD + 1]
            total_out[frame, head] = total
            high_out[frame, head] = jnp.broadcast_to(high, (8, 256))
            return None

        contexts = []
        scores = score(0)
        for head in range(HEADS_HERE):
            later = score(head + 1) if head + 1 < HEADS_HERE else None
            contexts.append(absorb(head, scores))
            scores = later
        if ends:
            context = jnp.concatenate(contexts, axis=0).T.astype(jnp.bfloat16)
            rows = pl.ds(pl.multiple_of(frame * QUARTER, QUARTER), QUARTER)
            for j in range(4):
                outs[j][rows, :] = context[j * QUARTER : (j + 1) * QUARTER]
        return carried

    lax.fori_loop(0, FRAMES_HERE, one_frame, 0)


def attend(kind, valid, query_a, query_b, block_list, state=()):
    ends = kind == "last"
    scratch = []
    if kind in ("wide", "last"):
        scratch = [
            pltpu.VMEM((2 * FRAMES_HERE, 256, 256), jnp.bfloat16),
            pltpu.SemaphoreType.DMA((2,)),
        ]
    if ends:
        out_shape = [jax.ShapeDtypeStruct((FRAMES_HERE * QUARTER, WIDTH), jnp.bfloat16)] * 4
    else:
        out_shape = [
            jax.ShapeDtypeStruct((FRAMES_HERE, HEADS_HERE, 8, 256), jnp.float32),
            jax.ShapeDtypeStruct((FRAMES_HERE, HEADS_HERE, HEAD + 16, 256), jnp.float32),
        ]
    inputs = [valid, query_a, query_b, *block_list, *state]
    return pl.pallas_call(
        functools.partial(attend_kernel, kind),
        in_specs=[SMEM] + [VMEM] * (len(inputs) - 1),
        out_specs=[VMEM] * len(out_shape),
        out_shape=out_shape,
        scratch_shapes=scratch,
        compiler_params=pltpu.CompilerParams(vmem_limit_bytes=36 << 20),
        cost_estimate=BRIEF,
    )(*inputs)


def finish_kernel(c0, c1, c2, c3, w0, w1, w2, w3, token_ref, gain_ref, proj_ref, out_ref, map_ref):
    total = token_ref[...].astype(jnp.float32)
    mixed = jnp.dot(c0[...], w0[...], preferred_element_type=jnp.float32)
    for c, w in ((c1, w1), (c2, w2), (c3, w3)):
        mixed = mixed + jnp.dot(c[...], w[...], preferred_element_type=jnp.float32)
    attended = (total + mixed).astype(jnp.bfloat16)
    out_ref[...] = attended
    lifted = layer_norm(attended.astype(jnp.float32), gain_ref[...]).astype(jnp.bfloat16)
    mapped = jnp.dot(lifted, proj_ref[...], preferred_element_type=jnp.float32)
    map_ref[...] = mapped.astype(jnp.bfloat16)


def finish(contexts, weights, tokens, gain, proj):
    return pl.pallas_call(
        finish_kernel,
        in_specs=[VMEM] * 11,
        out_specs=[VMEM] * 2,
        out_shape=[
            jax.ShapeDtypeStruct((256, 1024), jnp.bfloat16),
            jax.ShapeDtypeStruct((256, 256), jnp.bfloat16),
        ],
        compiler_params=pltpu.CompilerParams(vmem_limit_bytes=32 << 20),
        cost_estimate=BRIEF,
    )(*contexts, *weights, tokens, gain, proj)


def join_kernel(row_ref, beside_ref, own_ref, across_ref, one_ref, two_ref, out_ref):
    def widen(values):
        count = values.shape[0]
        column = lax.broadcasted_iota(jnp.int32, (count, 256), 0) % 32
        left = jnp.where(column == 0, 0.0, pltpu.roll(values, 1, 0))
        right = jnp.where(column == 31, 0.0, pltpu.roll(values, count - 1, 0))
        return jnp.concatenate(
            [left.astype(jnp.bfloat16), values.astype(jnp.bfloat16), right.astype(jnp.bfloat16)],
            axis=1,
        )

    def conv(wide, rows_in, weight_ref):
        rows_out = rows_in - 2
        summed = None
        for a in range(3):
            window = jnp.concatenate(
                [
                    wide[(f * rows_in + a) * 32 : (f * rows_in + a + rows_out) * 32]
                    for f in range(FRAMES_HERE)
                ],
                axis=0,
            )
            added = jnp.dot(window, weight_ref[a], preferred_element_type=jnp.float32)
            summed = added if summed is None else summed + added
        return summed

    own = own_ref[...].astype(jnp.float32)
    place = row_ref[0]
    odd = place % 2 == 1
    beside = beside_ref[...].astype(jnp.float32)
    across = across_ref[...].astype(jnp.float32)
    before = jnp.where(odd, beside, across)
    after = jnp.where(odd, across, beside)
    six = []
    for f in range(FRAMES_HERE):
        span = slice(f * QUARTER, (f + 1) * QUARTER)
        six += [before[span], own[span], after[span]]
    six = jnp.maximum(jnp.concatenate(six, axis=0), 0.0)
    inner = conv(widen(six), 6, one_ref)
    inner = jnp.maximum(inner, 0.0)
    row = (lax.broadcasted_iota(jnp.int32, (512, 256), 0) // 32) % 4
    drop = ((row == 0) & (place == 0)) | ((row == 3) & (place == 3))
    inner = jnp.where(drop, 0.0, inner)
    joined = conv(widen(inner), 4, two_ref)
    out_ref[...] = (own + joined).astype(jnp.bfloat16)


def join(row, beside, own, across, one, two):
    return pl.pallas_call(
        join_kernel,
        in_specs=[SMEM] + [VMEM] * 5,
        out_specs=VMEM,
        out_shape=jax.ShapeDtypeStruct((256, 256), jnp.bfloat16),
        compiler_params=pltpu.CompilerParams(vmem_limit_bytes=32 << 20),
        cost_estimate=BRIEF,
    )(row, beside, own, across, one, two)


def shards(
    tokens,
    norm_gain,
    qkv_weight,
    out_weight,
    key_offsets,
    feat_gain,
    proj_weight,
    conv_one,
    conv_two,
):
    own = tokens.reshape(FRAMES_HERE * QUARTER, 1024)
    core = lambda value: lax.ppermute(value, "row", CORE_PAIRS)
    chip = lambda value: lax.ppermute(value, "row", CHIP_PAIRS)
    tie = lax.optimization_barrier

    positions = np.arange(20)
    distance = positions[None, :] - 8 - np.arange(FRAMES_HERE)[:, None]
    valid = jnp.any(key_offsets[:, :, None] == distance[:, None, :], axis=1).astype(jnp.int32)
    block = lax.axis_index("frame")
    even = 1 - block % 2
    valid = jnp.concatenate([valid, jnp.full((1, 20), even, jnp.int32)], axis=0)
    edge_block = (block % EDGE == 0) | (block % EDGE == EDGE - 1)

    normed = normalise(own, norm_gain.reshape(1, 1024))
    near = core(normed)
    far = chip(normed)
    side = swapped(normed, 0)
    other = swapped(normed, 1, True)
    kv_a, query_a = project([normed, near], qkv_weight, True)
    far, kv_a = tie((far, kv_a))
    far_near = core(far)
    out_late, far = tie((out_weight, far))
    weight_chip = chip(out_late)
    far_near, side, other = tie((far_near, side, other))
    kv_b, query_b = project([far, far_near], qkv_weight, True)
    side_b = swapped(kv_b, 0)
    other_b = swapped(jnp.where(edge_block, kv_a, kv_b), 1)
    side, other, kv_b = tie((side, other, kv_b))
    side_near, other_near = core(side), core(other)
    state = attend("own", valid, query_a, query_b, [kv_a, kv_b])
    side, weight_chip, state = tie((side, weight_chip, state))
    side_a, other_a = project([side, side_near, other, other_near], qkv_weight, False)
    side_2a, other_2a = swapped(other_a, 0), swapped(side_a, 1)
    state = attend("near", valid, query_a, query_b, [side_a, other_a], state)
    side_b, other_b, state = tie((side_b, other_b, state))
    side_2b, other_2b = swapped(other_b, 0), swapped(side_b, 1)
    state = attend("near", valid, query_a, query_b, [side_b, other_b], state)
    state = attend("wide", valid, query_a, query_b, [side_2a, other_2a], state)
    out_last, weight_chip, state = tie((out_weight, weight_chip, state))
    weight_core = core(out_last)
    weight_cross = core(weight_chip)
    parts = attend("last", valid, query_a, query_b, [side_2b, other_2b], state)

    contexts = [
        parts[0],
        core(parts[1]),
        chip(parts[2]),
        lax.ppermute(parts[3], "row", CROSS_PAIRS),
    ]
    weights = [out_weight, weight_core, weight_chip, weight_cross]
    attended, mapped = finish(contexts, weights, own, feat_gain.reshape(1, 1024), proj_weight)

    across = lax.ppermute(mapped, "row", [(1, 2), (2, 1)])
    beside = core(mapped)
    place = lax.axis_index("row").astype(jnp.int32).reshape(1)
    joined = join(
        place,
        beside,
        mapped,
        across,
        conv_one.reshape(3, 768, 256),
        conv_two.reshape(3, 768, 256),
    )
    return attended.reshape(tokens.shape), joined.reshape(tokens.shape[:3] + (256,))


def solution(mesh):
    in_specs = (
        P("frame", "row", None, None),
        P(),
        P(None, None, "row"),
        P("row", None),
        P("frame", None),
        P(),
        P(),
        P(),
        P(),
    )
    out_specs = (P("frame", "row", None, None), P("frame", "row", None, None))
    return jax.shard_map(shards, mesh=mesh, in_specs=in_specs, out_specs=out_specs, check_vma=False)
```

```python
import functools

import jax
import jax.numpy as jnp
import numpy as np
from jax import lax
from jax.experimental import pallas as pl
from jax.experimental.pallas import tpu as pltpu
from jax.sharding import PartitionSpec as P

EPSILON = 1e-06
HEAD = 64
HEADS_HERE = 4
FRAMES_HERE = 4
QUARTER = 64
WIDTH = 256
QUERY_SCALE = 1.4426950408889634 / 8.0
LARGE = 20 << 20
BRIEF = pl.CostEstimate(flops=1, bytes_accessed=1, transcendentals=0)
EDGE = 8
EARLY = 128
VMEM = pl.BlockSpec(memory_space=pltpu.VMEM)
SMEM = pl.BlockSpec(memory_space=pltpu.SMEM)
ANY = pl.BlockSpec(memory_space=pl.ANY)
HBM = pl.BlockSpec(memory_space=pltpu.HBM)

CORE_PAIRS = [(0, 1), (1, 0), (2, 3), (3, 2)]
CHIP_PAIRS = [(0, 2), (2, 0), (1, 3), (3, 1)]
CROSS_PAIRS = [(0, 3), (3, 0), (1, 2), (2, 1)]


def swapped(value, offset, across=False):
    count = lax.axis_size("frame")
    pairs = []
    for low in range(offset, count, 2):
        high = (low + 1) % count
        flip = 2 if across and low // EDGE != high // EDGE else 0
        for row in range(4):
            pairs.append((low * 4 + row, high * 4 + (row ^ flip)))
            pairs.append((high * 4 + (row ^ flip), low * 4 + row))
    return lax.ppermute(value, ("frame", "row"), pairs)


def layer_norm(values, gain_vec):
    average = jnp.mean(values, axis=-1, keepdims=True)
    centered = values - average
    spread = jnp.mean(centered * centered, axis=-1, keepdims=True)
    return centered * lax.rsqrt(spread + EPSILON) * gain_vec


def norm_kernel(token_hbm, gain_hbm, out_ref, token, gain, sems):
    copies = [
        pltpu.make_async_copy(token_hbm, token, sems.at[0]),
        pltpu.make_async_copy(gain_hbm, gain, sems.at[1]),
    ]
    for copy in copies:
        copy.start()
    for copy in copies:
        copy.wait()
    values = layer_norm(token[...].astype(jnp.float32), gain[...])
    out_ref[...] = values.astype(jnp.bfloat16)


def normalise(tokens, gain):
    return pl.pallas_call(
        norm_kernel,
        in_specs=[HBM] * 2,
        out_specs=VMEM,
        out_shape=jax.ShapeDtypeStruct(tokens.shape, jnp.bfloat16),
        scratch_shapes=[
            pltpu.VMEM(tokens.shape, jnp.bfloat16),
            pltpu.VMEM(gain.shape, jnp.float32),
            pltpu.SemaphoreType.DMA((2,)),
        ],
        compiler_params=pltpu.CompilerParams(vmem_limit_bytes=60 << 20),
        cost_estimate=BRIEF,
    )(tokens, gain)


def project_kernel(blocks, queries, *refs):
    parts, refs = refs[: 2 * blocks], refs[2 * blocks :]
    weight_hbm, refs = refs[0], refs[1:]
    kv_refs, refs = refs[:blocks], refs[blocks:]
    if queries:
        query_ref, refs = refs[0], refs[1:]
    weight, sem = refs
    skip = 0 if queries else 1
    copies = [
        pltpu.make_async_copy(weight_hbm.at[which], weight.at[which - skip], sem.at[which - skip])
        for which in range(skip, 3)
    ]
    for which in ([1, 2, 0] if queries else [0, 1]):
        copies[which].start()
    for copy in copies:
        copy.wait()
    for block in range(blocks):
        rows = []
        for frame in range(FRAMES_HERE):
            for part in parts[2 * block : 2 * block + 2]:
                rows.append(part[frame * QUARTER : (frame + 1) * QUARTER])
        rows = jnp.concatenate(rows, axis=0)
        key = jnp.dot(rows, weight[1 - skip], preferred_element_type=jnp.float32)
        key = key.astype(jnp.bfloat16)
        value = jnp.dot(rows, weight[2 - skip], preferred_element_type=jnp.float32)
        value = value.T.astype(jnp.bfloat16)
        kv_ref = kv_refs[block]
        for frame in range(FRAMES_HERE):
            span = slice(frame * 128, (frame + 1) * 128)
            kv_ref[frame, 0:128, :] = key[span]
            kv_ref[frame, 128:256, 0:128] = value[0:128, span]
            kv_ref[frame, 128:256, 128:256] = value[128:256, span]
        if queries:
            query = jnp.dot(rows, weight[0], preferred_element_type=jnp.float32)
            query = (query * QUERY_SCALE).T.astype(jnp.bfloat16)
            for frame in range(FRAMES_HERE):
                query_ref[frame] = query[:, frame * 128 : (frame + 1) * 128]


def project(parts, weight, queries):
    blocks = len(parts) // 2
    out_shape = [jax.ShapeDtypeStruct((FRAMES_HERE, 256, 256), jnp.bfloat16)] * blocks
    if queries:
        out_shape.append(jax.ShapeDtypeStruct((FRAMES_HERE, WIDTH, 128), jnp.bfloat16))
    used = 3 if queries else 2
    return pl.pallas_call(
        functools.partial(project_kernel, blocks, queries),
        in_specs=[VMEM] * (2 * blocks) + [HBM],
        out_specs=[VMEM] * len(out_shape),
        out_shape=out_shape,
        scratch_shapes=[pltpu.VMEM((used, 1024, WIDTH), jnp.bfloat16), pltpu.SemaphoreType.DMA((used,))],
        compiler_params=pltpu.CompilerParams(vmem_limit_bytes=LARGE),
        cost_estimate=BRIEF,
    )(*parts, weight)


def weigh(scores, high):
    return jnp.exp2(scores - high).astype(jnp.bfloat16)


def near_tiles(refs, even):
    tiles = []
    for which, ref in enumerate(refs):
        ahead = even if which == 0 else 1 - even
        for t in range(FRAMES_HERE):
            tiles.append((ref, t, (t + 1) % FRAMES_HERE, 4 + 8 * ahead + t))
    return tiles


def own_tiles(refs):
    return [(ref, t, (t + 1) % FRAMES_HERE, 8 + t) for t in range(FRAMES_HERE) for ref in refs]


def wide_tiles(ref, frame):
    tiles = []
    for t in range(FRAMES_HERE + 1):
        slot = frame + t
        position = jnp.where(slot < FRAMES_HERE, slot, slot + 12)
        tiles.append((ref, slot, frame + (t + 1) % (FRAMES_HERE + 1), position))
    return tiles


def attend_kernel(kind, *refs):
    begins, ends = kind == "own", kind == "last"
    valid_ref, query_a, query_b = refs[:3]
    refs = refs[3:]
    wide = kind in ("wide", "last")
    block_refs, refs = refs[:2], refs[2:]
    if not begins:
        high_in, total_in, refs = refs[0], refs[1], refs[2:]
    even = valid_ref[FRAMES_HERE, 0]
    if ends:
        outs, refs = refs[:4], refs[4:]
    else:
        high_out, total_out, refs = refs[0], refs[1], refs[2:]
    if wide:
        held, sems = refs
        first = even * FRAMES_HERE
        copies = [
            pltpu.make_async_copy(block_refs[0], held.at[pl.ds(first, FRAMES_HERE)], sems.at[0]),
            pltpu.make_async_copy(
                block_refs[1], held.at[pl.ds(FRAMES_HERE - first, FRAMES_HERE)], sems.at[1]
            ),
        ]
        for copy in copies:
            copy.start()
        for copy in copies:
            copy.wait()
    ones = jnp.ones((16, 128), jnp.bfloat16)
    zeros = jnp.zeros((HEAD, 256), jnp.bfloat16)

    def one_frame(frame, carried):
        if kind == "own":
            tiles = own_tiles(block_refs)
        elif kind == "near":
            tiles = near_tiles(block_refs, even)
        else:
            tiles = wide_tiles(held, frame)
        held_refs, index, keep = [], [], []
        for ref, slot, other, position in tiles:
            there = valid_ref[frame, position]
            held_refs.append(ref)
            index.append(jnp.where(there != 0, slot, other))
            keep.append(there.astype(jnp.float32).astype(jnp.bfloat16))
        count = len(tiles)

        def score(head):
            pair = head // 2
            query = jnp.concatenate(
                [
                    query_a[frame, head * HEAD : (head + 1) * HEAD, :],
                    query_b[frame, head * HEAD : (head + 1) * HEAD, :],
                ],
                axis=1,
            )
            both = [query, zeros] if head % 2 == 0 else [zeros, query]
            both = jnp.concatenate(both, axis=0)
            return [
                jnp.dot(
                    held_refs[t][index[t], 0:128, pair * 128 : (pair + 1) * 128],
                    both,
                    preferred_element_type=jnp.float32,
                )
                for t in range(count)
            ]

        def absorb(head, scores):
            pair = head // 2
            start = 128 + (head % 2) * HEAD
            high = scores[0].reshape(-1, 8, 256).max(axis=0)
            for s in scores[1:]:
                high = jnp.maximum(high, s.reshape(-1, 8, 256).max(axis=0))
            high = jnp.max(high, axis=0, keepdims=True)
            total = None
            if not begins:
                old = high_in[frame, head, 0:1, :]
                high = jnp.maximum(high, old)
                total = total_in[frame, head] * jnp.exp2(old - high)
            for t in range(0, count, 2):
                group = range(t, min(t + 2, count))
                weights = [weigh(scores[g], high) for g in group]
                sides = []
                for g in group:
                    value = held_refs[g][
                        index[g], start : start + HEAD, pair * 128 : (pair + 1) * 128
                    ]
                    sides.append(jnp.concatenate([value, ones], axis=0) * keep[g])
                added = jnp.dot(
                    jnp.concatenate(sides, axis=1),
                    jnp.concatenate(weights, axis=0),
                    preferred_element_type=jnp.float32,
                )
                total = added if total is None else total + added
            if ends:
                return total[0:HEAD] / total[HEAD : HEAD + 1]
            total_out[frame, head] = total
            high_out[frame, head] = jnp.broadcast_to(high, (8, 256))
            return None

        contexts = []
        scores = score(0)
        for head in range(HEADS_HERE):
            later = score(head + 1) if head + 1 < HEADS_HERE else None
            contexts.append(absorb(head, scores))
            scores = later
        if ends:
            context = jnp.concatenate(contexts, axis=0).T.astype(jnp.bfloat16)
            rows = pl.ds(pl.multiple_of(frame * QUARTER, QUARTER), QUARTER)
            for j in range(4):
                outs[j][rows, :] = context[j * QUARTER : (j + 1) * QUARTER]
        return carried

    lax.fori_loop(0, FRAMES_HERE, one_frame, 0)


def attend(kind, valid, query_a, query_b, block_list, state=()):
    ends = kind == "last"
    scratch = []
    if kind in ("wide", "last"):
        scratch = [
            pltpu.VMEM((2 * FRAMES_HERE, 256, 256), jnp.bfloat16),
            pltpu.SemaphoreType.DMA((2,)),
        ]
    if ends:
        out_shape = [jax.ShapeDtypeStruct((FRAMES_HERE * QUARTER, WIDTH), jnp.bfloat16)] * 4
    else:
        out_shape = [
            jax.ShapeDtypeStruct((FRAMES_HERE, HEADS_HERE, 8, 256), jnp.float32),
            jax.ShapeDtypeStruct((FRAMES_HERE, HEADS_HERE, HEAD + 16, 256), jnp.float32),
        ]
    inputs = [valid, query_a, query_b, *block_list, *state]
    return pl.pallas_call(
        functools.partial(attend_kernel, kind),
        in_specs=[SMEM] + [VMEM] * (len(inputs) - 1),
        out_specs=[VMEM] * len(out_shape),
        out_shape=out_shape,
        scratch_shapes=scratch,
        compiler_params=pltpu.CompilerParams(vmem_limit_bytes=36 << 20),
        cost_estimate=BRIEF,
    )(*inputs)


def finish_kernel(*refs):
    contexts, weights, (token_ref, gain_ref, proj_ref, out_ref, map_ref) = (
        refs[:4],
        refs[4:10],
        refs[10:],
    )
    own, beside, *parts = [ref[...] for ref in weights]
    weights = [own, beside]
    for half in (parts[:2], parts[2:]):
        weights.append(jnp.concatenate(half, axis=0))
    total = token_ref[...].astype(jnp.float32)
    mixed = jnp.dot(contexts[0][...], weights[0], preferred_element_type=jnp.float32)
    for c, w in zip(contexts[1:], weights[1:]):
        mixed = mixed + jnp.dot(c[...], w, preferred_element_type=jnp.float32)
    attended = (total + mixed).astype(jnp.bfloat16)
    out_ref[...] = attended
    lifted = layer_norm(attended.astype(jnp.float32), gain_ref[...]).astype(jnp.bfloat16)
    mapped = jnp.dot(lifted, proj_ref[...], preferred_element_type=jnp.float32)
    map_ref[...] = mapped.astype(jnp.bfloat16)


def finish(contexts, weights, tokens, gain, proj):
    return pl.pallas_call(
        finish_kernel,
        in_specs=[VMEM] * 13,
        out_specs=[VMEM] * 2,
        out_shape=[
            jax.ShapeDtypeStruct((256, 1024), jnp.bfloat16),
            jax.ShapeDtypeStruct((256, 256), jnp.bfloat16),
        ],
        compiler_params=pltpu.CompilerParams(vmem_limit_bytes=32 << 20),
        cost_estimate=BRIEF,
    )(*contexts, *weights, tokens, gain, proj)


def join_kernel(row_ref, beside_ref, own_ref, across_ref, one_ref, two_ref, out_ref):
    def widen(values):
        count = values.shape[0]
        column = lax.broadcasted_iota(jnp.int32, (count, 256), 0) % 32
        left = jnp.where(column == 0, 0.0, pltpu.roll(values, 1, 0))
        right = jnp.where(column == 31, 0.0, pltpu.roll(values, count - 1, 0))
        return jnp.concatenate(
            [left.astype(jnp.bfloat16), values.astype(jnp.bfloat16), right.astype(jnp.bfloat16)],
            axis=1,
        )

    def conv(wide, rows_in, weight_ref):
        rows_out = rows_in - 2
        summed = None
        for a in range(3):
            window = jnp.concatenate(
                [
                    wide[(f * rows_in + a) * 32 : (f * rows_in + a + rows_out) * 32]
                    for f in range(FRAMES_HERE)
                ],
                axis=0,
            )
            added = jnp.dot(window, weight_ref[a], preferred_element_type=jnp.float32)
            summed = added if summed is None else summed + added
        return summed

    own = own_ref[...].astype(jnp.float32)
    place = row_ref[0]
    odd = place % 2 == 1
    beside = beside_ref[...].astype(jnp.float32)
    across = across_ref[...].astype(jnp.float32)
    before = jnp.where(odd, beside, across)
    after = jnp.where(odd, across, beside)
    six = []
    for f in range(FRAMES_HERE):
        span = slice(f * QUARTER, (f + 1) * QUARTER)
        six += [before[span], own[span], after[span]]
    six = jnp.maximum(jnp.concatenate(six, axis=0), 0.0)
    inner = conv(widen(six), 6, one_ref)
    inner = jnp.maximum(inner, 0.0)
    row = (lax.broadcasted_iota(jnp.int32, (512, 256), 0) // 32) % 4
    drop = ((row == 0) & (place == 0)) | ((row == 3) & (place == 3))
    inner = jnp.where(drop, 0.0, inner)
    joined = conv(widen(inner), 4, two_ref)
    out_ref[...] = (own + joined).astype(jnp.bfloat16)


def join(row, beside, own, across, one, two):
    return pl.pallas_call(
        join_kernel,
        in_specs=[SMEM] + [VMEM] * 5,
        out_specs=VMEM,
        out_shape=jax.ShapeDtypeStruct((256, 256), jnp.bfloat16),
        compiler_params=pltpu.CompilerParams(vmem_limit_bytes=32 << 20),
        cost_estimate=BRIEF,
    )(row, beside, own, across, one, two)


def shards(
    tokens,
    norm_gain,
    qkv_weight,
    out_weight,
    key_offsets,
    feat_gain,
    proj_weight,
    conv_one,
    conv_two,
):
    own = tokens.reshape(FRAMES_HERE * QUARTER, 1024)
    core = lambda value: lax.ppermute(value, "row", CORE_PAIRS)
    chip = lambda value: lax.ppermute(value, "row", CHIP_PAIRS)
    tie = lax.optimization_barrier

    positions = np.arange(20)
    distance = positions[None, :] - 8 - np.arange(FRAMES_HERE)[:, None]
    valid = jnp.any(key_offsets[:, :, None] == distance[:, None, :], axis=1).astype(jnp.int32)
    block = lax.axis_index("frame")
    even = 1 - block % 2
    valid = jnp.concatenate([valid, jnp.full((1, 20), even, jnp.int32)], axis=0)
    edge_block = (block % EDGE == 0) | (block % EDGE == EDGE - 1)

    normed = normalise(own, norm_gain.reshape(1, 1024))
    near = core(normed)
    far = chip(normed)
    side = swapped(normed, 0)
    other = swapped(normed, 1, True)
    kv_a, query_a = project([normed, near], qkv_weight, True)
    far, kv_a = tie((far, kv_a))
    far_near = core(far)
    out_early, far = tie((out_weight[:EARLY], far))
    chip_early = chip(out_early)
    far_near, side, other = tie((far_near, side, other))
    kv_b, query_b = project([far, far_near], qkv_weight, True)
    kv_b, chip_early = tie((kv_b, chip_early))
    side_b = swapped(kv_b, 0)
    other_b = swapped(jnp.where(edge_block, kv_a, kv_b), 1)
    side, other, kv_b = tie((side, other, kv_b))
    side_near, other_near = core(side), core(other)
    state = attend("own", valid, query_a, query_b, [kv_a, kv_b])
    out_late, side, state = tie((out_weight[EARLY:], side, state))
    chip_late = chip(out_late)
    side_a, other_a = project([side, side_near, other, other_near], qkv_weight, False)
    side_2a, other_2a = swapped(other_a, 0), swapped(side_a, 1)
    state = attend("near", valid, query_a, query_b, [side_a, other_a], state)
    side_b, other_b, chip_late, state = tie((side_b, other_b, chip_late, state))
    side_2b, other_2b = swapped(other_b, 0), swapped(side_b, 1)
    state = attend("near", valid, query_a, query_b, [side_b, other_b], state)
    state = attend("wide", valid, query_a, query_b, [side_2a, other_2a], state)
    out_last, chip_early, state = tie((out_weight, chip_early, state))
    weight_core = core(out_last)
    cross_early, cross_late = core(chip_early), core(chip_late)
    parts = attend("last", valid, query_a, query_b, [side_2b, other_2b], state)

    contexts = [
        parts[0],
        core(parts[1]),
        chip(parts[2]),
        lax.ppermute(parts[3], "row", CROSS_PAIRS),
    ]
    weights = [out_weight, weight_core, chip_early, chip_late, cross_early, cross_late]
    attended, mapped = finish(contexts, weights, own, feat_gain.reshape(1, 1024), proj_weight)

    across = lax.ppermute(mapped, "row", [(1, 2), (2, 1)])
    beside = core(mapped)
    place = lax.axis_index("row").astype(jnp.int32).reshape(1)
    joined = join(
        place,
        beside,
        mapped,
        across,
        conv_one.reshape(3, 768, 256),
        conv_two.reshape(3, 768, 256),
    )
    return attended.reshape(tokens.shape), joined.reshape(tokens.shape[:3] + (256,))


def solution(mesh):
    in_specs = (
        P("frame", "row", None, None),
        P(),
        P(None, None, "row"),
        P("row", None),
        P("frame", None),
        P(),
        P(),
        P(),
        P(),
    )
    out_specs = (P("frame", "row", None, None), P("frame", "row", None, None))
    return jax.shard_map(shards, mesh=mesh, in_specs=in_specs, out_specs=out_specs, check_vma=False)
```

```python
import functools

import jax
import jax.numpy as jnp
import numpy as np
from jax import lax
from jax.experimental import pallas as pl
from jax.experimental.pallas import tpu as pltpu
from jax.sharding import PartitionSpec as P

EPSILON = 1e-06
HEAD = 64
HEADS_HERE = 4
FRAMES_HERE = 4
QUARTER = 64
WIDTH = 256
QUERY_SCALE = 1.4426950408889634 / 8.0
LARGE = 20 << 20
BRIEF = pl.CostEstimate(flops=1, bytes_accessed=1, transcendentals=0)
EDGE = 8
EARLY = 80
VMEM = pl.BlockSpec(memory_space=pltpu.VMEM)
SMEM = pl.BlockSpec(memory_space=pltpu.SMEM)
ANY = pl.BlockSpec(memory_space=pl.ANY)
HBM = pl.BlockSpec(memory_space=pltpu.HBM)

CORE_PAIRS = [(0, 1), (1, 0), (2, 3), (3, 2)]
CHIP_PAIRS = [(0, 2), (2, 0), (1, 3), (3, 1)]
CROSS_PAIRS = [(0, 3), (3, 0), (1, 2), (2, 1)]


def swapped(value, offset, across=False):
    count = lax.axis_size("frame")
    pairs = []
    for low in range(offset, count, 2):
        high = (low + 1) % count
        flip = 2 if across and low // EDGE != high // EDGE else 0
        for row in range(4):
            pairs.append((low * 4 + row, high * 4 + (row ^ flip)))
            pairs.append((high * 4 + (row ^ flip), low * 4 + row))
    return lax.ppermute(value, ("frame", "row"), pairs)


def layer_norm(values, gain_vec):
    average = jnp.mean(values, axis=-1, keepdims=True)
    centered = values - average
    spread = jnp.mean(centered * centered, axis=-1, keepdims=True)
    return centered * lax.rsqrt(spread + EPSILON) * gain_vec


def norm_kernel(token_hbm, gain_hbm, out_ref, token, gain, sems):
    copies = [
        pltpu.make_async_copy(token_hbm, token, sems.at[0]),
        pltpu.make_async_copy(gain_hbm, gain, sems.at[1]),
    ]
    for copy in copies:
        copy.start()
    for copy in copies:
        copy.wait()
    values = layer_norm(token[...].astype(jnp.float32), gain[...])
    out_ref[...] = values.astype(jnp.bfloat16)


def normalise(tokens, gain):
    return pl.pallas_call(
        norm_kernel,
        in_specs=[HBM] * 2,
        out_specs=VMEM,
        out_shape=jax.ShapeDtypeStruct(tokens.shape, jnp.bfloat16),
        scratch_shapes=[
            pltpu.VMEM(tokens.shape, jnp.bfloat16),
            pltpu.VMEM(gain.shape, jnp.float32),
            pltpu.SemaphoreType.DMA((2,)),
        ],
        compiler_params=pltpu.CompilerParams(vmem_limit_bytes=60 << 20),
        cost_estimate=BRIEF,
    )(tokens, gain)


def project_kernel(blocks, queries, *refs):
    parts, refs = refs[: 2 * blocks], refs[2 * blocks :]
    weight_hbm, refs = refs[0], refs[1:]
    kv_refs, refs = refs[:blocks], refs[blocks:]
    if queries:
        query_ref, refs = refs[0], refs[1:]
    weight, sem = refs
    skip = 0 if queries else 1
    copies = [
        pltpu.make_async_copy(weight_hbm.at[which], weight.at[which - skip], sem.at[which - skip])
        for which in range(skip, 3)
    ]
    for which in ([1, 2, 0] if queries else [0, 1]):
        copies[which].start()
    for copy in copies:
        copy.wait()
    for block in range(blocks):
        rows = []
        for frame in range(FRAMES_HERE):
            for part in parts[2 * block : 2 * block + 2]:
                rows.append(part[frame * QUARTER : (frame + 1) * QUARTER])
        rows = jnp.concatenate(rows, axis=0)
        key = jnp.dot(rows, weight[1 - skip], preferred_element_type=jnp.float32)
        key = key.astype(jnp.bfloat16)
        value = jnp.dot(rows, weight[2 - skip], preferred_element_type=jnp.float32)
        value = value.T.astype(jnp.bfloat16)
        kv_ref = kv_refs[block]
        for frame in range(FRAMES_HERE):
            span = slice(frame * 128, (frame + 1) * 128)
            kv_ref[frame, 0:128, :] = key[span]
            kv_ref[frame, 128:256, 0:128] = value[0:128, span]
            kv_ref[frame, 128:256, 128:256] = value[128:256, span]
        if queries:
            query = jnp.dot(rows, weight[0], preferred_element_type=jnp.float32)
            query = (query * QUERY_SCALE).T.astype(jnp.bfloat16)
            for frame in range(FRAMES_HERE):
                query_ref[frame] = query[:, frame * 128 : (frame + 1) * 128]


def project(parts, weight, queries):
    blocks = len(parts) // 2
    out_shape = [jax.ShapeDtypeStruct((FRAMES_HERE, 256, 256), jnp.bfloat16)] * blocks
    if queries:
        out_shape.append(jax.ShapeDtypeStruct((FRAMES_HERE, WIDTH, 128), jnp.bfloat16))
    used = 3 if queries else 2
    return pl.pallas_call(
        functools.partial(project_kernel, blocks, queries),
        in_specs=[VMEM] * (2 * blocks) + [HBM],
        out_specs=[VMEM] * len(out_shape),
        out_shape=out_shape,
        scratch_shapes=[pltpu.VMEM((used, 1024, WIDTH), jnp.bfloat16), pltpu.SemaphoreType.DMA((used,))],
        compiler_params=pltpu.CompilerParams(vmem_limit_bytes=LARGE),
        cost_estimate=BRIEF,
    )(*parts, weight)


def weigh(scores, high):
    return jnp.exp2(scores - high).astype(jnp.bfloat16)


def near_tiles(refs, even):
    tiles = []
    for which, ref in enumerate(refs):
        ahead = even if which == 0 else 1 - even
        for t in range(FRAMES_HERE):
            tiles.append((ref, t, (t + 1) % FRAMES_HERE, 4 + 8 * ahead + t))
    return tiles


def own_tiles(refs):
    return [(ref, t, (t + 1) % FRAMES_HERE, 8 + t) for t in range(FRAMES_HERE) for ref in refs]


def wide_tiles(ref, frame):
    tiles = []
    for t in range(FRAMES_HERE + 1):
        slot = frame + t
        position = jnp.where(slot < FRAMES_HERE, slot, slot + 12)
        tiles.append((ref, slot, frame + (t + 1) % (FRAMES_HERE + 1), position))
    return tiles


def attend_kernel(kind, *refs):
    begins, ends = kind == "own", kind == "last"
    valid_ref, query_a, query_b = refs[:3]
    refs = refs[3:]
    wide = kind in ("wide", "last")
    block_refs, refs = refs[:2], refs[2:]
    if not begins:
        high_in, total_in, refs = refs[0], refs[1], refs[2:]
    even = valid_ref[FRAMES_HERE, 0]
    if ends:
        outs, refs = refs[:4], refs[4:]
    else:
        high_out, total_out, refs = refs[0], refs[1], refs[2:]
    if wide:
        held, sems = refs
        first = even * FRAMES_HERE
        copies = [
            pltpu.make_async_copy(block_refs[0], held.at[pl.ds(first, FRAMES_HERE)], sems.at[0]),
            pltpu.make_async_copy(
                block_refs[1], held.at[pl.ds(FRAMES_HERE - first, FRAMES_HERE)], sems.at[1]
            ),
        ]
        for copy in copies:
            copy.start()
        for copy in copies:
            copy.wait()
    ones = jnp.ones((16, 128), jnp.bfloat16)
    zeros = jnp.zeros((HEAD, 256), jnp.bfloat16)

    def one_frame(frame, carried):
        if kind == "own":
            tiles = own_tiles(block_refs)
        elif kind == "near":
            tiles = near_tiles(block_refs, even)
        else:
            tiles = wide_tiles(held, frame)
        held_refs, index, keep = [], [], []
        for ref, slot, other, position in tiles:
            there = valid_ref[frame, position]
            held_refs.append(ref)
            index.append(jnp.where(there != 0, slot, other))
            keep.append(there.astype(jnp.float32).astype(jnp.bfloat16))
        count = len(tiles)

        def score(head):
            pair = head // 2
            query = jnp.concatenate(
                [
                    query_a[frame, head * HEAD : (head + 1) * HEAD, :],
                    query_b[frame, head * HEAD : (head + 1) * HEAD, :],
                ],
                axis=1,
            )
            both = [query, zeros] if head % 2 == 0 else [zeros, query]
            both = jnp.concatenate(both, axis=0)
            return [
                jnp.dot(
                    held_refs[t][index[t], 0:128, pair * 128 : (pair + 1) * 128],
                    both,
                    preferred_element_type=jnp.float32,
                )
                for t in range(count)
            ]

        def absorb(head, scores):
            pair = head // 2
            start = 128 + (head % 2) * HEAD
            high = scores[0].reshape(-1, 8, 256).max(axis=0)
            for s in scores[1:]:
                high = jnp.maximum(high, s.reshape(-1, 8, 256).max(axis=0))
            high = jnp.max(high, axis=0, keepdims=True)
            total = None
            if not begins:
                old = high_in[frame, head, 0:1, :]
                high = jnp.maximum(high, old)
                total = total_in[frame, head] * jnp.exp2(old - high)
            for t in range(0, count, 2):
                group = range(t, min(t + 2, count))
                weights = [weigh(scores[g], high) for g in group]
                sides = []
                for g in group:
                    value = held_refs[g][
                        index[g], start : start + HEAD, pair * 128 : (pair + 1) * 128
                    ]
                    sides.append(jnp.concatenate([value, ones], axis=0) * keep[g])
                added = jnp.dot(
                    jnp.concatenate(sides, axis=1),
                    jnp.concatenate(weights, axis=0),
                    preferred_element_type=jnp.float32,
                )
                total = added if total is None else total + added
            if ends:
                return total[0:HEAD] / total[HEAD : HEAD + 1]
            total_out[frame, head] = total
            high_out[frame, head] = jnp.broadcast_to(high, (8, 256))
            return None

        contexts = []
        scores = score(0)
        for head in range(HEADS_HERE):
            later = score(head + 1) if head + 1 < HEADS_HERE else None
            contexts.append(absorb(head, scores))
            scores = later
        if ends:
            context = jnp.concatenate(contexts, axis=0).T.astype(jnp.bfloat16)
            rows = pl.ds(pl.multiple_of(frame * QUARTER, QUARTER), QUARTER)
            for j in range(4):
                outs[j][rows, :] = context[j * QUARTER : (j + 1) * QUARTER]
        return carried

    lax.fori_loop(0, FRAMES_HERE, one_frame, 0)


def attend(kind, valid, query_a, query_b, block_list, state=()):
    ends = kind == "last"
    scratch = []
    if kind in ("wide", "last"):
        scratch = [
            pltpu.VMEM((2 * FRAMES_HERE, 256, 256), jnp.bfloat16),
            pltpu.SemaphoreType.DMA((2,)),
        ]
    if ends:
        out_shape = [jax.ShapeDtypeStruct((FRAMES_HERE * QUARTER, WIDTH), jnp.bfloat16)] * 4
    else:
        out_shape = [
            jax.ShapeDtypeStruct((FRAMES_HERE, HEADS_HERE, 8, 256), jnp.float32),
            jax.ShapeDtypeStruct((FRAMES_HERE, HEADS_HERE, HEAD + 16, 256), jnp.float32),
        ]
    inputs = [valid, query_a, query_b, *block_list, *state]
    return pl.pallas_call(
        functools.partial(attend_kernel, kind),
        in_specs=[SMEM] + [VMEM] * (len(inputs) - 1),
        out_specs=[VMEM] * len(out_shape),
        out_shape=out_shape,
        scratch_shapes=scratch,
        compiler_params=pltpu.CompilerParams(vmem_limit_bytes=36 << 20),
        cost_estimate=BRIEF,
    )(*inputs)


def finish_kernel(*refs):
    contexts, weights, (token_ref, gain_ref, proj_ref, out_ref, map_ref) = (
        refs[:4],
        refs[4:10],
        refs[10:],
    )
    own, beside, *parts = [ref[...] for ref in weights]
    weights = [own, beside]
    for half in (parts[:2], parts[2:]):
        weights.append(jnp.concatenate(half, axis=0))
    total = token_ref[...].astype(jnp.float32)
    mixed = jnp.dot(contexts[0][...], weights[0], preferred_element_type=jnp.float32)
    for c, w in zip(contexts[1:], weights[1:]):
        mixed = mixed + jnp.dot(c[...], w, preferred_element_type=jnp.float32)
    attended = (total + mixed).astype(jnp.bfloat16)
    out_ref[...] = attended
    lifted = layer_norm(attended.astype(jnp.float32), gain_ref[...]).astype(jnp.bfloat16)
    mapped = jnp.dot(lifted, proj_ref[...], preferred_element_type=jnp.float32)
    map_ref[...] = mapped.astype(jnp.bfloat16)


def finish(contexts, weights, tokens, gain, proj):
    return pl.pallas_call(
        finish_kernel,
        in_specs=[VMEM] * 13,
        out_specs=[VMEM] * 2,
        out_shape=[
            jax.ShapeDtypeStruct((256, 1024), jnp.bfloat16),
            jax.ShapeDtypeStruct((256, 256), jnp.bfloat16),
        ],
        compiler_params=pltpu.CompilerParams(vmem_limit_bytes=32 << 20),
        cost_estimate=BRIEF,
    )(*contexts, *weights, tokens, gain, proj)


def join_kernel(row_ref, beside_ref, own_ref, across_ref, one_ref, two_ref, out_ref):
    def widen(values):
        count = values.shape[0]
        column = lax.broadcasted_iota(jnp.int32, (count, 256), 0) % 32
        left = jnp.where(column == 0, 0.0, pltpu.roll(values, 1, 0))
        right = jnp.where(column == 31, 0.0, pltpu.roll(values, count - 1, 0))
        return jnp.concatenate(
            [left.astype(jnp.bfloat16), values.astype(jnp.bfloat16), right.astype(jnp.bfloat16)],
            axis=1,
        )

    def conv(wide, rows_in, weight_ref):
        rows_out = rows_in - 2
        summed = None
        for a in range(3):
            window = jnp.concatenate(
                [
                    wide[(f * rows_in + a) * 32 : (f * rows_in + a + rows_out) * 32]
                    for f in range(FRAMES_HERE)
                ],
                axis=0,
            )
            added = jnp.dot(window, weight_ref[a], preferred_element_type=jnp.float32)
            summed = added if summed is None else summed + added
        return summed

    own = own_ref[...].astype(jnp.float32)
    place = row_ref[0]
    odd = place % 2 == 1
    beside = beside_ref[...].astype(jnp.float32)
    across = across_ref[...].astype(jnp.float32)
    before = jnp.where(odd, beside, across)
    after = jnp.where(odd, across, beside)
    six = []
    for f in range(FRAMES_HERE):
        span = slice(f * QUARTER, (f + 1) * QUARTER)
        six += [before[span], own[span], after[span]]
    six = jnp.maximum(jnp.concatenate(six, axis=0), 0.0)
    inner = conv(widen(six), 6, one_ref)
    inner = jnp.maximum(inner, 0.0)
    row = (lax.broadcasted_iota(jnp.int32, (512, 256), 0) // 32) % 4
    drop = ((row == 0) & (place == 0)) | ((row == 3) & (place == 3))
    inner = jnp.where(drop, 0.0, inner)
    joined = conv(widen(inner), 4, two_ref)
    out_ref[...] = (own + joined).astype(jnp.bfloat16)


def join(row, beside, own, across, one, two):
    return pl.pallas_call(
        join_kernel,
        in_specs=[SMEM] + [VMEM] * 5,
        out_specs=VMEM,
        out_shape=jax.ShapeDtypeStruct((256, 256), jnp.bfloat16),
        compiler_params=pltpu.CompilerParams(vmem_limit_bytes=32 << 20),
        cost_estimate=BRIEF,
    )(row, beside, own, across, one, two)


def shards(
    tokens,
    norm_gain,
    qkv_weight,
    out_weight,
    key_offsets,
    feat_gain,
    proj_weight,
    conv_one,
    conv_two,
):
    own = tokens.reshape(FRAMES_HERE * QUARTER, 1024)
    core = lambda value: lax.ppermute(value, "row", CORE_PAIRS)
    chip = lambda value: lax.ppermute(value, "row", CHIP_PAIRS)
    tie = lax.optimization_barrier

    positions = np.arange(20)
    distance = positions[None, :] - 8 - np.arange(FRAMES_HERE)[:, None]
    valid = jnp.any(key_offsets[:, :, None] == distance[:, None, :], axis=1).astype(jnp.int32)
    block = lax.axis_index("frame")
    even = 1 - block % 2
    valid = jnp.concatenate([valid, jnp.full((1, 20), even, jnp.int32)], axis=0)
    edge_block = (block % EDGE == 0) | (block % EDGE == EDGE - 1)

    normed = normalise(own, norm_gain.reshape(1, 1024))
    near = core(normed)
    far = chip(normed)
    side = swapped(normed, 0)
    other = swapped(normed, 1, True)
    kv_a, query_a = project([normed, near], qkv_weight, True)
    far, kv_a = tie((far, kv_a))
    far_near = core(far)
    out_early, far = tie((out_weight[:EARLY], far))
    chip_early = chip(out_early)
    far_near, side, other = tie((far_near, side, other))
    kv_b, query_b = project([far, far_near], qkv_weight, True)
    kv_b, chip_early = tie((kv_b, chip_early))
    side_b = swapped(kv_b, 0)
    other_b = swapped(jnp.where(edge_block, kv_a, kv_b), 1)
    side, other, kv_b = tie((side, other, kv_b))
    side_near, other_near = core(side), core(other)
    state = attend("own", valid, query_a, query_b, [kv_a, kv_b])
    out_late, side, state = tie((out_weight[EARLY:], side, state))
    chip_late = chip(out_late)
    side_a, other_a = project([side, side_near, other, other_near], qkv_weight, False)
    side_2a, other_2a = swapped(other_a, 0), swapped(side_a, 1)
    state = attend("near", valid, query_a, query_b, [side_a, other_a], state)
    side_b, other_b, state = tie((side_b, other_b, state))
    side_2b, other_2b = swapped(other_b, 0), swapped(side_b, 1)
    state = attend("near", valid, query_a, query_b, [side_b, other_b], state)
    side_2a, chip_late, state = tie((side_2a, chip_late, state))
    state = attend("wide", valid, query_a, query_b, [side_2a, other_2a], state)
    out_last, chip_early, state = tie((out_weight, chip_early, state))
    weight_core = core(out_last)
    cross_early, cross_late = core(chip_early), core(chip_late)
    parts = attend("last", valid, query_a, query_b, [side_2b, other_2b], state)

    contexts = [
        parts[0],
        core(parts[1]),
        chip(parts[2]),
        lax.ppermute(parts[3], "row", CROSS_PAIRS),
    ]
    weights = [out_weight, weight_core, chip_early, chip_late, cross_early, cross_late]
    attended, mapped = finish(contexts, weights, own, feat_gain.reshape(1, 1024), proj_weight)

    across = lax.ppermute(mapped, "row", [(1, 2), (2, 1)])
    beside = core(mapped)
    place = lax.axis_index("row").astype(jnp.int32).reshape(1)
    joined = join(
        place,
        beside,
        mapped,
        across,
        conv_one.reshape(3, 768, 256),
        conv_two.reshape(3, 768, 256),
    )
    return attended.reshape(tokens.shape), joined.reshape(tokens.shape[:3] + (256,))


def solution(mesh):
    in_specs = (
        P("frame", "row", None, None),
        P(),
        P(None, None, "row"),
        P("row", None),
        P("frame", None),
        P(),
        P(),
        P(),
        P(),
    )
    out_specs = (P("frame", "row", None, None), P("frame", "row", None, None))
    return jax.shard_map(shards, mesh=mesh, in_specs=in_specs, out_specs=out_specs, check_vma=False)
```

```python
import functools

import jax
import jax.numpy as jnp
import numpy as np
from jax import lax
from jax.experimental import pallas as pl
from jax.experimental.pallas import tpu as pltpu
from jax.sharding import PartitionSpec as P

EPSILON = 1e-06
HEAD = 64
HEADS_HERE = 4
FRAMES_HERE = 4
QUARTER = 64
WIDTH = 256
QUERY_SCALE = 1.4426950408889634 / 8.0
LARGE = 20 << 20
BRIEF = pl.CostEstimate(flops=1, bytes_accessed=1, transcendentals=0)
EDGE = 8
EARLY = 96
VMEM = pl.BlockSpec(memory_space=pltpu.VMEM)
SMEM = pl.BlockSpec(memory_space=pltpu.SMEM)
ANY = pl.BlockSpec(memory_space=pl.ANY)
HBM = pl.BlockSpec(memory_space=pltpu.HBM)

CORE_PAIRS = [(0, 1), (1, 0), (2, 3), (3, 2)]
CHIP_PAIRS = [(0, 2), (2, 0), (1, 3), (3, 1)]
CROSS_PAIRS = [(0, 3), (3, 0), (1, 2), (2, 1)]


def swapped(value, offset, across=False):
    count = lax.axis_size("frame")
    pairs = []
    for low in range(offset, count, 2):
        high = (low + 1) % count
        flip = 2 if across and low // EDGE != high // EDGE else 0
        for row in range(4):
            pairs.append((low * 4 + row, high * 4 + (row ^ flip)))
            pairs.append((high * 4 + (row ^ flip), low * 4 + row))
    return lax.ppermute(value, ("frame", "row"), pairs)


def layer_norm(values, gain_vec):
    average = jnp.mean(values, axis=-1, keepdims=True)
    centered = values - average
    spread = jnp.mean(centered * centered, axis=-1, keepdims=True)
    return centered * lax.rsqrt(spread + EPSILON) * gain_vec


def norm_kernel(token_hbm, gain_hbm, out_ref, token, gain, sems):
    copies = [
        pltpu.make_async_copy(token_hbm, token, sems.at[0]),
        pltpu.make_async_copy(gain_hbm, gain, sems.at[1]),
    ]
    for copy in copies:
        copy.start()
    for copy in copies:
        copy.wait()
    values = layer_norm(token[...].astype(jnp.float32), gain[...])
    out_ref[...] = values.astype(jnp.bfloat16)


def normalise(tokens, gain):
    return pl.pallas_call(
        norm_kernel,
        in_specs=[HBM] * 2,
        out_specs=VMEM,
        out_shape=jax.ShapeDtypeStruct(tokens.shape, jnp.bfloat16),
        scratch_shapes=[
            pltpu.VMEM(tokens.shape, jnp.bfloat16),
            pltpu.VMEM(gain.shape, jnp.float32),
            pltpu.SemaphoreType.DMA((2,)),
        ],
        compiler_params=pltpu.CompilerParams(vmem_limit_bytes=60 << 20),
        cost_estimate=BRIEF,
    )(tokens, gain)


def project_kernel(blocks, queries, *refs):
    parts, refs = refs[: 2 * blocks], refs[2 * blocks :]
    weight_hbm, refs = refs[0], refs[1:]
    kv_refs, refs = refs[:blocks], refs[blocks:]
    if queries:
        query_ref, refs = refs[0], refs[1:]
    weight, sem = refs
    skip = 0 if queries else 1
    copies = [
        pltpu.make_async_copy(weight_hbm.at[which], weight.at[which - skip], sem.at[which - skip])
        for which in range(skip, 3)
    ]
    for which in ([1, 2, 0] if queries else [0, 1]):
        copies[which].start()
    for copy in copies:
        copy.wait()
    for block in range(blocks):
        rows = []
        for frame in range(FRAMES_HERE):
            for part in parts[2 * block : 2 * block + 2]:
                rows.append(part[frame * QUARTER : (frame + 1) * QUARTER])
        rows = jnp.concatenate(rows, axis=0)
        key = jnp.dot(rows, weight[1 - skip], preferred_element_type=jnp.float32)
        key = key.astype(jnp.bfloat16)
        value = jnp.dot(rows, weight[2 - skip], preferred_element_type=jnp.float32)
        value = value.T.astype(jnp.bfloat16)
        kv_ref = kv_refs[block]
        for frame in range(FRAMES_HERE):
            span = slice(frame * 128, (frame + 1) * 128)
            kv_ref[frame, 0:128, :] = key[span]
            kv_ref[frame, 128:256, 0:128] = value[0:128, span]
            kv_ref[frame, 128:256, 128:256] = value[128:256, span]
        if queries:
            query = jnp.dot(rows, weight[0], preferred_element_type=jnp.float32)
            query = (query * QUERY_SCALE).T.astype(jnp.bfloat16)
            for frame in range(FRAMES_HERE):
                query_ref[frame] = query[:, frame * 128 : (frame + 1) * 128]


def project(parts, weight, queries):
    blocks = len(parts) // 2
    out_shape = [jax.ShapeDtypeStruct((FRAMES_HERE, 256, 256), jnp.bfloat16)] * blocks
    if queries:
        out_shape.append(jax.ShapeDtypeStruct((FRAMES_HERE, WIDTH, 128), jnp.bfloat16))
    used = 3 if queries else 2
    return pl.pallas_call(
        functools.partial(project_kernel, blocks, queries),
        in_specs=[VMEM] * (2 * blocks) + [HBM],
        out_specs=[VMEM] * len(out_shape),
        out_shape=out_shape,
        scratch_shapes=[pltpu.VMEM((used, 1024, WIDTH), jnp.bfloat16), pltpu.SemaphoreType.DMA((used,))],
        compiler_params=pltpu.CompilerParams(vmem_limit_bytes=LARGE),
        cost_estimate=BRIEF,
    )(*parts, weight)


def weigh(scores, high):
    return jnp.exp2(scores - high).astype(jnp.bfloat16)


def near_tiles(refs, even):
    tiles = []
    for which, ref in enumerate(refs):
        ahead = even if which == 0 else 1 - even
        for t in range(FRAMES_HERE):
            tiles.append((ref, t, (t + 1) % FRAMES_HERE, 4 + 8 * ahead + t))
    return tiles


def own_tiles(refs):
    return [(ref, t, (t + 1) % FRAMES_HERE, 8 + t) for t in range(FRAMES_HERE) for ref in refs]


def wide_tiles(ref, frame):
    tiles = []
    for t in range(FRAMES_HERE + 1):
        slot = frame + t
        position = jnp.where(slot < FRAMES_HERE, slot, slot + 12)
        tiles.append((ref, slot, frame + (t + 1) % (FRAMES_HERE + 1), position))
    return tiles


def attend_kernel(kind, *refs):
    begins, ends = kind == "own", kind == "last"
    valid_ref, query_a, query_b = refs[:3]
    refs = refs[3:]
    wide = kind in ("wide", "last")
    block_refs, refs = refs[:2], refs[2:]
    if not begins:
        high_in, total_in, refs = refs[0], refs[1], refs[2:]
    even = valid_ref[FRAMES_HERE, 0]
    if ends:
        outs, refs = refs[:4], refs[4:]
    else:
        high_out, total_out, refs = refs[0], refs[1], refs[2:]
    if wide:
        held, sems = refs
        first = even * FRAMES_HERE
        copies = [
            pltpu.make_async_copy(block_refs[0], held.at[pl.ds(first, FRAMES_HERE)], sems.at[0]),
            pltpu.make_async_copy(
                block_refs[1], held.at[pl.ds(FRAMES_HERE - first, FRAMES_HERE)], sems.at[1]
            ),
        ]
        for copy in copies:
            copy.start()
        for copy in copies:
            copy.wait()
    ones = jnp.ones((16, 128), jnp.bfloat16)
    zeros = jnp.zeros((HEAD, 256), jnp.bfloat16)

    def one_frame(frame, carried):
        if kind == "own":
            tiles = own_tiles(block_refs)
        elif kind == "near":
            tiles = near_tiles(block_refs, even)
        else:
            tiles = wide_tiles(held, frame)
        held_refs, index, keep = [], [], []
        for ref, slot, other, position in tiles:
            there = valid_ref[frame, position]
            held_refs.append(ref)
            index.append(jnp.where(there != 0, slot, other))
            keep.append(there.astype(jnp.float32).astype(jnp.bfloat16))
        count = len(tiles)

        def score(head):
            pair = head // 2
            query = jnp.concatenate(
                [
                    query_a[frame, head * HEAD : (head + 1) * HEAD, :],
                    query_b[frame, head * HEAD : (head + 1) * HEAD, :],
                ],
                axis=1,
            )
            both = [query, zeros] if head % 2 == 0 else [zeros, query]
            both = jnp.concatenate(both, axis=0)
            return [
                jnp.dot(
                    held_refs[t][index[t], 0:128, pair * 128 : (pair + 1) * 128],
                    both,
                    preferred_element_type=jnp.float32,
                )
                for t in range(count)
            ]

        def absorb(head, scores):
            pair = head // 2
            start = 128 + (head % 2) * HEAD
            high = scores[0].reshape(-1, 8, 256).max(axis=0)
            for s in scores[1:]:
                high = jnp.maximum(high, s.reshape(-1, 8, 256).max(axis=0))
            high = jnp.max(high, axis=0, keepdims=True)
            total = None
            if not begins:
                old = high_in[frame, head, 0:1, :]
                high = jnp.maximum(high, old)
                total = total_in[frame, head] * jnp.exp2(old - high)
            for t in range(0, count, 2):
                group = range(t, min(t + 2, count))
                weights = [weigh(scores[g], high) for g in group]
                sides = []
                for g in group:
                    value = held_refs[g][
                        index[g], start : start + HEAD, pair * 128 : (pair + 1) * 128
                    ]
                    sides.append(jnp.concatenate([value, ones], axis=0) * keep[g])
                added = jnp.dot(
                    jnp.concatenate(sides, axis=1),
                    jnp.concatenate(weights, axis=0),
                    preferred_element_type=jnp.float32,
                )
                total = added if total is None else total + added
            if ends:
                return total[0:HEAD] / total[HEAD : HEAD + 1]
            total_out[frame, head] = total
            high_out[frame, head] = jnp.broadcast_to(high, (8, 256))
            return None

        contexts = []
        scores = score(0)
        for head in range(HEADS_HERE):
            later = score(head + 1) if head + 1 < HEADS_HERE else None
            contexts.append(absorb(head, scores))
            scores = later
        if ends:
            context = jnp.concatenate(contexts, axis=0).T.astype(jnp.bfloat16)
            rows = pl.ds(pl.multiple_of(frame * QUARTER, QUARTER), QUARTER)
            for j in range(4):
                outs[j][rows, :] = context[j * QUARTER : (j + 1) * QUARTER]
        return carried

    lax.fori_loop(0, FRAMES_HERE, one_frame, 0)


def attend(kind, valid, query_a, query_b, block_list, state=()):
    ends = kind == "last"
    scratch = []
    if kind in ("wide", "last"):
        scratch = [
            pltpu.VMEM((2 * FRAMES_HERE, 256, 256), jnp.bfloat16),
            pltpu.SemaphoreType.DMA((2,)),
        ]
    if ends:
        out_shape = [jax.ShapeDtypeStruct((FRAMES_HERE * QUARTER, WIDTH), jnp.bfloat16)] * 4
    else:
        out_shape = [
            jax.ShapeDtypeStruct((FRAMES_HERE, HEADS_HERE, 8, 256), jnp.float32),
            jax.ShapeDtypeStruct((FRAMES_HERE, HEADS_HERE, HEAD + 16, 256), jnp.float32),
        ]
    inputs = [valid, query_a, query_b, *block_list, *state]
    return pl.pallas_call(
        functools.partial(attend_kernel, kind),
        in_specs=[SMEM] + [VMEM] * (len(inputs) - 1),
        out_specs=[VMEM] * len(out_shape),
        out_shape=out_shape,
        scratch_shapes=scratch,
        compiler_params=pltpu.CompilerParams(vmem_limit_bytes=36 << 20),
        cost_estimate=BRIEF,
    )(*inputs)


def finish_kernel(*refs):
    contexts, weights, (token_ref, gain_ref, proj_ref, out_ref, map_ref) = (
        refs[:4],
        refs[4:10],
        refs[10:],
    )
    own, beside, *parts = [ref[...] for ref in weights]
    weights = [own, beside]
    for half in (parts[:2], parts[2:]):
        weights.append(jnp.concatenate(half, axis=0))
    total = token_ref[...].astype(jnp.float32)
    mixed = jnp.dot(contexts[0][...], weights[0], preferred_element_type=jnp.float32)
    for c, w in zip(contexts[1:], weights[1:]):
        mixed = mixed + jnp.dot(c[...], w, preferred_element_type=jnp.float32)
    attended = (total + mixed).astype(jnp.bfloat16)
    out_ref[...] = attended
    lifted = layer_norm(attended.astype(jnp.float32), gain_ref[...]).astype(jnp.bfloat16)
    mapped = jnp.dot(lifted, proj_ref[...], preferred_element_type=jnp.float32)
    map_ref[...] = mapped.astype(jnp.bfloat16)


def finish(contexts, weights, tokens, gain, proj):
    return pl.pallas_call(
        finish_kernel,
        in_specs=[VMEM] * 13,
        out_specs=[VMEM] * 2,
        out_shape=[
            jax.ShapeDtypeStruct((256, 1024), jnp.bfloat16),
            jax.ShapeDtypeStruct((256, 256), jnp.bfloat16),
        ],
        compiler_params=pltpu.CompilerParams(vmem_limit_bytes=32 << 20),
        cost_estimate=BRIEF,
    )(*contexts, *weights, tokens, gain, proj)


def join_kernel(row_ref, beside_ref, own_ref, across_ref, one_ref, two_ref, out_ref):
    def widen(values):
        count = values.shape[0]
        column = lax.broadcasted_iota(jnp.int32, (count, 256), 0) % 32
        left = jnp.where(column == 0, 0.0, pltpu.roll(values, 1, 0))
        right = jnp.where(column == 31, 0.0, pltpu.roll(values, count - 1, 0))
        return jnp.concatenate(
            [left.astype(jnp.bfloat16), values.astype(jnp.bfloat16), right.astype(jnp.bfloat16)],
            axis=1,
        )

    def conv(wide, rows_in, weight_ref):
        rows_out = rows_in - 2
        summed = None
        for a in range(3):
            window = jnp.concatenate(
                [
                    wide[(f * rows_in + a) * 32 : (f * rows_in + a + rows_out) * 32]
                    for f in range(FRAMES_HERE)
                ],
                axis=0,
            )
            added = jnp.dot(window, weight_ref[a], preferred_element_type=jnp.float32)
            summed = added if summed is None else summed + added
        return summed

    own = own_ref[...].astype(jnp.float32)
    place = row_ref[0]
    odd = place % 2 == 1
    beside = beside_ref[...].astype(jnp.float32)
    across = across_ref[...].astype(jnp.float32)
    before = jnp.where(odd, beside, across)
    after = jnp.where(odd, across, beside)
    six = []
    for f in range(FRAMES_HERE):
        span = slice(f * QUARTER, (f + 1) * QUARTER)
        six += [before[span], own[span], after[span]]
    six = jnp.maximum(jnp.concatenate(six, axis=0), 0.0)
    inner = conv(widen(six), 6, one_ref)
    inner = jnp.maximum(inner, 0.0)
    row = (lax.broadcasted_iota(jnp.int32, (512, 256), 0) // 32) % 4
    drop = ((row == 0) & (place == 0)) | ((row == 3) & (place == 3))
    inner = jnp.where(drop, 0.0, inner)
    joined = conv(widen(inner), 4, two_ref)
    out_ref[...] = (own + joined).astype(jnp.bfloat16)


def join(row, beside, own, across, one, two):
    return pl.pallas_call(
        join_kernel,
        in_specs=[SMEM] + [VMEM] * 5,
        out_specs=VMEM,
        out_shape=jax.ShapeDtypeStruct((256, 256), jnp.bfloat16),
        compiler_params=pltpu.CompilerParams(vmem_limit_bytes=32 << 20),
        cost_estimate=BRIEF,
    )(row, beside, own, across, one, two)


def shards(
    tokens,
    norm_gain,
    qkv_weight,
    out_weight,
    key_offsets,
    feat_gain,
    proj_weight,
    conv_one,
    conv_two,
):
    own = tokens.reshape(FRAMES_HERE * QUARTER, 1024)
    core = lambda value: lax.ppermute(value, "row", CORE_PAIRS)
    chip = lambda value: lax.ppermute(value, "row", CHIP_PAIRS)
    tie = lax.optimization_barrier

    positions = np.arange(20)
    distance = positions[None, :] - 8 - np.arange(FRAMES_HERE)[:, None]
    valid = jnp.any(key_offsets[:, :, None] == distance[:, None, :], axis=1).astype(jnp.int32)
    block = lax.axis_index("frame")
    even = 1 - block % 2
    valid = jnp.concatenate([valid, jnp.full((1, 20), even, jnp.int32)], axis=0)
    edge_block = (block % EDGE == 0) | (block % EDGE == EDGE - 1)

    normed = normalise(own, norm_gain.reshape(1, 1024))
    near = core(normed)
    far = chip(normed)
    side = swapped(normed, 0)
    other = swapped(normed, 1, True)
    kv_a, query_a = project([normed, near], qkv_weight, True)
    far, kv_a = tie((far, kv_a))
    far_near = core(far)
    out_early, far = tie((out_weight[:EARLY], far))
    chip_early = chip(out_early)
    far_near, side, other = tie((far_near, side, other))
    kv_b, query_b = project([far, far_near], qkv_weight, True)
    kv_b, chip_early = tie((kv_b, chip_early))
    side_b = swapped(kv_b, 0)
    other_b = swapped(jnp.where(edge_block, kv_a, kv_b), 1)
    side, other, kv_b = tie((side, other, kv_b))
    side_near, other_near = core(side), core(other)
    state = attend("own", valid, query_a, query_b, [kv_a, kv_b])
    side, state = tie((side, state))
    side_a, other_a = project([side, side_near, other, other_near], qkv_weight, False)
    side_2a, other_2a = swapped(other_a, 0), swapped(side_a, 1)
    state = attend("near", valid, query_a, query_b, [side_a, other_a], state)
    side_b, other_b, state = tie((side_b, other_b, state))
    side_2b, other_2b = swapped(other_b, 0), swapped(side_b, 1)
    state = attend("near", valid, query_a, query_b, [side_b, other_b], state)
    state = attend("wide", valid, query_a, query_b, [side_2a, other_2a], state)
    out_last, out_late, chip_early, side_2b, other_2b, state = tie(
        (out_weight, out_weight[EARLY:], chip_early, side_2b, other_2b, state)
    )
    chip_late = chip(out_late)
    weight_core, cross_early = core(out_last), core(chip_early)
    parts = attend("last", valid, query_a, query_b, [side_2b, other_2b], state)
    chip_late, *parts = tie((chip_late, *parts))
    cross_late = core(chip_late)

    contexts = [
        parts[0],
        core(parts[1]),
        chip(parts[2]),
        lax.ppermute(parts[3], "row", CROSS_PAIRS),
    ]
    weights = [out_weight, weight_core, chip_early, chip_late, cross_early, cross_late]
    attended, mapped = finish(contexts, weights, own, feat_gain.reshape(1, 1024), proj_weight)

    across = lax.ppermute(mapped, "row", [(1, 2), (2, 1)])
    beside = core(mapped)
    place = lax.axis_index("row").astype(jnp.int32).reshape(1)
    joined = join(
        place,
        beside,
        mapped,
        across,
        conv_one.reshape(3, 768, 256),
        conv_two.reshape(3, 768, 256),
    )
    return attended.reshape(tokens.shape), joined.reshape(tokens.shape[:3] + (256,))


def solution(mesh):
    in_specs = (
        P("frame", "row", None, None),
        P(),
        P(None, None, "row"),
        P("row", None),
        P("frame", None),
        P(),
        P(),
        P(),
        P(),
    )
    out_specs = (P("frame", "row", None, None), P("frame", "row", None, None))
    return jax.shard_map(shards, mesh=mesh, in_specs=in_specs, out_specs=out_specs, check_vma=False)
```

```python
import functools

import jax
import jax.numpy as jnp
import numpy as np
from jax import lax
from jax.experimental import pallas as pl
from jax.experimental.pallas import tpu as pltpu
from jax.sharding import PartitionSpec as P

EPSILON = 1e-06
HEAD = 64
HEADS_HERE = 4
FRAMES_HERE = 4
QUARTER = 64
WIDTH = 256
QUERY_SCALE = 1.4426950408889634 / 8.0
LARGE = 20 << 20
BRIEF = pl.CostEstimate(flops=1, bytes_accessed=1, transcendentals=0)
EDGE = 8
TOGETHER = 4
EARLY = 96
VMEM = pl.BlockSpec(memory_space=pltpu.VMEM)
SMEM = pl.BlockSpec(memory_space=pltpu.SMEM)
ANY = pl.BlockSpec(memory_space=pl.ANY)
HBM = pl.BlockSpec(memory_space=pltpu.HBM)

CORE_PAIRS = [(0, 1), (1, 0), (2, 3), (3, 2)]
CHIP_PAIRS = [(0, 2), (2, 0), (1, 3), (3, 1)]
CROSS_PAIRS = [(0, 3), (3, 0), (1, 2), (2, 1)]


def swapped(value, offset, across=False):
    count = lax.axis_size("frame")
    pairs = []
    for low in range(offset, count, 2):
        high = (low + 1) % count
        flip = 2 if across and low // EDGE != high // EDGE else 0
        for row in range(4):
            pairs.append((low * 4 + row, high * 4 + (row ^ flip)))
            pairs.append((high * 4 + (row ^ flip), low * 4 + row))
    return lax.ppermute(value, ("frame", "row"), pairs)


def layer_norm(values, gain_vec):
    average = jnp.mean(values, axis=-1, keepdims=True)
    centered = values - average
    spread = jnp.mean(centered * centered, axis=-1, keepdims=True)
    return centered * lax.rsqrt(spread + EPSILON) * gain_vec


def norm_kernel(token_hbm, gain_hbm, out_ref, token, gain, sems):
    copies = [
        pltpu.make_async_copy(token_hbm, token, sems.at[0]),
        pltpu.make_async_copy(gain_hbm, gain, sems.at[1]),
    ]
    for copy in copies:
        copy.start()
    for copy in copies:
        copy.wait()
    values = layer_norm(token[...].astype(jnp.float32), gain[...])
    out_ref[...] = values.astype(jnp.bfloat16)


def normalise(tokens, gain):
    return pl.pallas_call(
        norm_kernel,
        in_specs=[HBM] * 2,
        out_specs=VMEM,
        out_shape=jax.ShapeDtypeStruct(tokens.shape, jnp.bfloat16),
        scratch_shapes=[
            pltpu.VMEM(tokens.shape, jnp.bfloat16),
            pltpu.VMEM(gain.shape, jnp.float32),
            pltpu.SemaphoreType.DMA((2,)),
        ],
        compiler_params=pltpu.CompilerParams(vmem_limit_bytes=60 << 20),
        cost_estimate=BRIEF,
    )(tokens, gain)


def project_kernel(blocks, queries, *refs):
    parts, refs = refs[: 2 * blocks], refs[2 * blocks :]
    weight_hbm, refs = refs[0], refs[1:]
    kv_refs, refs = refs[:blocks], refs[blocks:]
    if queries:
        query_ref, refs = refs[0], refs[1:]
    weight, sem = refs
    skip = 0 if queries else 1
    copies = [
        pltpu.make_async_copy(weight_hbm.at[which], weight.at[which - skip], sem.at[which - skip])
        for which in range(skip, 3)
    ]
    for which in ([1, 2, 0] if queries else [0, 1]):
        copies[which].start()
    for copy in copies:
        copy.wait()
    for block in range(blocks):
        rows = []
        for frame in range(FRAMES_HERE):
            for part in parts[2 * block : 2 * block + 2]:
                rows.append(part[frame * QUARTER : (frame + 1) * QUARTER])
        rows = jnp.concatenate(rows, axis=0)
        key = jnp.dot(rows, weight[1 - skip], preferred_element_type=jnp.float32)
        key = key.astype(jnp.bfloat16)
        value = jnp.dot(rows, weight[2 - skip], preferred_element_type=jnp.float32)
        value = value.T.astype(jnp.bfloat16)
        kv_ref = kv_refs[block]
        for frame in range(FRAMES_HERE):
            span = slice(frame * 128, (frame + 1) * 128)
            kv_ref[frame, 0:128, :] = key[span]
            kv_ref[frame, 128:256, 0:128] = value[0:128, span]
            kv_ref[frame, 128:256, 128:256] = value[128:256, span]
        if queries:
            query = jnp.dot(rows, weight[0], preferred_element_type=jnp.float32)
            query = (query * QUERY_SCALE).T.astype(jnp.bfloat16)
            for frame in range(FRAMES_HERE):
                query_ref[frame] = query[:, frame * 128 : (frame + 1) * 128]


def project(parts, weight, queries):
    blocks = len(parts) // 2
    out_shape = [jax.ShapeDtypeStruct((FRAMES_HERE, 256, 256), jnp.bfloat16)] * blocks
    if queries:
        out_shape.append(jax.ShapeDtypeStruct((FRAMES_HERE, WIDTH, 128), jnp.bfloat16))
    used = 3 if queries else 2
    return pl.pallas_call(
        functools.partial(project_kernel, blocks, queries),
        in_specs=[VMEM] * (2 * blocks) + [HBM],
        out_specs=[VMEM] * len(out_shape),
        out_shape=out_shape,
        scratch_shapes=[pltpu.VMEM((used, 1024, WIDTH), jnp.bfloat16), pltpu.SemaphoreType.DMA((used,))],
        compiler_params=pltpu.CompilerParams(vmem_limit_bytes=LARGE),
        cost_estimate=BRIEF,
    )(*parts, weight)


def weigh(scores, high):
    return jnp.exp2(scores - high).astype(jnp.bfloat16)


def near_tiles(refs, even):
    tiles = []
    for which, ref in enumerate(refs):
        ahead = even if which == 0 else 1 - even
        for t in range(FRAMES_HERE):
            tiles.append((ref, t, (t + 1) % FRAMES_HERE, 4 + 8 * ahead + t))
    return tiles


def own_tiles(refs):
    return [(ref, t, (t + 1) % FRAMES_HERE, 8 + t) for t in range(FRAMES_HERE) for ref in refs]


def wide_tiles(ref, frame):
    tiles = []
    for t in range(FRAMES_HERE + 1):
        slot = frame + t
        position = jnp.where(slot < FRAMES_HERE, slot, slot + 12)
        tiles.append((ref, slot, frame + (t + 1) % (FRAMES_HERE + 1), position))
    return tiles


def attend_kernel(kind, *refs):
    begins, ends = kind == "own", kind == "last"
    valid_ref, query_a, query_b = refs[:3]
    refs = refs[3:]
    wide = kind in ("wide", "last")
    block_refs, refs = refs[:2], refs[2:]
    if not begins:
        high_in, total_in, refs = refs[0], refs[1], refs[2:]
    even = valid_ref[FRAMES_HERE, 0]
    if ends:
        outs, refs = refs[:4], refs[4:]
    else:
        high_out, total_out, refs = refs[0], refs[1], refs[2:]
    if wide:
        held, sems = refs
        first = even * FRAMES_HERE
        copies = [
            pltpu.make_async_copy(block_refs[0], held.at[pl.ds(first, FRAMES_HERE)], sems.at[0]),
            pltpu.make_async_copy(
                block_refs[1], held.at[pl.ds(FRAMES_HERE - first, FRAMES_HERE)], sems.at[1]
            ),
        ]
        for copy in copies:
            copy.start()
        for copy in copies:
            copy.wait()
    ones = jnp.ones((16, 128), jnp.bfloat16)
    zeros = jnp.zeros((HEAD, 256), jnp.bfloat16)

    def prepare(frame):
        if kind == "own":
            tiles = own_tiles(block_refs)
        elif kind == "near":
            tiles = near_tiles(block_refs, even)
        else:
            tiles = wide_tiles(held, frame)
        held_refs, index, keep = [], [], []
        for ref, slot, other, position in tiles:
            there = valid_ref[frame, position]
            held_refs.append(ref)
            index.append(jnp.where(there != 0, slot, other))
            keep.append(there.astype(jnp.float32).astype(jnp.bfloat16))
        return frame, held_refs, index, keep

    def score(unit, head):
        frame, held_refs, index, _ = unit
        pair = head // 2
        query = jnp.concatenate(
            [
                query_a[frame, head * HEAD : (head + 1) * HEAD, :],
                query_b[frame, head * HEAD : (head + 1) * HEAD, :],
            ],
            axis=1,
        )
        both = [query, zeros] if head % 2 == 0 else [zeros, query]
        both = jnp.concatenate(both, axis=0)
        return [
            jnp.dot(
                ref[slot, 0:128, pair * 128 : (pair + 1) * 128],
                both,
                preferred_element_type=jnp.float32,
            )
            for ref, slot in zip(held_refs, index)
        ]

    def absorb(unit, head, scores):
        frame, held_refs, index, keep = unit
        pair = head // 2
        start = 128 + (head % 2) * HEAD
        high = scores[0].reshape(-1, 8, 256).max(axis=0)
        for s in scores[1:]:
            high = jnp.maximum(high, s.reshape(-1, 8, 256).max(axis=0))
        high = jnp.max(high, axis=0, keepdims=True)
        total = None
        if not begins:
            old = high_in[frame, head, 0:1, :]
            high = jnp.maximum(high, old)
            total = total_in[frame, head] * jnp.exp2(old - high)
        for t in range(0, len(scores), 2):
            group = range(t, min(t + 2, len(scores)))
            weights = [weigh(scores[g], high) for g in group]
            sides = []
            for g in group:
                value = held_refs[g][
                    index[g], start : start + HEAD, pair * 128 : (pair + 1) * 128
                ]
                sides.append(jnp.concatenate([value, ones], axis=0) * keep[g])
            added = jnp.dot(
                jnp.concatenate(sides, axis=1),
                jnp.concatenate(weights, axis=0),
                preferred_element_type=jnp.float32,
            )
            total = added if total is None else total + added
        if ends:
            return total[0:HEAD] / total[HEAD : HEAD + 1]
        total_out[frame, head] = total
        high_out[frame, head] = jnp.broadcast_to(high, (8, 256))
        return None

    def some_frames(step, carried):
        units = [prepare(step * TOGETHER + k) for k in range(TOGETHER)]
        order = [(unit, head) for unit in units for head in range(HEADS_HERE)]
        contexts = []
        scores = score(*order[0])
        for place, (unit, head) in enumerate(order):
            later = score(*order[place + 1]) if place + 1 < len(order) else None
            contexts.append(absorb(unit, head, scores))
            scores = later
            if ends and head == HEADS_HERE - 1:
                context = jnp.concatenate(contexts, axis=0).T.astype(jnp.bfloat16)
                contexts = []
                rows = pl.ds(pl.multiple_of(unit[0] * QUARTER, QUARTER), QUARTER)
                for j in range(4):
                    outs[j][rows, :] = context[j * QUARTER : (j + 1) * QUARTER]
        return carried

    lax.fori_loop(0, FRAMES_HERE // TOGETHER, some_frames, 0)


def attend(kind, valid, query_a, query_b, block_list, state=()):
    ends = kind == "last"
    scratch = []
    if kind in ("wide", "last"):
        scratch = [
            pltpu.VMEM((2 * FRAMES_HERE, 256, 256), jnp.bfloat16),
            pltpu.SemaphoreType.DMA((2,)),
        ]
    if ends:
        out_shape = [jax.ShapeDtypeStruct((FRAMES_HERE * QUARTER, WIDTH), jnp.bfloat16)] * 4
    else:
        out_shape = [
            jax.ShapeDtypeStruct((FRAMES_HERE, HEADS_HERE, 8, 256), jnp.float32),
            jax.ShapeDtypeStruct((FRAMES_HERE, HEADS_HERE, HEAD + 16, 256), jnp.float32),
        ]
    inputs = [valid, query_a, query_b, *block_list, *state]
    return pl.pallas_call(
        functools.partial(attend_kernel, kind),
        in_specs=[SMEM] + [VMEM] * (len(inputs) - 1),
        out_specs=[VMEM] * len(out_shape),
        out_shape=out_shape,
        scratch_shapes=scratch,
        compiler_params=pltpu.CompilerParams(vmem_limit_bytes=36 << 20),
        cost_estimate=BRIEF,
    )(*inputs)


def finish_kernel(*refs):
    contexts, weights, (token_ref, gain_ref, proj_ref, out_ref, map_ref) = (
        refs[:4],
        refs[4:10],
        refs[10:],
    )
    own, beside, *parts = [ref[...] for ref in weights]
    weights = [own, beside]
    for half in (parts[:2], parts[2:]):
        weights.append(jnp.concatenate(half, axis=0))
    total = token_ref[...].astype(jnp.float32)
    mixed = jnp.dot(contexts[0][...], weights[0], preferred_element_type=jnp.float32)
    for c, w in zip(contexts[1:], weights[1:]):
        mixed = mixed + jnp.dot(c[...], w, preferred_element_type=jnp.float32)
    attended = (total + mixed).astype(jnp.bfloat16)
    out_ref[...] = attended
    lifted = layer_norm(attended.astype(jnp.float32), gain_ref[...]).astype(jnp.bfloat16)
    mapped = jnp.dot(lifted, proj_ref[...], preferred_element_type=jnp.float32)
    map_ref[...] = mapped.astype(jnp.bfloat16)


def finish(contexts, weights, tokens, gain, proj):
    return pl.pallas_call(
        finish_kernel,
        in_specs=[VMEM] * 13,
        out_specs=[VMEM] * 2,
        out_shape=[
            jax.ShapeDtypeStruct((256, 1024), jnp.bfloat16),
            jax.ShapeDtypeStruct((256, 256), jnp.bfloat16),
        ],
        compiler_params=pltpu.CompilerParams(vmem_limit_bytes=32 << 20),
        cost_estimate=BRIEF,
    )(*contexts, *weights, tokens, gain, proj)


def join_kernel(row_ref, beside_ref, own_ref, across_ref, one_ref, two_ref, out_ref):
    def widen(values):
        count = values.shape[0]
        column = lax.broadcasted_iota(jnp.int32, (count, 256), 0) % 32
        left = jnp.where(column == 0, 0.0, pltpu.roll(values, 1, 0))
        right = jnp.where(column == 31, 0.0, pltpu.roll(values, count - 1, 0))
        return jnp.concatenate(
            [left.astype(jnp.bfloat16), values.astype(jnp.bfloat16), right.astype(jnp.bfloat16)],
            axis=1,
        )

    def conv(wide, rows_in, weight_ref):
        rows_out = rows_in - 2
        summed = None
        for a in range(3):
            window = jnp.concatenate(
                [
                    wide[(f * rows_in + a) * 32 : (f * rows_in + a + rows_out) * 32]
                    for f in range(FRAMES_HERE)
                ],
                axis=0,
            )
            added = jnp.dot(window, weight_ref[a], preferred_element_type=jnp.float32)
            summed = added if summed is None else summed + added
        return summed

    own = own_ref[...].astype(jnp.float32)
    place = row_ref[0]
    odd = place % 2 == 1
    beside = beside_ref[...].astype(jnp.float32)
    across = across_ref[...].astype(jnp.float32)
    before = jnp.where(odd, beside, across)
    after = jnp.where(odd, across, beside)
    six = []
    for f in range(FRAMES_HERE):
        span = slice(f * QUARTER, (f + 1) * QUARTER)
        six += [before[span], own[span], after[span]]
    six = jnp.maximum(jnp.concatenate(six, axis=0), 0.0)
    inner = conv(widen(six), 6, one_ref)
    inner = jnp.maximum(inner, 0.0)
    row = (lax.broadcasted_iota(jnp.int32, (512, 256), 0) // 32) % 4
    drop = ((row == 0) & (place == 0)) | ((row == 3) & (place == 3))
    inner = jnp.where(drop, 0.0, inner)
    joined = conv(widen(inner), 4, two_ref)
    out_ref[...] = (own + joined).astype(jnp.bfloat16)


def join(row, beside, own, across, one, two):
    return pl.pallas_call(
        join_kernel,
        in_specs=[SMEM] + [VMEM] * 5,
        out_specs=VMEM,
        out_shape=jax.ShapeDtypeStruct((256, 256), jnp.bfloat16),
        compiler_params=pltpu.CompilerParams(vmem_limit_bytes=32 << 20),
        cost_estimate=BRIEF,
    )(row, beside, own, across, one, two)


def shards(
    tokens,
    norm_gain,
    qkv_weight,
    out_weight,
    key_offsets,
    feat_gain,
    proj_weight,
    conv_one,
    conv_two,
):
    own = tokens.reshape(FRAMES_HERE * QUARTER, 1024)
    core = lambda value: lax.ppermute(value, "row", CORE_PAIRS)
    chip = lambda value: lax.ppermute(value, "row", CHIP_PAIRS)
    tie = lax.optimization_barrier

    positions = np.arange(20)
    distance = positions[None, :] - 8 - np.arange(FRAMES_HERE)[:, None]
    valid = jnp.any(key_offsets[:, :, None] == distance[:, None, :], axis=1).astype(jnp.int32)
    block = lax.axis_index("frame")
    even = 1 - block % 2
    valid = jnp.concatenate([valid, jnp.full((1, 20), even, jnp.int32)], axis=0)
    edge_block = (block % EDGE == 0) | (block % EDGE == EDGE - 1)

    normed = normalise(own, norm_gain.reshape(1, 1024))
    near = core(normed)
    far = chip(normed)
    side = swapped(normed, 0)
    other = swapped(normed, 1, True)
    kv_a, query_a = project([normed, near], qkv_weight, True)
    far, kv_a = tie((far, kv_a))
    far_near = core(far)
    out_early, far = tie((out_weight[:EARLY], far))
    chip_early = chip(out_early)
    far_near, side, other = tie((far_near, side, other))
    kv_b, query_b = project([far, far_near], qkv_weight, True)
    kv_b, chip_early = tie((kv_b, chip_early))
    side_b = swapped(kv_b, 0)
    other_b = swapped(jnp.where(edge_block, kv_a, kv_b), 1)
    side, other, kv_b = tie((side, other, kv_b))
    side_near, other_near = core(side), core(other)
    state = attend("own", valid, query_a, query_b, [kv_a, kv_b])
    side, state = tie((side, state))
    side_a, other_a = project([side, side_near, other, other_near], qkv_weight, False)
    side_2a, other_2a = swapped(other_a, 0), swapped(side_a, 1)
    state = attend("near", valid, query_a, query_b, [side_a, other_a], state)
    side_b, other_b, state = tie((side_b, other_b, state))
    side_2b, other_2b = swapped(other_b, 0), swapped(side_b, 1)
    state = attend("near", valid, query_a, query_b, [side_b, other_b], state)
    state = attend("wide", valid, query_a, query_b, [side_2a, other_2a], state)
    out_last, out_late, chip_early, side_2b, other_2b, state = tie(
        (out_weight, out_weight[EARLY:], chip_early, side_2b, other_2b, state)
    )
    chip_late = chip(out_late)
    weight_core, cross_early = core(out_last), core(chip_early)
    parts = attend("last", valid, query_a, query_b, [side_2b, other_2b], state)
    chip_late, *parts = tie((chip_late, *parts))
    cross_late = core(chip_late)

    contexts = [
        parts[0],
        core(parts[1]),
        chip(parts[2]),
        lax.ppermute(parts[3], "row", CROSS_PAIRS),
    ]
    weights = [out_weight, weight_core, chip_early, chip_late, cross_early, cross_late]
    attended, mapped = finish(contexts, weights, own, feat_gain.reshape(1, 1024), proj_weight)

    across = lax.ppermute(mapped, "row", [(1, 2), (2, 1)])
    beside = core(mapped)
    place = lax.axis_index("row").astype(jnp.int32).reshape(1)
    joined = join(
        place,
        beside,
        mapped,
        across,
        conv_one.reshape(3, 768, 256),
        conv_two.reshape(3, 768, 256),
    )
    return attended.reshape(tokens.shape), joined.reshape(tokens.shape[:3] + (256,))


def solution(mesh):
    in_specs = (
        P("frame", "row", None, None),
        P(),
        P(None, None, "row"),
        P("row", None),
        P("frame", None),
        P(),
        P(),
        P(),
        P(),
    )
    out_specs = (P("frame", "row", None, None), P("frame", "row", None, None))
    return jax.shard_map(shards, mesh=mesh, in_specs=in_specs, out_specs=out_specs, check_vma=False)
```

```python
import functools

import jax
import jax.numpy as jnp
import numpy as np
from jax import lax
from jax.experimental import pallas as pl
from jax.experimental.pallas import tpu as pltpu
from jax.sharding import PartitionSpec as P

EPSILON = 1e-06
HEAD = 64
HEADS_HERE = 4
FRAMES_HERE = 4
QUARTER = 64
WIDTH = 256
QUERY_SCALE = 1.4426950408889634 / 8.0
LARGE = 20 << 20
BRIEF = pl.CostEstimate(flops=1, bytes_accessed=1, transcendentals=0)
EDGE = 8
TOGETHER = 2
EARLY = 96
VMEM = pl.BlockSpec(memory_space=pltpu.VMEM)
SMEM = pl.BlockSpec(memory_space=pltpu.SMEM)
ANY = pl.BlockSpec(memory_space=pl.ANY)
HBM = pl.BlockSpec(memory_space=pltpu.HBM)

CORE_PAIRS = [(0, 1), (1, 0), (2, 3), (3, 2)]
CHIP_PAIRS = [(0, 2), (2, 0), (1, 3), (3, 1)]
CROSS_PAIRS = [(0, 3), (3, 0), (1, 2), (2, 1)]


def swapped(value, offset, across=False):
    count = lax.axis_size("frame")
    pairs = []
    for low in range(offset, count, 2):
        high = (low + 1) % count
        flip = 2 if across and low // EDGE != high // EDGE else 0
        for row in range(4):
            pairs.append((low * 4 + row, high * 4 + (row ^ flip)))
            pairs.append((high * 4 + (row ^ flip), low * 4 + row))
    return lax.ppermute(value, ("frame", "row"), pairs)


def layer_norm(values, gain_vec):
    average = jnp.mean(values, axis=-1, keepdims=True)
    centered = values - average
    spread = jnp.mean(centered * centered, axis=-1, keepdims=True)
    return centered * lax.rsqrt(spread + EPSILON) * gain_vec


def norm_kernel(token_hbm, gain_hbm, out_ref, token, gain, sems):
    copies = [
        pltpu.make_async_copy(token_hbm, token, sems.at[0]),
        pltpu.make_async_copy(gain_hbm, gain, sems.at[1]),
    ]
    for copy in copies:
        copy.start()
    for copy in copies:
        copy.wait()
    values = layer_norm(token[...].astype(jnp.float32), gain[...])
    out_ref[...] = values.astype(jnp.bfloat16)


def normalise(tokens, gain):
    return pl.pallas_call(
        norm_kernel,
        in_specs=[HBM] * 2,
        out_specs=VMEM,
        out_shape=jax.ShapeDtypeStruct(tokens.shape, jnp.bfloat16),
        scratch_shapes=[
            pltpu.VMEM(tokens.shape, jnp.bfloat16),
            pltpu.VMEM(gain.shape, jnp.float32),
            pltpu.SemaphoreType.DMA((2,)),
        ],
        compiler_params=pltpu.CompilerParams(vmem_limit_bytes=60 << 20),
        cost_estimate=BRIEF,
    )(tokens, gain)


def project_kernel(blocks, queries, *refs):
    parts, refs = refs[: 2 * blocks], refs[2 * blocks :]
    weight_hbm, refs = refs[0], refs[1:]
    kv_refs, refs = refs[:blocks], refs[blocks:]
    if queries:
        query_ref, refs = refs[0], refs[1:]
    weight, sem = refs
    skip = 0 if queries else 1
    copies = [
        pltpu.make_async_copy(weight_hbm.at[which], weight.at[which - skip], sem.at[which - skip])
        for which in range(skip, 3)
    ]
    for which in ([1, 2, 0] if queries else [0, 1]):
        copies[which].start()
    for copy in copies:
        copy.wait()
    for block in range(blocks):
        rows = []
        for frame in range(FRAMES_HERE):
            for part in parts[2 * block : 2 * block + 2]:
                rows.append(part[frame * QUARTER : (frame + 1) * QUARTER])
        rows = jnp.concatenate(rows, axis=0)
        key = jnp.dot(rows, weight[1 - skip], preferred_element_type=jnp.float32)
        key = key.astype(jnp.bfloat16)
        value = jnp.dot(rows, weight[2 - skip], preferred_element_type=jnp.float32)
        value = value.T.astype(jnp.bfloat16)
        kv_ref = kv_refs[block]
        for frame in range(FRAMES_HERE):
            span = slice(frame * 128, (frame + 1) * 128)
            kv_ref[frame, 0:128, :] = key[span]
            kv_ref[frame, 128:256, 0:128] = value[0:128, span]
            kv_ref[frame, 128:256, 128:256] = value[128:256, span]
        if queries:
            query = jnp.dot(rows, weight[0], preferred_element_type=jnp.float32)
            query = (query * QUERY_SCALE).T.astype(jnp.bfloat16)
            for frame in range(FRAMES_HERE):
                query_ref[frame] = query[:, frame * 128 : (frame + 1) * 128]


def project(parts, weight, queries):
    blocks = len(parts) // 2
    out_shape = [jax.ShapeDtypeStruct((FRAMES_HERE, 256, 256), jnp.bfloat16)] * blocks
    if queries:
        out_shape.append(jax.ShapeDtypeStruct((FRAMES_HERE, WIDTH, 128), jnp.bfloat16))
    used = 3 if queries else 2
    return pl.pallas_call(
        functools.partial(project_kernel, blocks, queries),
        in_specs=[VMEM] * (2 * blocks) + [HBM],
        out_specs=[VMEM] * len(out_shape),
        out_shape=out_shape,
        scratch_shapes=[pltpu.VMEM((used, 1024, WIDTH), jnp.bfloat16), pltpu.SemaphoreType.DMA((used,))],
        compiler_params=pltpu.CompilerParams(vmem_limit_bytes=LARGE),
        cost_estimate=BRIEF,
    )(*parts, weight)


def weigh(scores, high):
    return jnp.exp2(scores - high).astype(jnp.bfloat16)


def near_tiles(refs, even):
    tiles = []
    for which, ref in enumerate(refs):
        ahead = even if which == 0 else 1 - even
        for t in range(FRAMES_HERE):
            tiles.append((ref, t, (t + 1) % FRAMES_HERE, 4 + 8 * ahead + t))
    return tiles


def own_tiles(refs):
    return [(ref, t, (t + 1) % FRAMES_HERE, 8 + t) for t in range(FRAMES_HERE) for ref in refs]


def wide_tiles(ref, frame):
    tiles = []
    for t in range(FRAMES_HERE + 1):
        slot = frame + t
        position = jnp.where(slot < FRAMES_HERE, slot, slot + 12)
        tiles.append((ref, slot, frame + (t + 1) % (FRAMES_HERE + 1), position))
    return tiles


def attend_kernel(kind, *refs):
    begins, ends = kind == "own", kind == "last"
    valid_ref, query_a, query_b = refs[:3]
    refs = refs[3:]
    wide = kind in ("wide", "last")
    block_refs, refs = refs[:2], refs[2:]
    if not begins:
        high_in, total_in, refs = refs[0], refs[1], refs[2:]
    even = valid_ref[FRAMES_HERE, 0]
    if ends:
        outs, refs = refs[:4], refs[4:]
    else:
        high_out, total_out, refs = refs[0], refs[1], refs[2:]
    if wide:
        held, sems = refs
        first = even * FRAMES_HERE
        copies = [
            pltpu.make_async_copy(block_refs[0], held.at[pl.ds(first, FRAMES_HERE)], sems.at[0]),
            pltpu.make_async_copy(
                block_refs[1], held.at[pl.ds(FRAMES_HERE - first, FRAMES_HERE)], sems.at[1]
            ),
        ]
        for copy in copies:
            copy.start()
        for copy in copies:
            copy.wait()
    ones = jnp.ones((16, 128), jnp.bfloat16)
    zeros = jnp.zeros((HEAD, 256), jnp.bfloat16)

    def prepare(frame):
        if kind == "own":
            tiles = own_tiles(block_refs)
        elif kind == "near":
            tiles = near_tiles(block_refs, even)
        else:
            tiles = wide_tiles(held, frame)
        held_refs, index, keep = [], [], []
        for ref, slot, other, position in tiles:
            there = valid_ref[frame, position]
            held_refs.append(ref)
            index.append(jnp.where(there != 0, slot, other))
            keep.append(there.astype(jnp.float32).astype(jnp.bfloat16))
        return frame, held_refs, index, keep

    def score(unit, head):
        frame, held_refs, index, _ = unit
        pair = head // 2
        query = jnp.concatenate(
            [
                query_a[frame, head * HEAD : (head + 1) * HEAD, :],
                query_b[frame, head * HEAD : (head + 1) * HEAD, :],
            ],
            axis=1,
        )
        both = [query, zeros] if head % 2 == 0 else [zeros, query]
        both = jnp.concatenate(both, axis=0)
        return [
            jnp.dot(
                ref[slot, 0:128, pair * 128 : (pair + 1) * 128],
                both,
                preferred_element_type=jnp.float32,
            )
            for ref, slot in zip(held_refs, index)
        ]

    def absorb(unit, head, scores):
        frame, held_refs, index, keep = unit
        pair = head // 2
        start = 128 + (head % 2) * HEAD
        high = scores[0].reshape(-1, 8, 256).max(axis=0)
        for s in scores[1:]:
            high = jnp.maximum(high, s.reshape(-1, 8, 256).max(axis=0))
        high = jnp.max(high, axis=0, keepdims=True)
        total = None
        if not begins:
            old = high_in[frame, head, 0:1, :]
            high = jnp.maximum(high, old)
            total = total_in[frame, head] * jnp.exp2(old - high)
        for t in range(0, len(scores), 2):
            group = range(t, min(t + 2, len(scores)))
            weights = [weigh(scores[g], high) for g in group]
            sides = []
            for g in group:
                value = held_refs[g][
                    index[g], start : start + HEAD, pair * 128 : (pair + 1) * 128
                ]
                sides.append(jnp.concatenate([value, ones], axis=0) * keep[g])
            added = jnp.dot(
                jnp.concatenate(sides, axis=1),
                jnp.concatenate(weights, axis=0),
                preferred_element_type=jnp.float32,
            )
            total = added if total is None else total + added
        if ends:
            return total[0:HEAD] / total[HEAD : HEAD + 1]
        total_out[frame, head] = total
        high_out[frame, head] = jnp.broadcast_to(high, (8, 256))
        return None

    def some_frames(step, carried):
        units = [prepare(step * TOGETHER + k) for k in range(TOGETHER)]
        order = [(unit, head) for unit in units for head in range(HEADS_HERE)]
        contexts = []
        scores = score(*order[0])
        for place, (unit, head) in enumerate(order):
            later = score(*order[place + 1]) if place + 1 < len(order) else None
            contexts.append(absorb(unit, head, scores))
            scores = later
            if ends and head == HEADS_HERE - 1:
                context = jnp.concatenate(contexts, axis=0).T.astype(jnp.bfloat16)
                contexts = []
                rows = pl.ds(pl.multiple_of(unit[0] * QUARTER, QUARTER), QUARTER)
                for j in range(4):
                    outs[j][rows, :] = context[j * QUARTER : (j + 1) * QUARTER]
        return carried

    lax.fori_loop(0, FRAMES_HERE // TOGETHER, some_frames, 0)


def attend(kind, valid, query_a, query_b, block_list, state=()):
    ends = kind == "last"
    scratch = []
    if kind in ("wide", "last"):
        scratch = [
            pltpu.VMEM((2 * FRAMES_HERE, 256, 256), jnp.bfloat16),
            pltpu.SemaphoreType.DMA((2,)),
        ]
    if ends:
        out_shape = [jax.ShapeDtypeStruct((FRAMES_HERE * QUARTER, WIDTH), jnp.bfloat16)] * 4
    else:
        out_shape = [
            jax.ShapeDtypeStruct((FRAMES_HERE, HEADS_HERE, 8, 256), jnp.float32),
            jax.ShapeDtypeStruct((FRAMES_HERE, HEADS_HERE, HEAD + 16, 256), jnp.float32),
        ]
    inputs = [valid, query_a, query_b, *block_list, *state]
    return pl.pallas_call(
        functools.partial(attend_kernel, kind),
        in_specs=[SMEM] + [VMEM] * (len(inputs) - 1),
        out_specs=[VMEM] * len(out_shape),
        out_shape=out_shape,
        scratch_shapes=scratch,
        compiler_params=pltpu.CompilerParams(vmem_limit_bytes=36 << 20),
        cost_estimate=BRIEF,
    )(*inputs)


def finish_kernel(*refs):
    contexts, weights, (token_ref, gain_ref, proj_ref, out_ref, map_ref) = (
        refs[:4],
        refs[4:10],
        refs[10:],
    )
    own, beside, *parts = [ref[...] for ref in weights]
    weights = [own, beside]
    for half in (parts[:2], parts[2:]):
        weights.append(jnp.concatenate(half, axis=0))
    total = token_ref[...].astype(jnp.float32)
    mixed = jnp.dot(contexts[0][...], weights[0], preferred_element_type=jnp.float32)
    for c, w in zip(contexts[1:], weights[1:]):
        mixed = mixed + jnp.dot(c[...], w, preferred_element_type=jnp.float32)
    attended = (total + mixed).astype(jnp.bfloat16)
    out_ref[...] = attended
    lifted = layer_norm(attended.astype(jnp.float32), gain_ref[...]).astype(jnp.bfloat16)
    mapped = jnp.dot(lifted, proj_ref[...], preferred_element_type=jnp.float32)
    map_ref[...] = mapped.astype(jnp.bfloat16)


def finish(contexts, weights, tokens, gain, proj):
    return pl.pallas_call(
        finish_kernel,
        in_specs=[VMEM] * 13,
        out_specs=[VMEM] * 2,
        out_shape=[
            jax.ShapeDtypeStruct((256, 1024), jnp.bfloat16),
            jax.ShapeDtypeStruct((256, 256), jnp.bfloat16),
        ],
        compiler_params=pltpu.CompilerParams(vmem_limit_bytes=32 << 20),
        cost_estimate=BRIEF,
    )(*contexts, *weights, tokens, gain, proj)


def join_kernel(row_ref, beside_ref, own_ref, across_ref, one_ref, two_ref, out_ref):
    def widen(values):
        count = values.shape[0]
        column = lax.broadcasted_iota(jnp.int32, (count, 256), 0) % 32
        left = jnp.where(column == 0, 0.0, pltpu.roll(values, 1, 0))
        right = jnp.where(column == 31, 0.0, pltpu.roll(values, count - 1, 0))
        return jnp.concatenate(
            [left.astype(jnp.bfloat16), values.astype(jnp.bfloat16), right.astype(jnp.bfloat16)],
            axis=1,
        )

    def conv(wide, rows_in, weight_ref):
        rows_out = rows_in - 2
        summed = None
        for a in range(3):
            window = jnp.concatenate(
                [
                    wide[(f * rows_in + a) * 32 : (f * rows_in + a + rows_out) * 32]
                    for f in range(FRAMES_HERE)
                ],
                axis=0,
            )
            added = jnp.dot(window, weight_ref[a], preferred_element_type=jnp.float32)
            summed = added if summed is None else summed + added
        return summed

    own = own_ref[...].astype(jnp.float32)
    place = row_ref[0]
    odd = place % 2 == 1
    beside = beside_ref[...].astype(jnp.float32)
    across = across_ref[...].astype(jnp.float32)
    before = jnp.where(odd, beside, across)
    after = jnp.where(odd, across, beside)
    six = []
    for f in range(FRAMES_HERE):
        span = slice(f * QUARTER, (f + 1) * QUARTER)
        six += [before[span], own[span], after[span]]
    six = jnp.maximum(jnp.concatenate(six, axis=0), 0.0)
    inner = conv(widen(six), 6, one_ref)
    inner = jnp.maximum(inner, 0.0)
    row = (lax.broadcasted_iota(jnp.int32, (512, 256), 0) // 32) % 4
    drop = ((row == 0) & (place == 0)) | ((row == 3) & (place == 3))
    inner = jnp.where(drop, 0.0, inner)
    joined = conv(widen(inner), 4, two_ref)
    out_ref[...] = (own + joined).astype(jnp.bfloat16)


def join(row, beside, own, across, one, two):
    return pl.pallas_call(
        join_kernel,
        in_specs=[SMEM] + [VMEM] * 5,
        out_specs=VMEM,
        out_shape=jax.ShapeDtypeStruct((256, 256), jnp.bfloat16),
        compiler_params=pltpu.CompilerParams(vmem_limit_bytes=32 << 20),
        cost_estimate=BRIEF,
    )(row, beside, own, across, one, two)


def shards(
    tokens,
    norm_gain,
    qkv_weight,
    out_weight,
    key_offsets,
    feat_gain,
    proj_weight,
    conv_one,
    conv_two,
):
    own = tokens.reshape(FRAMES_HERE * QUARTER, 1024)
    core = lambda value: lax.ppermute(value, "row", CORE_PAIRS)
    chip = lambda value: lax.ppermute(value, "row", CHIP_PAIRS)
    tie = lax.optimization_barrier

    positions = np.arange(20)
    distance = positions[None, :] - 8 - np.arange(FRAMES_HERE)[:, None]
    valid = jnp.any(key_offsets[:, :, None] == distance[:, None, :], axis=1).astype(jnp.int32)
    block = lax.axis_index("frame")
    even = 1 - block % 2
    valid = jnp.concatenate([valid, jnp.full((1, 20), even, jnp.int32)], axis=0)
    edge_block = (block % EDGE == 0) | (block % EDGE == EDGE - 1)

    normed = normalise(own, norm_gain.reshape(1, 1024))
    near = core(normed)
    far = chip(normed)
    side = swapped(normed, 0)
    other = swapped(normed, 1, True)
    kv_a, query_a = project([normed, near], qkv_weight, True)
    far, kv_a = tie((far, kv_a))
    far_near = core(far)
    out_early, far = tie((out_weight[:EARLY], far))
    chip_early = chip(out_early)
    far_near, side, other = tie((far_near, side, other))
    kv_b, query_b = project([far, far_near], qkv_weight, True)
    kv_b, chip_early = tie((kv_b, chip_early))
    side_b = swapped(kv_b, 0)
    other_b = swapped(jnp.where(edge_block, kv_a, kv_b), 1)
    side, other, kv_b = tie((side, other, kv_b))
    side_near, other_near = core(side), core(other)
    state = attend("own", valid, query_a, query_b, [kv_a, kv_b])
    side, state = tie((side, state))
    side_a, other_a = project([side, side_near, other, other_near], qkv_weight, False)
    side_2a, other_2a = swapped(other_a, 0), swapped(side_a, 1)
    state = attend("near", valid, query_a, query_b, [side_a, other_a], state)
    side_b, other_b, state = tie((side_b, other_b, state))
    side_2b, other_2b = swapped(other_b, 0), swapped(side_b, 1)
    state = attend("near", valid, query_a, query_b, [side_b, other_b], state)
    state = attend("wide", valid, query_a, query_b, [side_2a, other_2a], state)
    out_last, out_late, chip_early, state = tie((out_weight, out_weight[EARLY:], chip_early, state))
    chip_late = chip(out_late)
    weight_core, cross_early = core(out_last), core(chip_early)
    parts = attend("last", valid, query_a, query_b, [side_2b, other_2b], state)
    chip_late, *parts = tie((chip_late, *parts))
    cross_late = core(chip_late)

    contexts = [
        parts[0],
        core(parts[1]),
        chip(parts[2]),
        lax.ppermute(parts[3], "row", CROSS_PAIRS),
    ]
    weights = [out_weight, weight_core, chip_early, chip_late, cross_early, cross_late]
    attended, mapped = finish(contexts, weights, own, feat_gain.reshape(1, 1024), proj_weight)

    across = lax.ppermute(mapped, "row", [(1, 2), (2, 1)])
    beside = core(mapped)
    place = lax.axis_index("row").astype(jnp.int32).reshape(1)
    joined = join(
        place,
        beside,
        mapped,
        across,
        conv_one.reshape(3, 768, 256),
        conv_two.reshape(3, 768, 256),
    )
    return attended.reshape(tokens.shape), joined.reshape(tokens.shape[:3] + (256,))


def solution(mesh):
    in_specs = (
        P("frame", "row", None, None),
        P(),
        P(None, None, "row"),
        P("row", None),
        P("frame", None),
        P(),
        P(),
        P(),
        P(),
    )
    out_specs = (P("frame", "row", None, None), P("frame", "row", None, None))
    return jax.shard_map(shards, mesh=mesh, in_specs=in_specs, out_specs=out_specs, check_vma=False)
```

```python
import functools

import jax
import jax.numpy as jnp
import numpy as np
from jax import lax
from jax.experimental import pallas as pl
from jax.experimental.pallas import tpu as pltpu
from jax.sharding import PartitionSpec as P

EPSILON = 1e-06
HEAD = 64
HEADS_HERE = 4
FRAMES_HERE = 4
QUARTER = 64
WIDTH = 256
QUERY_SCALE = 1.4426950408889634 / 8.0
LARGE = 20 << 20
BRIEF = pl.CostEstimate(flops=1, bytes_accessed=1, transcendentals=0)
EDGE = 8
TOGETHER = 2
EARLY = 96
VMEM = pl.BlockSpec(memory_space=pltpu.VMEM)
SMEM = pl.BlockSpec(memory_space=pltpu.SMEM)
ANY = pl.BlockSpec(memory_space=pl.ANY)
HBM = pl.BlockSpec(memory_space=pltpu.HBM)

CORE_PAIRS = [(0, 1), (1, 0), (2, 3), (3, 2)]
CHIP_PAIRS = [(0, 2), (2, 0), (1, 3), (3, 1)]
CROSS_PAIRS = [(0, 3), (3, 0), (1, 2), (2, 1)]


def swapped(value, offset, across=False):
    count = lax.axis_size("frame")
    pairs = []
    for low in range(offset, count, 2):
        high = (low + 1) % count
        flip = 2 if across and low // EDGE != high // EDGE else 0
        for row in range(4):
            pairs.append((low * 4 + row, high * 4 + (row ^ flip)))
            pairs.append((high * 4 + (row ^ flip), low * 4 + row))
    return lax.ppermute(value, ("frame", "row"), pairs)


def layer_norm(values, gain_vec):
    average = jnp.mean(values, axis=-1, keepdims=True)
    centered = values - average
    spread = jnp.mean(centered * centered, axis=-1, keepdims=True)
    return centered * lax.rsqrt(spread + EPSILON) * gain_vec


def norm_kernel(token_hbm, gain_hbm, out_ref, token, gain, sems):
    copies = [
        pltpu.make_async_copy(token_hbm, token, sems.at[0]),
        pltpu.make_async_copy(gain_hbm, gain, sems.at[1]),
    ]
    for copy in copies:
        copy.start()
    for copy in copies:
        copy.wait()
    values = layer_norm(token[...].astype(jnp.float32), gain[...])
    out_ref[...] = values.astype(jnp.bfloat16)


def normalise(tokens, gain):
    return pl.pallas_call(
        norm_kernel,
        in_specs=[HBM] * 2,
        out_specs=VMEM,
        out_shape=jax.ShapeDtypeStruct(tokens.shape, jnp.bfloat16),
        scratch_shapes=[
            pltpu.VMEM(tokens.shape, jnp.bfloat16),
            pltpu.VMEM(gain.shape, jnp.float32),
            pltpu.SemaphoreType.DMA((2,)),
        ],
        compiler_params=pltpu.CompilerParams(vmem_limit_bytes=60 << 20),
        cost_estimate=BRIEF,
    )(tokens, gain)


def project_kernel(blocks, queries, *refs):
    parts, refs = refs[: 2 * blocks], refs[2 * blocks :]
    weight_hbm, refs = refs[0], refs[1:]
    kv_refs, refs = refs[:blocks], refs[blocks:]
    if queries:
        query_ref, refs = refs[0], refs[1:]
    weight, sem = refs
    skip = 0 if queries else 1
    copies = [
        pltpu.make_async_copy(weight_hbm.at[which], weight.at[which - skip], sem.at[which - skip])
        for which in range(skip, 3)
    ]
    for which in ([1, 2, 0] if queries else [0, 1]):
        copies[which].start()
    for copy in copies:
        copy.wait()
    for block in range(blocks):
        rows = []
        for frame in range(FRAMES_HERE):
            for part in parts[2 * block : 2 * block + 2]:
                rows.append(part[frame * QUARTER : (frame + 1) * QUARTER])
        rows = jnp.concatenate(rows, axis=0)
        key = jnp.dot(rows, weight[1 - skip], preferred_element_type=jnp.float32)
        key = key.astype(jnp.bfloat16)
        value = jnp.dot(rows, weight[2 - skip], preferred_element_type=jnp.float32)
        value = value.T.astype(jnp.bfloat16)
        kv_ref = kv_refs[block]
        for frame in range(FRAMES_HERE):
            span = slice(frame * 128, (frame + 1) * 128)
            kv_ref[frame, 0:128, :] = key[span]
            kv_ref[frame, 128:256, 0:128] = value[0:128, span]
            kv_ref[frame, 128:256, 128:256] = value[128:256, span]
        if queries:
            query = jnp.dot(rows, weight[0], preferred_element_type=jnp.float32)
            query = (query * QUERY_SCALE).T.astype(jnp.bfloat16)
            for frame in range(FRAMES_HERE):
                query_ref[frame] = query[:, frame * 128 : (frame + 1) * 128]


def project(parts, weight, queries):
    blocks = len(parts) // 2
    out_shape = [jax.ShapeDtypeStruct((FRAMES_HERE, 256, 256), jnp.bfloat16)] * blocks
    if queries:
        out_shape.append(jax.ShapeDtypeStruct((FRAMES_HERE, WIDTH, 128), jnp.bfloat16))
    used = 3 if queries else 2
    return pl.pallas_call(
        functools.partial(project_kernel, blocks, queries),
        in_specs=[VMEM] * (2 * blocks) + [HBM],
        out_specs=[VMEM] * len(out_shape),
        out_shape=out_shape,
        scratch_shapes=[pltpu.VMEM((used, 1024, WIDTH), jnp.bfloat16), pltpu.SemaphoreType.DMA((used,))],
        compiler_params=pltpu.CompilerParams(vmem_limit_bytes=LARGE),
        cost_estimate=BRIEF,
    )(*parts, weight)


def weigh(scores, high):
    return jnp.exp2(scores - high).astype(jnp.bfloat16)


def near_tiles(refs, even):
    tiles = []
    for which, ref in enumerate(refs):
        ahead = even if which == 0 else 1 - even
        for t in range(FRAMES_HERE):
            tiles.append((ref, t, (t + 1) % FRAMES_HERE, 4 + 8 * ahead + t))
    return tiles


def own_tiles(refs):
    return [(ref, t, (t + 1) % FRAMES_HERE, 8 + t) for t in range(FRAMES_HERE) for ref in refs]


def wide_tiles(ref, frame):
    tiles = []
    for t in range(FRAMES_HERE + 1):
        slot = frame + t
        position = jnp.where(slot < FRAMES_HERE, slot, slot + 12)
        tiles.append((ref, slot, frame + (t + 1) % (FRAMES_HERE + 1), position))
    return tiles


def attend_kernel(kind, *refs):
    begins, ends = kind == "own", kind == "last"
    valid_ref, query_a, query_b = refs[:3]
    refs = refs[3:]
    wide = kind in ("wide", "last")
    together = FRAMES_HERE if ends else TOGETHER
    block_refs, refs = refs[:2], refs[2:]
    if not begins:
        high_in, total_in, refs = refs[0], refs[1], refs[2:]
    even = valid_ref[FRAMES_HERE, 0]
    if ends:
        outs, refs = refs[:4], refs[4:]
    else:
        high_out, total_out, refs = refs[0], refs[1], refs[2:]
    if wide:
        held, sems = refs
        first = even * FRAMES_HERE
        copies = [
            pltpu.make_async_copy(block_refs[0], held.at[pl.ds(first, FRAMES_HERE)], sems.at[0]),
            pltpu.make_async_copy(
                block_refs[1], held.at[pl.ds(FRAMES_HERE - first, FRAMES_HERE)], sems.at[1]
            ),
        ]
        for copy in copies:
            copy.start()
        for copy in copies:
            copy.wait()
    ones = jnp.ones((16, 128), jnp.bfloat16)
    zeros = jnp.zeros((HEAD, 256), jnp.bfloat16)

    def prepare(frame):
        if kind == "own":
            tiles = own_tiles(block_refs)
        elif kind == "near":
            tiles = near_tiles(block_refs, even)
        else:
            tiles = wide_tiles(held, frame)
        held_refs, index, keep = [], [], []
        for ref, slot, other, position in tiles:
            there = valid_ref[frame, position]
            held_refs.append(ref)
            index.append(jnp.where(there != 0, slot, other))
            keep.append(there.astype(jnp.float32).astype(jnp.bfloat16))
        return frame, held_refs, index, keep

    def score(unit, head):
        frame, held_refs, index, _ = unit
        pair = head // 2
        query = jnp.concatenate(
            [
                query_a[frame, head * HEAD : (head + 1) * HEAD, :],
                query_b[frame, head * HEAD : (head + 1) * HEAD, :],
            ],
            axis=1,
        )
        both = [query, zeros] if head % 2 == 0 else [zeros, query]
        both = jnp.concatenate(both, axis=0)
        return [
            jnp.dot(
                ref[slot, 0:128, pair * 128 : (pair + 1) * 128],
                both,
                preferred_element_type=jnp.float32,
            )
            for ref, slot in zip(held_refs, index)
        ]

    def absorb(unit, head, scores):
        frame, held_refs, index, keep = unit
        pair = head // 2
        start = 128 + (head % 2) * HEAD
        high = scores[0].reshape(-1, 8, 256).max(axis=0)
        for s in scores[1:]:
            high = jnp.maximum(high, s.reshape(-1, 8, 256).max(axis=0))
        high = jnp.max(high, axis=0, keepdims=True)
        total = None
        if not begins:
            old = high_in[frame, head, 0:1, :]
            high = jnp.maximum(high, old)
            total = total_in[frame, head] * jnp.exp2(old - high)
        for t in range(0, len(scores), 2):
            group = range(t, min(t + 2, len(scores)))
            weights = [weigh(scores[g], high) for g in group]
            sides = []
            for g in group:
                value = held_refs[g][
                    index[g], start : start + HEAD, pair * 128 : (pair + 1) * 128
                ]
                sides.append(jnp.concatenate([value, ones], axis=0) * keep[g])
            added = jnp.dot(
                jnp.concatenate(sides, axis=1),
                jnp.concatenate(weights, axis=0),
                preferred_element_type=jnp.float32,
            )
            total = added if total is None else total + added
        if ends:
            return total[0:HEAD] / total[HEAD : HEAD + 1]
        total_out[frame, head] = total
        high_out[frame, head] = jnp.broadcast_to(high, (8, 256))
        return None

    def some_frames(step, carried):
        units = [prepare(step * together + k) for k in range(together)]
        order = [(unit, head) for unit in units for head in range(HEADS_HERE)]
        contexts = []
        scores = score(*order[0])
        for place, (unit, head) in enumerate(order):
            later = score(*order[place + 1]) if place + 1 < len(order) else None
            contexts.append(absorb(unit, head, scores))
            scores = later
            if ends and head == HEADS_HERE - 1:
                context = jnp.concatenate(contexts, axis=0).T.astype(jnp.bfloat16)
                contexts = []
                rows = pl.ds(pl.multiple_of(unit[0] * QUARTER, QUARTER), QUARTER)
                for j in range(4):
                    outs[j][rows, :] = context[j * QUARTER : (j + 1) * QUARTER]
        return carried

    lax.fori_loop(0, FRAMES_HERE // together, some_frames, 0)


def attend(kind, valid, query_a, query_b, block_list, state=()):
    ends = kind == "last"
    scratch = []
    if kind in ("wide", "last"):
        scratch = [
            pltpu.VMEM((2 * FRAMES_HERE, 256, 256), jnp.bfloat16),
            pltpu.SemaphoreType.DMA((2,)),
        ]
    if ends:
        out_shape = [jax.ShapeDtypeStruct((FRAMES_HERE * QUARTER, WIDTH), jnp.bfloat16)] * 4
    else:
        out_shape = [
            jax.ShapeDtypeStruct((FRAMES_HERE, HEADS_HERE, 8, 256), jnp.float32),
            jax.ShapeDtypeStruct((FRAMES_HERE, HEADS_HERE, HEAD + 16, 256), jnp.float32),
        ]
    inputs = [valid, query_a, query_b, *block_list, *state]
    return pl.pallas_call(
        functools.partial(attend_kernel, kind),
        in_specs=[SMEM] + [VMEM] * (len(inputs) - 1),
        out_specs=[VMEM] * len(out_shape),
        out_shape=out_shape,
        scratch_shapes=scratch,
        compiler_params=pltpu.CompilerParams(vmem_limit_bytes=36 << 20),
        cost_estimate=BRIEF,
    )(*inputs)


def finish_kernel(*refs):
    contexts, weights, (token_ref, gain_ref, proj_ref, out_ref, map_ref) = (
        refs[:4],
        refs[4:10],
        refs[10:],
    )
    own, beside, *parts = [ref[...] for ref in weights]
    weights = [own, beside]
    for half in (parts[:2], parts[2:]):
        weights.append(jnp.concatenate(half, axis=0))
    total = token_ref[...].astype(jnp.float32)
    mixed = jnp.dot(contexts[0][...], weights[0], preferred_element_type=jnp.float32)
    for c, w in zip(contexts[1:], weights[1:]):
        mixed = mixed + jnp.dot(c[...], w, preferred_element_type=jnp.float32)
    attended = (total + mixed).astype(jnp.bfloat16)
    out_ref[...] = attended
    lifted = layer_norm(attended.astype(jnp.float32), gain_ref[...]).astype(jnp.bfloat16)
    mapped = jnp.dot(lifted, proj_ref[...], preferred_element_type=jnp.float32)
    map_ref[...] = mapped.astype(jnp.bfloat16)


def finish(contexts, weights, tokens, gain, proj):
    return pl.pallas_call(
        finish_kernel,
        in_specs=[VMEM] * 13,
        out_specs=[VMEM] * 2,
        out_shape=[
            jax.ShapeDtypeStruct((256, 1024), jnp.bfloat16),
            jax.ShapeDtypeStruct((256, 256), jnp.bfloat16),
        ],
        compiler_params=pltpu.CompilerParams(vmem_limit_bytes=32 << 20),
        cost_estimate=BRIEF,
    )(*contexts, *weights, tokens, gain, proj)


def join_kernel(row_ref, beside_ref, own_ref, across_ref, one_ref, two_ref, out_ref):
    def widen(values):
        count = values.shape[0]
        column = lax.broadcasted_iota(jnp.int32, (count, 256), 0) % 32
        left = jnp.where(column == 0, 0.0, pltpu.roll(values, 1, 0))
        right = jnp.where(column == 31, 0.0, pltpu.roll(values, count - 1, 0))
        return jnp.concatenate(
            [left.astype(jnp.bfloat16), values.astype(jnp.bfloat16), right.astype(jnp.bfloat16)],
            axis=1,
        )

    def conv(wide, rows_in, weight_ref):
        rows_out = rows_in - 2
        summed = None
        for a in range(3):
            window = jnp.concatenate(
                [
                    wide[(f * rows_in + a) * 32 : (f * rows_in + a + rows_out) * 32]
                    for f in range(FRAMES_HERE)
                ],
                axis=0,
            )
            added = jnp.dot(window, weight_ref[a], preferred_element_type=jnp.float32)
            summed = added if summed is None else summed + added
        return summed

    own = own_ref[...].astype(jnp.float32)
    place = row_ref[0]
    odd = place % 2 == 1
    beside = beside_ref[...].astype(jnp.float32)
    across = across_ref[...].astype(jnp.float32)
    before = jnp.where(odd, beside, across)
    after = jnp.where(odd, across, beside)
    six = []
    for f in range(FRAMES_HERE):
        span = slice(f * QUARTER, (f + 1) * QUARTER)
        six += [before[span], own[span], after[span]]
    six = jnp.maximum(jnp.concatenate(six, axis=0), 0.0)
    inner = conv(widen(six), 6, one_ref)
    inner = jnp.maximum(inner, 0.0)
    row = (lax.broadcasted_iota(jnp.int32, (512, 256), 0) // 32) % 4
    drop = ((row == 0) & (place == 0)) | ((row == 3) & (place == 3))
    inner = jnp.where(drop, 0.0, inner)
    joined = conv(widen(inner), 4, two_ref)
    out_ref[...] = (own + joined).astype(jnp.bfloat16)


def join(row, beside, own, across, one, two):
    return pl.pallas_call(
        join_kernel,
        in_specs=[SMEM] + [VMEM] * 5,
        out_specs=VMEM,
        out_shape=jax.ShapeDtypeStruct((256, 256), jnp.bfloat16),
        compiler_params=pltpu.CompilerParams(vmem_limit_bytes=32 << 20),
        cost_estimate=BRIEF,
    )(row, beside, own, across, one, two)


def shards(
    tokens,
    norm_gain,
    qkv_weight,
    out_weight,
    key_offsets,
    feat_gain,
    proj_weight,
    conv_one,
    conv_two,
):
    own = tokens.reshape(FRAMES_HERE * QUARTER, 1024)
    core = lambda value: lax.ppermute(value, "row", CORE_PAIRS)
    chip = lambda value: lax.ppermute(value, "row", CHIP_PAIRS)
    tie = lax.optimization_barrier

    positions = np.arange(20)
    distance = positions[None, :] - 8 - np.arange(FRAMES_HERE)[:, None]
    valid = jnp.any(key_offsets[:, :, None] == distance[:, None, :], axis=1).astype(jnp.int32)
    block = lax.axis_index("frame")
    even = 1 - block % 2
    valid = jnp.concatenate([valid, jnp.full((1, 20), even, jnp.int32)], axis=0)
    edge_block = (block % EDGE == 0) | (block % EDGE == EDGE - 1)

    normed = normalise(own, norm_gain.reshape(1, 1024))
    near = core(normed)
    far = chip(normed)
    side = swapped(normed, 0)
    other = swapped(normed, 1, True)
    kv_a, query_a = project([normed, near], qkv_weight, True)
    far, kv_a = tie((far, kv_a))
    far_near = core(far)
    out_early, far = tie((out_weight[:EARLY], far))
    chip_early = chip(out_early)
    far_near, side, other = tie((far_near, side, other))
    kv_b, query_b = project([far, far_near], qkv_weight, True)
    kv_b, chip_early = tie((kv_b, chip_early))
    side_b = swapped(kv_b, 0)
    other_b = swapped(jnp.where(edge_block, kv_a, kv_b), 1)
    side, other, kv_b = tie((side, other, kv_b))
    side_near, other_near = core(side), core(other)
    state = attend("own", valid, query_a, query_b, [kv_a, kv_b])
    side, state = tie((side, state))
    side_a, other_a = project([side, side_near, other, other_near], qkv_weight, False)
    side_2a, other_2a = swapped(other_a, 0), swapped(side_a, 1)
    state = attend("near", valid, query_a, query_b, [side_a, other_a], state)
    side_b, other_b, state = tie((side_b, other_b, state))
    side_2b, other_2b = swapped(other_b, 0), swapped(side_b, 1)
    state = attend("near", valid, query_a, query_b, [side_b, other_b], state)
    state = attend("wide", valid, query_a, query_b, [side_2a, other_2a], state)
    out_last, out_late, chip_early, state = tie((out_weight, out_weight[EARLY:], chip_early, state))
    chip_late = chip(out_late)
    weight_core, cross_early = core(out_last), core(chip_early)
    parts = attend("last", valid, query_a, query_b, [side_2b, other_2b], state)
    chip_late, *parts = tie((chip_late, *parts))
    cross_late = core(chip_late)

    contexts = [
        parts[0],
        core(parts[1]),
        chip(parts[2]),
        lax.ppermute(parts[3], "row", CROSS_PAIRS),
    ]
    weights = [out_weight, weight_core, chip_early, chip_late, cross_early, cross_late]
    attended, mapped = finish(contexts, weights, own, feat_gain.reshape(1, 1024), proj_weight)

    across = lax.ppermute(mapped, "row", [(1, 2), (2, 1)])
    beside = core(mapped)
    place = lax.axis_index("row").astype(jnp.int32).reshape(1)
    joined = join(
        place,
        beside,
        mapped,
        across,
        conv_one.reshape(3, 768, 256),
        conv_two.reshape(3, 768, 256),
    )
    return attended.reshape(tokens.shape), joined.reshape(tokens.shape[:3] + (256,))


def solution(mesh):
    in_specs = (
        P("frame", "row", None, None),
        P(),
        P(None, None, "row"),
        P("row", None),
        P("frame", None),
        P(),
        P(),
        P(),
        P(),
    )
    out_specs = (P("frame", "row", None, None), P("frame", "row", None, None))
    return jax.shard_map(shards, mesh=mesh, in_specs=in_specs, out_specs=out_specs, check_vma=False)
```
